256 devices in a mesh: gx: 8 (over z), gy: 32 (over x, y, core).
Axes of the slice: x: 4, y: 4, z: 8, core: 2. Of those that a mesh axis runs over, the one named last changes fastest.
Arguments:
- charge: float32 [1024, 1024, 128], P('gx', 'gy'), may hold values from -6.1 to 6.1
- level_taps: float32 [4, 9], replicated, may hold values from 0.03 to 0.3, as said below
Outputs:
- potential: float32 [1024, 1024, 128], P('gx', 'gy')
The draws below stay inside these ranges and needn't reach their ends.
Inputs may be any that keep to these rules, and one draw needn't show every extreme that they name: Each row is symmetric: level_taps[l, k] = level_taps[l, 8 - k].
All inputs are finite; a program needn't handle non-finite values.
Results may differ from the reference program's by a relative error of at most 0.0001.
Values sent between devices are 32-bit elements; how exact they have to be, the bound alone decides.
A program may use at most 128 MiB of HBM per device.

```python
import math
import jax
import jax.numpy as jnp
from jax import lax

NZ = 128
LEVELS = 4
HALO = 4
NX = 1024
NY = 1024


def draw_charge(key, part):
    key = jax.random.fold_in(key, 7)
    rough_key, wave_key, phase_key = jax.random.split(key, 3)
    waves = jax.random.randint(wave_key, (3,), 1, 3).astype(jnp.float32)
    phase = jax.random.uniform(phase_key, (), jnp.float32, -math.pi, math.pi)
    places_x = (jnp.arange(NX, dtype=jnp.float32) / NX)[:, None, None]
    places_y = (jnp.arange(NY, dtype=jnp.float32) / NY)[None, :, None]
    places_z = (jnp.arange(NZ, dtype=jnp.float32) / NZ)[None, None, :]
    smooth = jnp.sin(2.0 * math.pi * (waves[0] * places_x + waves[1] * places_y + waves[2] * places_z) + phase)
    rough = jnp.clip(jax.random.normal(rough_key, (NX, NY, NZ), jnp.float32), -5.8, 5.8)
    return rough + 0.12 * (1.25 + smooth)


def draw_level_taps(key, part):
    key = jax.random.fold_in(key, 13)
    side_key, centre_key = jax.random.split(key, 2)
    sides = jax.random.uniform(side_key, (LEVELS, HALO), jnp.float32, 0.03, 0.3)
    centre = jax.random.uniform(centre_key, (LEVELS, 1), jnp.float32, 0.03, 0.3)
    return jnp.concatenate([sides[:, ::-1], centre, sides], axis=1)


def setup_inputs(seed: int = 0) -> dict:
    key_list = jax.random.split(jax.random.key(seed), 3)
    charge = draw_charge(jax.random.fold_in(key_list[2], 71), 0)
    level_taps = draw_level_taps(jax.random.fold_in(key_list[2], 71), 0)
    return {"charge": charge, "level_taps": level_taps}


def tap_sum(values, weights, length, dimension):
    summed = weights[0] * lax.slice_in_dim(values, 0, length, axis=dimension)
    for offset in range(1, weights.shape[0]):
        summed = summed + weights[offset] * lax.slice_in_dim(values, offset, offset + length, axis=dimension)
    return summed

def convolve(bordered, weights, cells_x, cells_y):
    margin = (weights.shape[0] - 1) // 2
    along_x = tap_sum(bordered, weights, cells_x, 0)
    along_y = tap_sum(along_x, weights, cells_y, 1)
    cells_z = along_y.shape[2]
    deeper = jnp.pad(along_y, ((0, 0), (0, 0), (margin, margin)))
    return tap_sum(deeper, weights, cells_z, 2)

def restrict_axis(values, anchor, length, dimension):
    low_cells = lax.slice_in_dim(values, anchor - 1, anchor - 1 + 2 * length, stride=2, axis=dimension)
    middle = lax.slice_in_dim(values, anchor, anchor + 2 * length, stride=2, axis=dimension)
    high_cells = lax.slice_in_dim(values, anchor + 1, anchor + 2 * length, stride=2, axis=dimension)
    return 0.25 * low_cells + 0.5 * middle + 0.25 * high_cells

def restrict_block(bordered, cells_x, cells_y):
    margin = (bordered.shape[0] - cells_x) // 2
    coarse_x = restrict_axis(bordered, margin, cells_x // 2, 0)
    coarse_y = restrict_axis(coarse_x, margin, cells_y // 2, 1)
    deeper = jnp.pad(coarse_y, ((0, 0), (0, 0), (1, 0)))
    return restrict_axis(deeper, 1, coarse_y.shape[2] // 2, 2)

def alternate(even_cells, odd_cells, dimension):
    stacked = jnp.stack([even_cells, odd_cells], axis=dimension + 1)
    target = list(even_cells.shape)
    target[dimension] = 2 * target[dimension]
    return stacked.reshape(target)

def prolong_axis(values, length, dimension):
    low_cells = lax.slice_in_dim(values, 0, length, axis=dimension)
    high_cells = lax.slice_in_dim(values, 1, length + 1, axis=dimension)
    return alternate(low_cells, 0.5 * (low_cells + high_cells), dimension)

def prolong_block(bordered):
    cells_x = bordered.shape[0] - 1
    cells_y = bordered.shape[1] - 1
    finer_x = prolong_axis(bordered, cells_x, 0)
    finer_y = prolong_axis(finer_x, cells_y, 1)
    cells_z = finer_y.shape[2]
    deeper = jnp.pad(finer_y, ((0, 0), (0, 0), (0, 1)))
    return prolong_axis(deeper, cells_z, 2)

def gaussian_matrix(length):
    spread = max(length, 4) / 2.0
    places = jnp.arange(length, dtype=jnp.float32)
    offsets = (places[:, None] - places[None, :]) / spread
    return jnp.exp(-offsets * offsets) / (math.sqrt(math.pi) * spread)

def coarsest_field(coarse, levels):
    along_x = jnp.einsum('ai,ijk->ajk', gaussian_matrix(coarse.shape[0]), coarse, precision=lax.Precision.HIGHEST)
    along_y = jnp.einsum('bj,ajk->abk', gaussian_matrix(coarse.shape[1]), along_x, precision=lax.Precision.HIGHEST)
    along_z = jnp.einsum('ck,abk->abc', gaussian_matrix(coarse.shape[2]), along_y, precision=lax.Precision.HIGHEST)
    return 2.0 ** levels * along_z

def reference(charge, level_taps):
    charges = charge
    potentials = []
    for at_level in range(LEVELS):
        cells_x, cells_y = (charges.shape[0], charges.shape[1])
        bordered = jnp.pad(charges, ((HALO, HALO), (HALO, HALO), (0, 0)))
        potentials.append(2.0 ** at_level * convolve(bordered, level_taps[at_level], cells_x, cells_y))
        charges = restrict_block(bordered, cells_x, cells_y)
    current = coarsest_field(charges, LEVELS)
    for at_level in range(LEVELS - 1, -1, -1):
        current = potentials[at_level] + prolong_block(jnp.pad(current, ((0, 1), (0, 1), (0, 0))))
    return current
```

```python
import functools
import math

import jax
import jax.numpy as jnp
from jax import lax
from jax.experimental import pallas as pl
from jax.experimental.pallas import tpu as pltpu
from jax.sharding import PartitionSpec as P

F32 = jnp.float32
BF16 = jnp.bfloat16
HIGHEST = lax.Precision.HIGHEST
MESH = pl.DeviceIdType.MESH

CX, CY, CZ = 128, 32, 128
REACH = 4
LANES = {1: (0, 64), 2: (64, 32), 3: (96, 16), 4: (112, 8)}
NXL = {1: 64, 2: 32, 3: 16, 4: 8}
NYL = {1: 16, 2: 8, 3: 4, 4: 2}
ROWS = {1: 24, 2: 16, 3: 8, 4: 8}


def iota(shape, dim):
    return lax.broadcasted_iota(jnp.int32, shape, dim)


def gauss(distance, length):
    spread = max(length, 4) / 2.0
    scaled = distance.astype(F32) / spread
    return jnp.exp(-scaled * scaled) / (math.sqrt(math.pi) * spread)


def split(value):
    high = value.astype(BF16)
    return high, (value - high.astype(F32)).astype(BF16)


def stacked(matrix):
    high, low = split(matrix)
    return jnp.concatenate([high, high, low], axis=0)


def product(value, weights):
    high, low = split(value)
    both = jnp.concatenate([high, low, high], axis=1)
    return jnp.dot(both, weights, preferred_element_type=F32)


def toeplitz(taps, level, shape, offset):
    matrix = jnp.zeros(shape, F32)
    for k in range(2 * REACH + 1):
        matrix = jnp.where(offset == k - REACH, taps[level, k], matrix)
    return matrix


def coarse_z(taps):
    a, c = iota((CZ, CZ), 0), iota((CZ, CZ), 1)
    down = jnp.zeros((CZ, CZ), F32)
    mix = jnp.zeros((CZ, CZ), F32)
    for level, (first, cells) in LANES.items():
        step = 2**level
        here = (c >= first) & (c < first + cells)
        weight = jnp.maximum(0, step - jnp.abs(a - step * (c - first)))
        down = jnp.where(here, weight.astype(F32) * 2.0 ** (-5 * level), down)
        inside = here & (a >= first) & (a < first + cells)
        if level < 4:
            block = toeplitz(taps, level, (CZ, CZ), a - c)
        else:
            block = gauss(a - c, cells)
        mix = jnp.where(inside, block, mix)
    return jnp.dot(down, mix, precision=HIGHEST, preferred_element_type=F32)


def prolong_z():
    r, a = iota((CZ, CZ), 0), iota((CZ, CZ), 1)
    up = jnp.zeros((CZ, CZ), F32)
    for level, (first, cells) in LANES.items():
        step = 2**level
        here = (r >= first) & (r < first + cells)
        weight = jnp.maximum(0, step - jnp.abs(a - step * (r - first)))
        up = jnp.where(here, weight.astype(F32) * 2.0**-level, up)
    return up.astype(BF16)


def weighted(pieces, weights):
    total = weights[REACH] * pieces[REACH]
    for k in range(REACH):
        total = total + weights[k] * (pieces[k] + pieces[2 * REACH - k])
    return total


def kernel(
    across_x, across_y, taps, q, out,
    E, C, T1, T2, T3, T4, A1, A2, A3, A4, B1, B2, B3, U1, U2, U3, E4, G3, G2, G1, G0,
    XS, XR, YS, YR, GA, GB, WZ, W0, PZ, E1Z,
    in_sem, y0_send, y0_recv, x0_send, x0_recv, cx_send, cx_recv, cy_send, cy_recv,
    c2_send, c2_recv, ga_send, ga_recv, gb_send, gb_recv,
):
    me_x, me_y = lax.axis_index("gx"), lax.axis_index("gy")
    first_x, last_x = me_x == 0, me_x == across_x - 1
    first_y, last_y = me_y == 0, me_y == across_y - 1
    A, B, U, T = {1: A1, 2: A2, 3: A3}, {1: B1, 2: B2, 3: B3}, {1: U1, 2: U2, 3: U3}, {2: T2, 3: T3, 4: T4}

    barrier = pltpu.get_barrier_semaphore()

    def greet_y(step, carry):
        pl.semaphore_signal(barrier, inc=1, device_id={"gy": lax.rem(me_y + step, across_y)}, device_id_type=MESH)
        return carry

    def greet_x(step, carry):
        pl.semaphore_signal(barrier, inc=1, device_id={"gx": lax.rem(me_x + step, across_x)}, device_id_type=MESH)
        return carry

    lax.fori_loop(1, across_y, greet_y, 0)
    lax.fori_loop(1, across_x, greet_x, 0)

    parts = 4
    depth = CX // parts
    loads = [
        pltpu.make_async_copy(
            q.at[pl.ds(i * depth, depth)], E.at[pl.ds(i * depth, depth), pl.ds(8, CY)], in_sem.at[i]
        )
        for i in range(parts)
    ]
    for load in loads:
        load.start()

    WZ[...] = stacked(coarse_z(taps))
    W0[...] = stacked(toeplitz(taps, 0, (CZ, CZ), iota((CZ, CZ), 0) - iota((CZ, CZ), 1)))
    rise = prolong_z()
    PZ[...] = jnp.concatenate([rise, rise], axis=0)

    def blank(ref, count, *spans):
        def body(i, carry):
            for start, size in spans:
                ref[i, pl.ds(start, size), :] = jnp.zeros((size, CZ), F32)
            return carry
        lax.fori_loop(0, count, body, 0)

    blank(T1, 65, (0, 8), (40, 16))
    blank(T2, 33, (0, 8), (32, 8))
    blank(T3, 17, (0, 8))
    blank(T4, 9, (0, 8), (16, 8))
    for level in (1, 2, 3):
        blank(B[level], NXL[level] + 1, (0, 8), *(((16, 8),) if level == 3 else ()))
        rows = ROWS[level]
        A[level][0:4] = jnp.zeros((4, rows, CZ), F32)
        A[level][NXL[level] + 5 : NXL[level] + 9] = jnp.zeros((4, rows, CZ), F32)

    @pl.when(first_y)
    def _():
        E[:, 4:8, :] = jnp.zeros((CX, 4, CZ), F32)
        YR[0, :, 0:5, :] = jnp.zeros((65, 5, CZ), F32)

    @pl.when(last_y)
    def _():
        E[:, 40:44, :] = jnp.zeros((CX, 4, CZ), F32)
        YR[1, :, 0:5, :] = jnp.zeros((65, 5, CZ), F32)

    @pl.when(me_y < 2)
    def _():
        YR[0, 0:17, 5:6, :] = jnp.zeros((17, 1, CZ), F32)

    @pl.when(me_y >= across_y - 2)
    def _():
        YR[1, 0:17, 5:6, :] = jnp.zeros((17, 1, CZ), F32)

    @pl.when(first_x)
    def _():
        C[0:4] = jnp.zeros((4, CY, CZ), F32)
        XR[0] = jnp.zeros((5, 24, CZ), F32)

    @pl.when(last_x)
    def _():
        C[CX + 4 : CX + 8] = jnp.zeros((4, CY, CZ), F32)
        XR[1] = jnp.zeros((5, 24, CZ), F32)

    pl.semaphore_wait(barrier, across_x + across_y - 2)

    def remote(src, dst, send, recv, **target):
        return pltpu.make_async_remote_copy(
            src_ref=src, dst_ref=dst, send_sem=send, recv_sem=recv, device_id=target, device_id_type=MESH
        )

    above_y, below_y = lax.rem(me_y + 1, across_y), lax.rem(me_y + across_y - 1, across_y)
    above_x, below_x = lax.rem(me_x + 1, across_x), lax.rem(me_x + across_x - 1, across_x)

    y0_up = remote(q.at[:, pl.ds(CY - 4, 4)], E.at[:, pl.ds(4, 4)], y0_send.at[0], y0_recv.at[0], gy=above_y)
    y0_down = remote(q.at[:, pl.ds(0, 4)], E.at[:, pl.ds(40, 4)], y0_send.at[1], y0_recv.at[1], gy=below_y)
    pl.when(jnp.logical_not(last_y))(y0_up.start)
    pl.when(jnp.logical_not(first_y))(y0_down.start)

    for load in loads:
        load.wait()

    T1[0, 8:40, :] = 2.0 * E[0, 8:40, :] + E[1, 8:40, :]
    T1[64, 8:40, :] = E[CX - 1, 8:40, :]

    def down_x(i, carry):
        T1[i, 8:40, :] = E[2 * i - 1, 8:40, :] + 2.0 * E[2 * i, 8:40, :] + E[2 * i + 1, 8:40, :]
        return carry

    lax.fori_loop(1, 64, down_x, 0, unroll=3)

    def down_yz(i, carry):
        at = pl.ds(i * 5, 5)
        value = (
            T1[at, pl.ds(7, 24, stride=2), :]
            + 2.0 * T1[at, pl.ds(8, 24, stride=2), :]
            + T1[at, pl.ds(9, 24, stride=2), :]
        )
        A1[pl.ds(4 + i * 5, 5)] = product(value.reshape(5 * 24, CZ), WZ[...]).reshape(5, 24, CZ)
        return carry

    lax.fori_loop(0, 13, down_yz, 0)

    for level in (2, 3, 4):
        finer, mid = A[level - 1], T[level]
        coarser, shift = (A[level], 4) if level < 4 else (A4, 0)
        inner, rows = ROWS[level - 1], ROWS[level]

        def down(i, carry, finer=finer, mid=mid, coarser=coarser, shift=shift, inner=inner, rows=rows):
            mid[i, pl.ds(8, inner), :] = finer[2 * i + 3] + 2.0 * finer[2 * i + 4] + finer[2 * i + 5]
            coarser[i + shift] = (
                mid[i, pl.ds(7, rows, stride=2), :]
                + 2.0 * mid[i, pl.ds(8, rows, stride=2), :]
                + mid[i, pl.ds(9, rows, stride=2), :]
            )
            return carry

        lax.fori_loop(0, NXL[level] + 1, down, 0)

    lane8 = iota((8, CZ), 1)
    message = jnp.zeros((8, CZ), F32)
    for x in range(9):
        value = jnp.where((lane8 >= 112) & (lane8 < 120), A4[x], 0.0)
        message = message + pltpu.roll(value, (8 * x - 112) % CZ, 1)
    GA[me_y] = message

    def send_a(step, carry):
        remote(GA.at[me_y], GA.at[me_y], ga_send, ga_recv, gy=lax.rem(me_y + step, across_y)).start()
        return carry

    lax.fori_loop(1, across_y, send_a, 0)

    @pl.when(last_x)
    def _():
        for level in (1, 2, 3):
            A[level][NXL[level] + 4] = jnp.zeros((ROWS[level], CZ), F32)

    for way in (0, 1):
        for i in range(5):
            at = {level: (NXL[level] if way == 0 else 4) + i for level in (1, 2, 3)}
            wide = A1[at[1]]
            lane = iota((24, CZ), 1)
            XS[way, i] = jnp.where(lane < 64, wide, 0.0)
            lane = iota((16, CZ), 1)
            XS[way, i, 0:16, :] = jnp.where(lane >= 64, A2[at[2]], XS[way, i, 0:16, :])
            lane = iota((8, CZ), 1)
            XS[way, i, 0:8, :] = jnp.where(lane >= 96, A3[at[3]], XS[way, i, 0:8, :])
    cx_up = remote(XS.at[0], XR.at[0], cx_send.at[0], cx_recv.at[0], gx=above_x)
    cx_down = remote(XS.at[1], XR.at[1], cx_send.at[1], cx_recv.at[1], gx=below_x)
    pl.when(jnp.logical_not(last_x))(cx_up.start)
    pl.when(jnp.logical_not(first_x))(cx_down.start)

    w0 = [taps[0, k] for k in range(2 * REACH + 1)]

    def mid_y(i, carry):
        C[4 + i, 8:24, :] = weighted([E[i, 12 + k : 28 + k, :] for k in range(9)], w0)
        return carry

    lax.fori_loop(0, CX, mid_y, 0, unroll=2)

    pl.when(jnp.logical_not(first_x))(cx_up.wait_recv)
    pl.when(jnp.logical_not(last_x))(cx_down.wait_recv)
    for level in (1, 2, 3):
        array, rows, n = A[level], ROWS[level], NXL[level]
        array[0:4] = XR[0, 0:4, 0:rows, :]
        array[4] = array[4] + XR[0, 4, 0:rows, :]
        array[n + 4] = array[n + 4] + XR[1, 0, 0:rows, :]
        array[n + 5 : n + 9] = XR[1, 1:5, 0:rows, :]
        wl = [taps[level, k] for k in range(2 * REACH + 1)]

        def along_x(i, carry, array=array, target=B[level], rows=rows, wl=wl):
            target[i, pl.ds(8, rows), :] = weighted([array[i + k] for k in range(9)], wl)
            return carry

        lax.fori_loop(0, n + 1, along_x, 0)

        @pl.when(last_x)
        def _(target=B[level], rows=rows, n=n):
            target[n, pl.ds(8, rows), :] = jnp.zeros((rows, CZ), F32)

        @pl.when(last_y)
        def _(target=B[level], level=level, n=n):
            target[:, pl.ds(8 + NYL[level], 1), :] = jnp.zeros((n + 1, 1, CZ), F32)

    def pack(x, levels):
        for way in (0, 1):
            lane = iota((8, CZ), 1)
            value = None
            for level in levels:
                start = 8 + (NYL[level] - 4 if way == 0 else 0)
                piece = B[level][x, pl.ds(start, 8), :]
                value = piece if value is None else jnp.where(lane >= LANES[level][0], piece, value)
            YS[way, x] = value

    lax.fori_loop(0, 17, lambda x, c: (pack(x, (1, 2, 3)), c)[1], 0)
    lax.fori_loop(17, 33, lambda x, c: (pack(x, (1, 2)), c)[1], 0)
    lax.fori_loop(33, 65, lambda x, c: (pack(x, (1,)), c)[1], 0)
    rows5 = pl.ds(0, 5)
    cy_up = remote(YS.at[0, :, rows5], YR.at[0, :, rows5], cy_send.at[0], cy_recv.at[0], gy=above_y)
    cy_down = remote(YS.at[1, :, rows5], YR.at[1, :, rows5], cy_send.at[1], cy_recv.at[1], gy=below_y)
    pl.when(jnp.logical_not(last_y))(cy_up.start)
    pl.when(jnp.logical_not(first_y))(cy_down.start)
    near, far = pl.ds(0, 17), pl.ds(5, 1)
    c2_up = remote(
        YS.at[0, near, pl.ds(4, 1)], YR.at[0, near, far], c2_send.at[0], c2_recv.at[0],
        gy=lax.rem(me_y + 2, across_y),
    )
    c2_down = remote(
        YS.at[1, near, pl.ds(0, 1)], YR.at[1, near, far], c2_send.at[1], c2_recv.at[1],
        gy=lax.rem(me_y + across_y - 2, across_y),
    )
    pl.when(me_y < across_y - 2)(c2_up.start)
    pl.when(me_y >= 2)(c2_down.start)

    others = pl.ds(0, across_y - 1)
    pltpu.make_async_copy(GA.at[others], GA.at[others], ga_recv).wait()
    row, col = iota((8, 8 * across_y), 0), iota((8, 8 * across_y), 1)
    spot, place = 2 * me_y + row, 2 * (col // 8) + col % 8
    valid = (row < 3) & (spot < 2 * across_y) & (col % 8 < 3) & (place < 2 * across_y)
    along = jnp.where(valid, gauss(spot - place, 2 * across_y), 0.0)
    value = jnp.dot(along, GA[...].reshape(8 * across_y, CZ), precision=HIGHEST, preferred_element_type=F32)
    lane16, row16 = iota((16, CZ), 1), iota((16, CZ), 0)
    keep = (lane16 // 8 == row16) & (row16 < 9)
    spread = jnp.concatenate(
        [jnp.where(keep, jnp.broadcast_to(value[y : y + 1], (16, CZ)), 0.0) for y in range(3)], axis=1
    )
    r, c = iota((3 * CZ, CZ), 0), iota((3 * CZ, CZ), 1)
    pick = (c == 8 * (r // CZ) + r % 8).astype(F32)
    GB[me_x] = jnp.dot(spread, pick, precision=HIGHEST, preferred_element_type=F32)

    def send_b(step, carry):
        remote(GB.at[me_x], GB.at[me_x], gb_send, gb_recv, gx=lax.rem(me_x + step, across_x)).start()
        return carry

    lax.fori_loop(1, across_x, send_b, 0)

    pl.when(jnp.logical_not(first_y))(y0_up.wait_recv)
    pl.when(jnp.logical_not(last_y))(y0_down.wait_recv)

    def outer_y(i, carry):
        C[4 + i, 0:8, :] = weighted([E[i, 4 + k : 12 + k, :] for k in range(9)], w0)
        C[4 + i, 24:32, :] = weighted([E[i, 28 + k : 36 + k, :] for k in range(9)], w0)
        return carry

    lax.fori_loop(0, 4, outer_y, 0)
    lax.fori_loop(CX - 4, CX, outer_y, 0)
    x0_up = remote(C.at[pl.ds(CX, 4)], C.at[pl.ds(0, 4)], x0_send.at[0], x0_recv.at[0], gx=above_x)
    x0_down = remote(C.at[pl.ds(4, 4)], C.at[pl.ds(CX + 4, 4)], x0_send.at[1], x0_recv.at[1], gx=below_x)
    pl.when(jnp.logical_not(last_x))(x0_up.start)
    pl.when(jnp.logical_not(first_x))(x0_down.start)
    lax.fori_loop(4, CX - 4, outer_y, 0, unroll=2)

    pl.when(jnp.logical_not(first_x))(x0_up.wait_recv)
    pl.when(jnp.logical_not(last_x))(x0_down.wait_recv)

    def finest_xz(i, carry):
        for t in range(4):
            rows = pl.ds(8 * t, 8)
            value = C[pl.ds(16 * i, 24), rows, :]
            moved = weighted([value[k : k + 16] for k in range(9)], w0)
            out[pl.ds(16 * i, 16), rows, :] = product(moved.reshape(128, CZ), W0[...]).reshape(16, 8, CZ)
        return carry

    lax.fori_loop(0, CX // 16, finest_xz, 0)

    pl.when(jnp.logical_not(first_y))(cy_up.wait_recv)
    pl.when(jnp.logical_not(last_y))(cy_down.wait_recv)
    pl.when(me_y >= 2)(c2_up.wait_recv)
    pl.when(me_y < across_y - 2)(c2_down.wait_recv)
    row8 = iota((8, CZ), 0)
    for level in (1, 2, 3):
        array, n, rows, count = B[level], NYL[level], ROWS[level], NXL[level] + 1
        wl = [taps[level, k] for k in range(2 * REACH + 1)]

        def along_y(x, carry, array=array, target=U[level], n=n, rows=rows, level=level, wl=wl):
            array[x, 4:12, :] = array[x, 4:12, :] + jnp.where(row8 < 5, YR[0, x], 0.0)
            array[x, 8 + n : 16 + n, :] = array[x, 8 + n : 16 + n, :] + jnp.where(row8 < 5, YR[1, x], 0.0)
            if level == 3:
                array[x, 4:5, :] = array[x, 4:5, :] + YR[0, x, 5:6, :]
                array[x, 16:17, :] = array[x, 16:17, :] + YR[1, x, 5:6, :]
            target[x] = weighted([array[x, 4 + k : 4 + k + rows, :] for k in range(9)], wl)
            return carry

        lax.fori_loop(0, count, along_y, 0)

        @pl.when(last_y)
        def _(target=U[level], n=n, count=count):
            target[:, n : n + 1, :] = jnp.zeros((count, 1, CZ), F32)

    others = pl.ds(0, across_x - 1)
    pltpu.make_async_copy(GB.at[others], GB.at[others], gb_recv).wait()
    row, col = iota((16, 16 * across_x), 0), iota((16, 16 * across_x), 1)
    spot, place = 8 * me_x + row, 8 * (col // 16) + col % 16
    valid = (row < 9) & (spot < 8 * across_x) & (col % 16 < 9) & (place < 8 * across_x)
    along = jnp.where(valid, gauss(spot - place, 8 * across_x), 0.0)
    value = jnp.dot(along, GB[...].reshape(16 * across_x, CZ), precision=HIGHEST, preferred_element_type=F32)
    keep = (lane8 // 8 == row8) & (lane8 < 24)
    spread = jnp.concatenate(
        [jnp.where(keep, jnp.broadcast_to(value[x : x + 1], (8, CZ)), 0.0) for x in range(9)], axis=0
    )
    r, c = iota((CZ, CZ), 0), iota((CZ, CZ), 1)
    pick = (c == 112 + r % 8).astype(F32)
    E4[:, 0:8, :] = jnp.dot(spread, pick, precision=HIGHEST, preferred_element_type=F32).reshape(9, 8, CZ)
    E4[:, 8:16, :] = jnp.zeros((9, 8, CZ), F32)

    for level, source, wide in ((3, E4, G3), (2, U3, G2), (1, U2, G1)):
        half = {3: 8, 2: 8, 1: 16}[level]
        target, rows, n = U[level], ROWS[level], NXL[level]
        first, cells = LANES[level]

        def widen(i, carry, source=source, wide=wide, half=half):
            low = source[i, pl.ds(0, half), :]
            wide[i, pl.ds(0, half, stride=2), :] = low
            if half == 8 and source is U3:
                high = pltpu.roll(low, 7, 0)
            elif half == 16:
                high = pltpu.roll(low, 15, 0)
            else:
                high = source[i, pl.ds(1, half), :]
            wide[i, pl.ds(1, half, stride=2), :] = 0.5 * (low + high)
            return carry

        lax.fori_loop(0, n // 2 + 1, widen, 0)
        lane = iota((rows, CZ), 1)
        own = (lane >= first) & (lane < first + cells)

        def climb(i, carry, target=target, wide=wide, rows=rows, own=own):
            low, high = wide[i, pl.ds(0, rows), :], wide[i + 1, pl.ds(0, rows), :]
            target[2 * i] = jnp.where(own, target[2 * i], low)
            target[2 * i + 1] = jnp.where(own, target[2 * i + 1], 0.5 * (low + high))
            return carry

        lax.fori_loop(0, n // 2, climb, 0)
        target[n] = jnp.where(own, target[n], wide[n // 2, pl.ds(0, rows), :])

    def rise_zy(i, carry):
        high, low = split(U1[pl.ds(i * 5, 5)].reshape(5 * 24, CZ))
        both = jnp.concatenate([high, low], axis=1)
        E1Z[pl.ds(i * 5, 5)] = jnp.dot(both, PZ[...], preferred_element_type=F32).reshape(5, 24, CZ)
        for j in range(5):
            x = i * 5 + j
            low, high = E1Z[x, 0:16, :], E1Z[x, 1:17, :]
            G0[x, pl.ds(0, 16, stride=2), :] = low
            G0[x, pl.ds(1, 16, stride=2), :] = 0.5 * (low + high)
        return carry

    lax.fori_loop(0, 13, rise_zy, 0)

    def finish(i, carry):
        low, high = G0[i], G0[i + 1]
        out[2 * i] = out[2 * i] + low
        out[2 * i + 1] = out[2 * i + 1] + 0.5 * (low + high)
        return carry

    lax.fori_loop(0, CX // 2, finish, 0)

    pl.when(jnp.logical_not(last_y))(y0_up.wait_send)
    pl.when(jnp.logical_not(first_y))(y0_down.wait_send)
    pl.when(jnp.logical_not(last_x))(x0_up.wait_send)
    pl.when(jnp.logical_not(first_x))(x0_down.wait_send)
    pl.when(jnp.logical_not(last_x))(cx_up.wait_send)
    pl.when(jnp.logical_not(first_x))(cx_down.wait_send)
    pl.when(jnp.logical_not(last_y))(cy_up.wait_send)
    pl.when(jnp.logical_not(first_y))(cy_down.wait_send)
    pl.when(me_y < across_y - 2)(c2_up.wait_send)
    pl.when(me_y >= 2)(c2_down.wait_send)
    others = pl.ds(0, across_y - 1)
    pltpu.make_async_copy(GA.at[others], GA.at[others], ga_send).wait()
    others = pl.ds(0, across_x - 1)
    pltpu.make_async_copy(GB.at[others], GB.at[others], gb_send).wait()


def solution(mesh):
    across_x, across_y = mesh.shape["gx"], mesh.shape["gy"]

    def vmem(*shape, dtype=F32):
        return pltpu.VMEM(shape, dtype)

    pair = pltpu.SemaphoreType.DMA((2,))
    single = pltpu.SemaphoreType.DMA
    scratch = [
        vmem(CX, 48, CZ),
        vmem(CX + 8, CY, CZ),
        vmem(65, 56, CZ), vmem(33, 40, CZ), vmem(17, 24, CZ), vmem(9, 24, CZ),
        vmem(73, 24, CZ), vmem(41, 16, CZ), vmem(25, 8, CZ), vmem(9, 8, CZ),
        vmem(65, 40, CZ), vmem(33, 32, CZ), vmem(17, 24, CZ),
        vmem(65, 24, CZ), vmem(33, 16, CZ), vmem(17, 8, CZ),
        vmem(9, 16, CZ), vmem(9, 16, CZ), vmem(17, 16, CZ), vmem(33, 32, CZ), vmem(65, 32, CZ),
        vmem(2, 5, 24, CZ), vmem(2, 5, 24, CZ),
        vmem(2, 65, 8, CZ), vmem(2, 65, 8, CZ),
        vmem(across_y, 8, CZ), vmem(across_x, 16, CZ),
        vmem(3 * CZ, CZ, dtype=BF16), vmem(3 * CZ, CZ, dtype=BF16), vmem(2 * CZ, CZ, dtype=BF16),
        vmem(65, 24, CZ),
        pltpu.SemaphoreType.DMA((4,)),
        pair, pair, pair, pair, pair, pair, pair, pair, pair, pair,
        single, single, single, single,
    ]

    def local(charge, level_taps):
        return pl.pallas_call(
            functools.partial(kernel, across_x, across_y),
            out_shape=jax.ShapeDtypeStruct((CX, CY, CZ), F32),
            in_specs=[pl.BlockSpec(memory_space=pltpu.SMEM), pl.BlockSpec(memory_space=pl.ANY)],
            out_specs=pl.BlockSpec(memory_space=pltpu.VMEM),
            scratch_shapes=scratch,
            compiler_params=pltpu.CompilerParams(
                collective_id=0, has_side_effects=True, vmem_limit_bytes=48 * 1024 * 1024
            ),
        )(level_taps, charge)

    spec = P("gx", "gy", None)
    return jax.shard_map(local, mesh=mesh, in_specs=(spec, P()), out_specs=spec, check_vma=False)
```

```python
import functools
import math

import jax
import jax.numpy as jnp
from jax import lax
from jax.experimental import pallas as pl
from jax.experimental.pallas import tpu as pltpu
from jax.sharding import PartitionSpec as P

F32 = jnp.float32
BF16 = jnp.bfloat16
HIGHEST = lax.Precision.HIGHEST
MESH = pl.DeviceIdType.MESH

CX, CY, CZ = 128, 32, 128
REACH = 4
LANES = {1: (0, 64), 2: (64, 32), 3: (96, 16), 4: (112, 8)}
NXL = {1: 64, 2: 32, 3: 16, 4: 8}
NYL = {1: 16, 2: 8, 3: 4, 4: 2}
ROWS = {1: 24, 2: 16, 3: 8, 4: 8}


def iota(shape, dim):
    return lax.broadcasted_iota(jnp.int32, shape, dim)


def gauss(distance, length):
    spread = max(length, 4) / 2.0
    scaled = distance.astype(F32) / spread
    return jnp.exp(-scaled * scaled) / (math.sqrt(math.pi) * spread)


def split(value):
    high = value.astype(BF16)
    return high, (value - high.astype(F32)).astype(BF16)


def stacked(matrix):
    high, low = split(matrix)
    upper = jnp.concatenate([high, low], axis=1)
    lower = jnp.concatenate([high, jnp.zeros_like(high)], axis=1)
    return jnp.concatenate([upper, lower], axis=0)


def product(value, weights):
    high, low = split(value)
    both = jnp.dot(jnp.concatenate([high, low], axis=1), weights, preferred_element_type=F32)
    return both[:, :CZ] + both[:, CZ:]


def toeplitz(taps, level, shape, offset):
    matrix = jnp.zeros(shape, F32)
    for k in range(2 * REACH + 1):
        matrix = jnp.where(offset == k - REACH, taps[level, k], matrix)
    return matrix


def coarse_z(taps):
    a, c = iota((CZ, CZ), 0), iota((CZ, CZ), 1)
    down = jnp.zeros((CZ, CZ), F32)
    mix = jnp.zeros((CZ, CZ), F32)
    for level, (first, cells) in LANES.items():
        step = 2**level
        here = (c >= first) & (c < first + cells)
        weight = jnp.maximum(0, step - jnp.abs(a - step * (c - first)))
        down = jnp.where(here, weight.astype(F32) * 2.0 ** (-5 * level), down)
        inside = here & (a >= first) & (a < first + cells)
        if level < 4:
            block = toeplitz(taps, level, (CZ, CZ), a - c)
        else:
            block = gauss(a - c, cells)
        mix = jnp.where(inside, block, mix)
    return jnp.dot(down, mix, precision=HIGHEST, preferred_element_type=F32)


def prolong_z():
    r, a = iota((CZ, CZ), 0), iota((CZ, CZ), 1)
    up = jnp.zeros((CZ, CZ), F32)
    for level, (first, cells) in LANES.items():
        step = 2**level
        here = (r >= first) & (r < first + cells)
        weight = jnp.maximum(0, step - jnp.abs(a - step * (r - first)))
        up = jnp.where(here, weight.astype(F32) * 2.0**-level, up)
    return up.astype(BF16)


def weighted(pieces, weights):
    total = weights[REACH] * pieces[REACH]
    for k in range(REACH):
        total = total + weights[k] * (pieces[k] + pieces[2 * REACH - k])
    return total


def kernel(
    across_x, across_y, taps_in, q, out,
    taps,
    E, C, T1, T2, T3, T4, A1, A2, A3, A4, B1, B2, B3, U1, U2, U3, E4, G3, G2, G1, G0,
    XS, XR, YS, YR, GA, GB, WZ, W0, PZ, E1Z,
    taps_sem, in_sem, y0_send, y0_recv, x0_send, x0_recv, cx_send, cx_recv, cy_send, cy_recv,
    c2_send, c2_recv, ga_send, ga_recv, gb_send, gb_recv,
):
    me_x, me_y = lax.axis_index("gx"), lax.axis_index("gy")
    first_x, last_x = me_x == 0, me_x == across_x - 1
    first_y, last_y = me_y == 0, me_y == across_y - 1
    A, B, U, T = {1: A1, 2: A2, 3: A3}, {1: B1, 2: B2, 3: B3}, {1: U1, 2: U2, 3: U3}, {2: T2, 3: T3, 4: T4}

    few = pltpu.make_async_copy(taps_in, taps, taps_sem)
    few.start()
    barrier = pltpu.get_barrier_semaphore()

    def greet_y(step, carry):
        pl.semaphore_signal(barrier, inc=1, device_id={"gy": lax.rem(me_y + step, across_y)}, device_id_type=MESH)
        return carry

    def greet_x(step, carry):
        pl.semaphore_signal(barrier, inc=1, device_id={"gx": lax.rem(me_x + step, across_x)}, device_id_type=MESH)
        return carry

    lax.fori_loop(1, across_y, greet_y, 0)
    lax.fori_loop(1, across_x, greet_x, 0)

    parts = 4
    depth = CX // parts
    loads = [
        pltpu.make_async_copy(
            q.at[pl.ds(i * depth, depth)], E.at[pl.ds(i * depth, depth), pl.ds(8, CY)], in_sem.at[i]
        )
        for i in range(parts)
    ]
    for load in loads:
        load.start()

    few.wait()
    WZ[...] = stacked(coarse_z(taps))
    W0[...] = stacked(toeplitz(taps, 0, (CZ, CZ), iota((CZ, CZ), 0) - iota((CZ, CZ), 1)))
    rise = prolong_z()
    PZ[...] = jnp.concatenate([rise, rise], axis=0)

    def blank(ref, count, *spans):
        for start, size in spans:
            ref[:, start : start + size, :] = jnp.zeros((count, size, CZ), F32)

    blank(T1, 65, (0, 8), (40, 16))
    blank(T2, 33, (0, 8), (32, 8))
    blank(T3, 17, (0, 8))
    blank(T4, 9, (0, 8), (16, 8))
    for level in (1, 2, 3):
        blank(B[level], NXL[level] + 1, (0, 8), *(((16, 8),) if level == 3 else ()))
        rows = ROWS[level]
        A[level][0:4] = jnp.zeros((4, rows, CZ), F32)
        A[level][NXL[level] + 5 : NXL[level] + 9] = jnp.zeros((4, rows, CZ), F32)

    @pl.when(first_y)
    def _():
        E[:, 4:8, :] = jnp.zeros((CX, 4, CZ), F32)
        YR[0, :, 0:5, :] = jnp.zeros((65, 5, CZ), F32)

    @pl.when(last_y)
    def _():
        E[:, 40:44, :] = jnp.zeros((CX, 4, CZ), F32)
        YR[1, :, 0:5, :] = jnp.zeros((65, 5, CZ), F32)

    @pl.when(me_y < 2)
    def _():
        YR[0, 0:17, 5:6, :] = jnp.zeros((17, 1, CZ), F32)

    @pl.when(me_y >= across_y - 2)
    def _():
        YR[1, 0:17, 5:6, :] = jnp.zeros((17, 1, CZ), F32)

    @pl.when(first_x)
    def _():
        C[0:4] = jnp.zeros((4, CY, CZ), F32)
        XR[0] = jnp.zeros((5, 24, CZ), F32)

    @pl.when(last_x)
    def _():
        C[CX + 4 : CX + 8] = jnp.zeros((4, CY, CZ), F32)
        XR[1] = jnp.zeros((5, 24, CZ), F32)

    pl.semaphore_wait(barrier, across_x + across_y - 2)

    def remote(src, dst, send, recv, **target):
        return pltpu.make_async_remote_copy(
            src_ref=src, dst_ref=dst, send_sem=send, recv_sem=recv, device_id=target, device_id_type=MESH
        )

    above_y, below_y = lax.rem(me_y + 1, across_y), lax.rem(me_y + across_y - 1, across_y)
    above_x, below_x = lax.rem(me_x + 1, across_x), lax.rem(me_x + across_x - 1, across_x)

    y0_up = remote(q.at[:, pl.ds(CY - 4, 4)], E.at[:, pl.ds(4, 4)], y0_send.at[0], y0_recv.at[0], gy=above_y)
    y0_down = remote(q.at[:, pl.ds(0, 4)], E.at[:, pl.ds(40, 4)], y0_send.at[1], y0_recv.at[1], gy=below_y)
    pl.when(jnp.logical_not(last_y))(y0_up.start)
    pl.when(jnp.logical_not(first_y))(y0_down.start)

    for load in loads:
        load.wait()

    T1[0, 8:40, :] = 2.0 * E[0, 8:40, :] + E[1, 8:40, :]
    T1[64, 8:40, :] = E[CX - 1, 8:40, :]

    def down_x(i, carry):
        T1[i, 8:40, :] = E[2 * i - 1, 8:40, :] + 2.0 * E[2 * i, 8:40, :] + E[2 * i + 1, 8:40, :]
        return carry

    lax.fori_loop(1, 64, down_x, 0, unroll=3)

    def down_y(i, carry):
        E1Z[i] = (
            T1[i, pl.ds(7, 24, stride=2), :] + 2.0 * T1[i, pl.ds(8, 24, stride=2), :] + T1[i, pl.ds(9, 24, stride=2), :]
        )
        return carry

    lax.fori_loop(0, 65, down_y, 0, unroll=5)

    A1[4:69] = product(E1Z[...].reshape(66 * 24, CZ), WZ[...]).reshape(66, 24, CZ)[0:65]

    for level in (2, 3, 4):
        finer, mid = A[level - 1], T[level]
        coarser, shift = (A[level], 4) if level < 4 else (A4, 0)
        inner, rows = ROWS[level - 1], ROWS[level]

        n = NXL[level]
        pairs = finer[4 : 2 * n + 4].reshape(n, 2, inner, CZ)
        even, odd = pairs[:, 0], pairs[:, 1]
        mid[0:n, 8 : 8 + inner, :] = 2.0 * even + odd + finer[3 : 2 * n + 3].reshape(n, 2, inner, CZ)[:, 0]
        mid[n, 8 : 8 + inner, :] = finer[2 * n + 3] + 2.0 * finer[2 * n + 4]
        coarser[shift : shift + n + 1] = (
            mid[:, pl.ds(7, rows, stride=2), :]
            + 2.0 * mid[:, pl.ds(8, rows, stride=2), :]
            + mid[:, pl.ds(9, rows, stride=2), :]
        )

    lane8 = iota((8, CZ), 1)
    message = jnp.zeros((8, CZ), F32)
    for x in range(9):
        value = jnp.where((lane8 >= 112) & (lane8 < 120), A4[x], 0.0)
        message = message + pltpu.roll(value, (8 * x - 112) % CZ, 1)
    GA[me_y] = message

    def send_a(step, carry):
        remote(GA.at[me_y], GA.at[me_y], ga_send, ga_recv, gy=lax.rem(me_y + step, across_y)).start()
        return carry

    lax.fori_loop(1, across_y, send_a, 0)

    @pl.when(last_x)
    def _():
        for level in (1, 2, 3):
            A[level][NXL[level] + 4] = jnp.zeros((ROWS[level], CZ), F32)

    for way in (0, 1):
        for i in range(5):
            at = {level: (NXL[level] if way == 0 else 4) + i for level in (1, 2, 3)}
            wide = A1[at[1]]
            lane = iota((24, CZ), 1)
            XS[way, i] = jnp.where(lane < 64, wide, 0.0)
            lane = iota((16, CZ), 1)
            XS[way, i, 0:16, :] = jnp.where(lane >= 64, A2[at[2]], XS[way, i, 0:16, :])
            lane = iota((8, CZ), 1)
            XS[way, i, 0:8, :] = jnp.where(lane >= 96, A3[at[3]], XS[way, i, 0:8, :])
    cx_up = remote(XS.at[0], XR.at[0], cx_send.at[0], cx_recv.at[0], gx=above_x)
    cx_down = remote(XS.at[1], XR.at[1], cx_send.at[1], cx_recv.at[1], gx=below_x)
    pl.when(jnp.logical_not(last_x))(cx_up.start)
    pl.when(jnp.logical_not(first_x))(cx_down.start)

    w0 = [taps[0, k] for k in range(2 * REACH + 1)]

    def mid_y(i, carry):
        C[4 + i, 8:24, :] = weighted([E[i, 12 + k : 28 + k, :] for k in range(9)], w0)
        return carry

    lax.fori_loop(0, CX, mid_y, 0, unroll=2)

    pl.when(jnp.logical_not(first_x))(cx_up.wait_recv)
    pl.when(jnp.logical_not(last_x))(cx_down.wait_recv)
    for level in (1, 2, 3):
        array, rows, n = A[level], ROWS[level], NXL[level]
        array[0:4] = XR[0, 0:4, 0:rows, :]
        array[4] = array[4] + XR[0, 4, 0:rows, :]
        array[n + 4] = array[n + 4] + XR[1, 0, 0:rows, :]
        array[n + 5 : n + 9] = XR[1, 1:5, 0:rows, :]
        wl = [taps[level, k] for k in range(2 * REACH + 1)]

        def along_x(i, carry, array=array, target=B[level], rows=rows, wl=wl):
            target[i, pl.ds(8, rows), :] = weighted([array[i + k] for k in range(9)], wl)
            return carry

        lax.fori_loop(0, n + 1, along_x, 0, unroll={1: 5, 2: 3, 3: 1}[level])

        @pl.when(last_x)
        def _(target=B[level], rows=rows, n=n):
            target[n, pl.ds(8, rows), :] = jnp.zeros((rows, CZ), F32)

        @pl.when(last_y)
        def _(target=B[level], level=level, n=n):
            target[:, pl.ds(8 + NYL[level], 1), :] = jnp.zeros((n + 1, 1, CZ), F32)

    lane = iota((8, CZ), 1)
    for way in (0, 1):
        start = {level: 8 + (NYL[level] - 4 if way == 0 else 0) for level in (1, 2, 3)}
        YS[way] = B1[:, start[1] : start[1] + 8, :]
        YS[way, 0:33] = jnp.where(lane >= 64, B2[:, start[2] : start[2] + 8, :], B1[0:33, start[1] : start[1] + 8, :])
        YS[way, 0:17] = jnp.where(lane >= 96, B3[:, start[3] : start[3] + 8, :], YS[way, 0:17])
    rows5 = pl.ds(0, 5)
    cy_up = remote(YS.at[0, :, rows5], YR.at[0, :, rows5], cy_send.at[0], cy_recv.at[0], gy=above_y)
    cy_down = remote(YS.at[1, :, rows5], YR.at[1, :, rows5], cy_send.at[1], cy_recv.at[1], gy=below_y)
    pl.when(jnp.logical_not(last_y))(cy_up.start)
    pl.when(jnp.logical_not(first_y))(cy_down.start)
    near, far = pl.ds(0, 17), pl.ds(5, 1)
    c2_up = remote(
        YS.at[0, near, pl.ds(4, 1)], YR.at[0, near, far], c2_send.at[0], c2_recv.at[0],
        gy=lax.rem(me_y + 2, across_y),
    )
    c2_down = remote(
        YS.at[1, near, pl.ds(0, 1)], YR.at[1, near, far], c2_send.at[1], c2_recv.at[1],
        gy=lax.rem(me_y + across_y - 2, across_y),
    )
    pl.when(me_y < across_y - 2)(c2_up.start)
    pl.when(me_y >= 2)(c2_down.start)

    others = pl.ds(0, across_y - 1)
    pltpu.make_async_copy(GA.at[others], GA.at[others], ga_recv).wait()
    row, col = iota((8, 8 * across_y), 0), iota((8, 8 * across_y), 1)
    spot, place = 2 * me_y + row, 2 * (col // 8) + col % 8
    valid = (row < 3) & (spot < 2 * across_y) & (col % 8 < 3) & (place < 2 * across_y)
    along = jnp.where(valid, gauss(spot - place, 2 * across_y), 0.0)
    value = jnp.dot(along, GA[...].reshape(8 * across_y, CZ), precision=HIGHEST, preferred_element_type=F32)
    lane16, row16 = iota((16, CZ), 1), iota((16, CZ), 0)
    keep = (lane16 // 8 == row16) & (row16 < 9)
    spread = jnp.concatenate(
        [jnp.where(keep, jnp.broadcast_to(value[y : y + 1], (16, CZ)), 0.0) for y in range(3)], axis=1
    )
    r, c = iota((3 * CZ, CZ), 0), iota((3 * CZ, CZ), 1)
    pick = (c == 8 * (r // CZ) + r % 8).astype(F32)
    GB[me_x] = jnp.dot(spread, pick, precision=HIGHEST, preferred_element_type=F32)

    def send_b(step, carry):
        remote(GB.at[me_x], GB.at[me_x], gb_send, gb_recv, gx=lax.rem(me_x + step, across_x)).start()
        return carry

    lax.fori_loop(1, across_x, send_b, 0)

    pl.when(jnp.logical_not(first_y))(y0_up.wait_recv)
    pl.when(jnp.logical_not(last_y))(y0_down.wait_recv)

    def outer_y(i, carry):
        C[4 + i, 0:8, :] = weighted([E[i, 4 + k : 12 + k, :] for k in range(9)], w0)
        C[4 + i, 24:32, :] = weighted([E[i, 28 + k : 36 + k, :] for k in range(9)], w0)
        return carry

    lax.fori_loop(0, 4, outer_y, 0)
    lax.fori_loop(CX - 4, CX, outer_y, 0)
    x0_up = remote(C.at[pl.ds(CX, 4)], C.at[pl.ds(0, 4)], x0_send.at[0], x0_recv.at[0], gx=above_x)
    x0_down = remote(C.at[pl.ds(4, 4)], C.at[pl.ds(CX + 4, 4)], x0_send.at[1], x0_recv.at[1], gx=below_x)
    pl.when(jnp.logical_not(last_x))(x0_up.start)
    pl.when(jnp.logical_not(first_x))(x0_down.start)
    lax.fori_loop(4, CX - 4, outer_y, 0, unroll=2)

    pl.when(jnp.logical_not(first_x))(x0_up.wait_recv)
    pl.when(jnp.logical_not(last_x))(x0_down.wait_recv)

    def finest_x(i, carry):
        w0 = [taps[0, k] for k in range(2 * REACH + 1)]
        for t in range(4):
            rows = pl.ds(8 * t, 8)
            value = C[pl.ds(16 * i, 24), rows, :]
            out[pl.ds(16 * i, 16), rows, :] = weighted([value[k : k + 16] for k in range(9)], w0)
        return carry

    lax.fori_loop(0, CX // 16, finest_x, 0)

    out[...] = product(out[...].reshape(CX * CY, CZ), W0[...]).reshape(CX, CY, CZ)

    pl.when(jnp.logical_not(first_y))(cy_up.wait_recv)
    pl.when(jnp.logical_not(last_y))(cy_down.wait_recv)
    pl.when(me_y >= 2)(c2_up.wait_recv)
    pl.when(me_y < across_y - 2)(c2_down.wait_recv)
    row8 = iota((8, CZ), 0)
    for level in (1, 2, 3):
        array, n, rows, count = B[level], NYL[level], ROWS[level], NXL[level] + 1
        wl = [taps[level, k] for k in range(2 * REACH + 1)]

        def along_y(x, carry, array=array, target=U[level], n=n, rows=rows, level=level, wl=wl):
            array[x, 4:12, :] = array[x, 4:12, :] + jnp.where(row8 < 5, YR[0, x], 0.0)
            array[x, 8 + n : 16 + n, :] = array[x, 8 + n : 16 + n, :] + jnp.where(row8 < 5, YR[1, x], 0.0)
            if level == 3:
                array[x, 4:5, :] = array[x, 4:5, :] + YR[0, x, 5:6, :]
                array[x, 16:17, :] = array[x, 16:17, :] + YR[1, x, 5:6, :]
            target[x] = weighted([array[x, 4 + k : 4 + k + rows, :] for k in range(9)], wl)
            return carry

        lax.fori_loop(0, count, along_y, 0, unroll={1: 5, 2: 3, 3: 1}[level])

        @pl.when(last_y)
        def _(target=U[level], n=n, count=count):
            target[0:count, n : n + 1, :] = jnp.zeros((count, 1, CZ), F32)

    others = pl.ds(0, across_x - 1)
    pltpu.make_async_copy(GB.at[others], GB.at[others], gb_recv).wait()
    row, col = iota((16, 16 * across_x), 0), iota((16, 16 * across_x), 1)
    spot, place = 8 * me_x + row, 8 * (col // 16) + col % 16
    valid = (row < 9) & (spot < 8 * across_x) & (col % 16 < 9) & (place < 8 * across_x)
    along = jnp.where(valid, gauss(spot - place, 8 * across_x), 0.0)
    value = jnp.dot(along, GB[...].reshape(16 * across_x, CZ), precision=HIGHEST, preferred_element_type=F32)
    keep = (lane8 // 8 == row8) & (lane8 < 24)
    spread = jnp.concatenate(
        [jnp.where(keep, jnp.broadcast_to(value[x : x + 1], (8, CZ)), 0.0) for x in range(9)], axis=0
    )
    r, c = iota((CZ, CZ), 0), iota((CZ, CZ), 1)
    pick = (c == 112 + r % 8).astype(F32)
    E4[:, 0:8, :] = jnp.dot(spread, pick, precision=HIGHEST, preferred_element_type=F32).reshape(9, 8, CZ)
    E4[:, 8:16, :] = jnp.zeros((9, 8, CZ), F32)

    for level, source, wide in ((3, E4, G3), (2, U3, G2), (1, U2, G1)):
        half = {3: 8, 2: 8, 1: 16}[level]
        target, rows, n = U[level], ROWS[level], NXL[level]
        first, cells = LANES[level]

        low = source[:, 0:half, :]
        if half == source.shape[1]:
            high = pltpu.roll(low, half - 1, 1)
        else:
            high = source[:, 1 : half + 1, :]
        wide[:, pl.ds(0, half, stride=2), :] = low
        wide[:, pl.ds(1, half, stride=2), :] = 0.5 * (low + high)
        lane = iota((rows, CZ), 1)
        own = (lane >= first) & (lane < first + cells)
        low, high = wide[0 : n // 2, 0:rows, :], wide[1 : n // 2 + 1, 0:rows, :]
        both = jnp.stack([low, 0.5 * (low + high)], axis=1).reshape(n, rows, CZ)
        target[0:n] = jnp.where(own, target[0:n], both)
        target[n] = jnp.where(own, target[n], wide[n // 2, 0:rows, :])

    high, low = split(U1[...].reshape(66 * 24, CZ))
    both = jnp.concatenate([high, low], axis=1)
    E1Z[...] = jnp.dot(both, PZ[...], preferred_element_type=F32).reshape(66, 24, CZ)

    def rise_y(x, carry):
        low, high = E1Z[x, 0:16, :], E1Z[x, 1:17, :]
        G0[x, pl.ds(0, 16, stride=2), :] = low
        G0[x, pl.ds(1, 16, stride=2), :] = 0.5 * (low + high)
        return carry

    lax.fori_loop(0, 65, rise_y, 0, unroll=5)

    def finish(i, carry):
        low, high = G0[i], G0[i + 1]
        out[2 * i] = out[2 * i] + low
        out[2 * i + 1] = out[2 * i + 1] + 0.5 * (low + high)
        return carry

    lax.fori_loop(0, CX // 2, finish, 0, unroll=2)

    pl.when(jnp.logical_not(last_y))(y0_up.wait_send)
    pl.when(jnp.logical_not(first_y))(y0_down.wait_send)
    pl.when(jnp.logical_not(last_x))(x0_up.wait_send)
    pl.when(jnp.logical_not(first_x))(x0_down.wait_send)
    pl.when(jnp.logical_not(last_x))(cx_up.wait_send)
    pl.when(jnp.logical_not(first_x))(cx_down.wait_send)
    pl.when(jnp.logical_not(last_y))(cy_up.wait_send)
    pl.when(jnp.logical_not(first_y))(cy_down.wait_send)
    pl.when(me_y < across_y - 2)(c2_up.wait_send)
    pl.when(me_y >= 2)(c2_down.wait_send)
    others = pl.ds(0, across_y - 1)
    pltpu.make_async_copy(GA.at[others], GA.at[others], ga_send).wait()
    others = pl.ds(0, across_x - 1)
    pltpu.make_async_copy(GB.at[others], GB.at[others], gb_send).wait()


def solution(mesh):
    across_x, across_y = mesh.shape["gx"], mesh.shape["gy"]

    def vmem(*shape, dtype=F32):
        return pltpu.VMEM(shape, dtype)

    pair = pltpu.SemaphoreType.DMA((2,))
    single = pltpu.SemaphoreType.DMA
    scratch = [
        pltpu.SMEM((4, 9), F32),
        vmem(CX, 48, CZ),
        vmem(CX + 8, CY, CZ),
        vmem(65, 56, CZ), vmem(33, 40, CZ), vmem(17, 24, CZ), vmem(9, 24, CZ),
        vmem(73, 24, CZ), vmem(41, 16, CZ), vmem(25, 8, CZ), vmem(9, 8, CZ),
        vmem(65, 40, CZ), vmem(33, 32, CZ), vmem(17, 24, CZ),
        vmem(66, 24, CZ), vmem(33, 16, CZ), vmem(17, 8, CZ),
        vmem(9, 16, CZ), vmem(9, 16, CZ), vmem(17, 16, CZ), vmem(33, 32, CZ), vmem(65, 32, CZ),
        vmem(2, 5, 24, CZ), vmem(2, 5, 24, CZ),
        vmem(2, 65, 8, CZ), vmem(2, 65, 8, CZ),
        vmem(across_y, 8, CZ), vmem(across_x, 16, CZ),
        vmem(2 * CZ, 2 * CZ, dtype=BF16), vmem(2 * CZ, 2 * CZ, dtype=BF16), vmem(2 * CZ, CZ, dtype=BF16),
        vmem(66, 24, CZ),
        single, pltpu.SemaphoreType.DMA((4,)),
        pair, pair, pair, pair, pair, pair, pair, pair, pair, pair,
        single, single, single, single,
    ]

    def local(charge, level_taps):
        return pl.pallas_call(
            functools.partial(kernel, across_x, across_y),
            out_shape=jax.ShapeDtypeStruct((CX, CY, CZ), F32),
            in_specs=[pl.BlockSpec(memory_space=pltpu.HBM), pl.BlockSpec(memory_space=pltpu.HBM)],
            out_specs=pl.BlockSpec(memory_space=pltpu.VMEM),
            scratch_shapes=scratch,
            compiler_params=pltpu.CompilerParams(
                collective_id=0, has_side_effects=True, vmem_limit_bytes=48 * 1024 * 1024
            ),
        )(*(pltpu.with_memory_space_constraint(array, pltpu.HBM) for array in (level_taps, charge)))

    spec = P("gx", "gy", None)
    return jax.shard_map(local, mesh=mesh, in_specs=(spec, P()), out_specs=spec, check_vma=False)
```

```python
import functools
import math

import jax
import jax.numpy as jnp
from jax import lax
from jax.experimental import pallas as pl
from jax.experimental.pallas import tpu as pltpu
from jax.sharding import PartitionSpec as P

F32 = jnp.float32
BF16 = jnp.bfloat16
HIGHEST = lax.Precision.HIGHEST
MESH = pl.DeviceIdType.MESH

CX, CY, CZ = 128, 32, 128
REACH = 4
LANES = {1: (0, 64), 2: (64, 32), 3: (96, 16), 4: (112, 8)}
NXL = {1: 64, 2: 32, 3: 16, 4: 8}
NYL = {1: 16, 2: 8, 3: 4, 4: 2}
ROWS = {1: 24, 2: 16, 3: 8, 4: 8}


def iota(shape, dim):
    return lax.broadcasted_iota(jnp.int32, shape, dim)


def gauss(distance, length):
    spread = max(length, 4) / 2.0
    scaled = distance.astype(F32) / spread
    return jnp.exp(-scaled * scaled) / (math.sqrt(math.pi) * spread)


def split(value):
    high = value.astype(BF16)
    return high, (value - high.astype(F32)).astype(BF16)


def stacked(matrix):
    high, low = split(matrix)
    upper = jnp.concatenate([high, low], axis=1)
    lower = jnp.concatenate([high, jnp.zeros_like(high)], axis=1)
    return jnp.concatenate([upper, lower], axis=0)


def product(value, weights):
    high, low = split(value)
    both = jnp.dot(jnp.concatenate([high, low], axis=1), weights, preferred_element_type=F32)
    return both[:, :CZ] + both[:, CZ:]


def toeplitz(taps, level, shape, offset):
    matrix = jnp.zeros(shape, F32)
    for k in range(2 * REACH + 1):
        matrix = jnp.where(offset == k - REACH, taps[level, k], matrix)
    return matrix


def coarse_z(taps):
    a, c = iota((CZ, CZ), 0), iota((CZ, CZ), 1)
    down = jnp.zeros((CZ, CZ), F32)
    mix = jnp.zeros((CZ, CZ), F32)
    for level, (first, cells) in LANES.items():
        step = 2**level
        here = (c >= first) & (c < first + cells)
        weight = jnp.maximum(0, step - jnp.abs(a - step * (c - first)))
        down = jnp.where(here, weight.astype(F32) * 2.0 ** (-5 * level), down)
        inside = here & (a >= first) & (a < first + cells)
        if level < 4:
            block = toeplitz(taps, level, (CZ, CZ), a - c)
        else:
            block = gauss(a - c, cells)
        mix = jnp.where(inside, block, mix)
    return jnp.dot(down, mix, precision=HIGHEST, preferred_element_type=F32)


def prolong_z():
    r, a = iota((CZ, CZ), 0), iota((CZ, CZ), 1)
    up = jnp.zeros((CZ, CZ), F32)
    for level, (first, cells) in LANES.items():
        step = 2**level
        here = (r >= first) & (r < first + cells)
        weight = jnp.maximum(0, step - jnp.abs(a - step * (r - first)))
        up = jnp.where(here, weight.astype(F32) * 2.0**-level, up)
    return up.astype(BF16)


def weighted(pieces, weights):
    total = weights[REACH] * pieces[REACH]
    for k in range(REACH):
        total = total + weights[k] * (pieces[k] + pieces[2 * REACH - k])
    return total


def kernel(
    across_x, across_y, taps_in, q, out, coarsest, slopes,
    taps,
    E, C, T1, T2, T3, T4, A1, A2, A3, A4, B1, B2, B3, U1, U2, U3, G2, G1, G0,
    XS, XR, YS, YR, GA, GB, WZ, W0, PZ, P4, E1Z,
    taps_sem, in_sem, y0_send, y0_recv, x0_send, x0_recv, cx_send, cx_recv, cy_send, cy_recv,
    c2_send, c2_recv, ga_send, ga_recv, gc_send, gc_recv, gb_send, gb_recv,
):
    me_x, me_y = lax.axis_index("gx"), lax.axis_index("gy")
    first_x, last_x = me_x == 0, me_x == across_x - 1
    first_y, last_y = me_y == 0, me_y == across_y - 1
    A, B, U, T = {1: A1, 2: A2, 3: A3}, {1: B1, 2: B2, 3: B3}, {1: U1, 2: U2, 3: U3}, {2: T2, 3: T3, 4: T4}

    few = pltpu.make_async_copy(taps_in, taps, taps_sem)
    few.start()
    barrier = pltpu.get_barrier_semaphore()

    group = min(8, across_y)
    groups = across_y // group
    rank, base = lax.rem(me_y, group), me_y - lax.rem(me_y, group)
    mates = [base + lax.rem(rank + s, group) for s in range(1, group)]
    peers = [lax.rem(me_y + group * s, across_y) for s in range(1, groups)]
    columns = [lax.rem(me_x + s, across_x) for s in range(1, across_x)]
    steps = (1, 2, across_y - 2, across_y - 1) if across_y > 4 else ()
    around = [lax.rem(me_y + s, across_y) for s in steps]
    for y in around + mates + peers:
        pl.semaphore_signal(barrier, inc=1, device_id={"gy": y}, device_id_type=MESH)
    for x in columns:
        pl.semaphore_signal(barrier, inc=1, device_id={"gx": x}, device_id_type=MESH)

    parts = 4
    depth = CX // parts
    loads = [
        pltpu.make_async_copy(
            q.at[pl.ds(i * depth, depth)], E.at[pl.ds(i * depth, depth), pl.ds(8, CY)], in_sem.at[i]
        )
        for i in range(parts)
    ]
    for load in loads:
        load.start()

    def blank(ref, count, *spans):
        for start, size in spans:
            ref[:, start : start + size, :] = jnp.zeros((count, size, CZ), F32)

    blank(T1, 65, (0, 8), (40, 16))
    blank(T2, 33, (0, 8), (32, 8))
    blank(T3, 17, (0, 8))
    blank(T4, 9, (0, 8), (16, 8))
    for level in (1, 2, 3):
        blank(B[level], NXL[level] + 1, (0, 8), *(((16, 8),) if level == 3 else ()))
        rows = ROWS[level]
        A[level][0:4] = jnp.zeros((4, rows, CZ), F32)
        A[level][NXL[level] + 5 : NXL[level] + 9] = jnp.zeros((4, rows, CZ), F32)

    @pl.when(first_y)
    def _():
        E[:, 4:8, :] = jnp.zeros((CX, 4, CZ), F32)
        YR[0, :, 0:5, :] = jnp.zeros((65, 5, CZ), F32)

    @pl.when(last_y)
    def _():
        E[:, 40:44, :] = jnp.zeros((CX, 4, CZ), F32)
        YR[1, :, 0:5, :] = jnp.zeros((65, 5, CZ), F32)

    @pl.when(me_y < 2)
    def _():
        YR[0, 0:17, 5:6, :] = jnp.zeros((17, 1, CZ), F32)

    @pl.when(me_y >= across_y - 2)
    def _():
        YR[1, 0:17, 5:6, :] = jnp.zeros((17, 1, CZ), F32)

    @pl.when(first_x)
    def _():
        C[0:4] = jnp.zeros((4, CY, CZ), F32)
        XR[0] = jnp.zeros((5, 24, CZ), F32)

    @pl.when(last_x)
    def _():
        C[CX + 4 : CX + 8] = jnp.zeros((4, CY, CZ), F32)
        XR[1] = jnp.zeros((5, 24, CZ), F32)

    rise = prolong_z()
    PZ[...] = jnp.concatenate([rise, rise], axis=0)
    r, a = iota((CZ, CZ), 0), iota((CZ, CZ), 1)
    rise = jnp.maximum(0, 16 - jnp.abs(a - 16 * (r % 8))).astype(F32) / 16.0
    rise = jnp.where(r < 24, rise, 0.0).astype(BF16)
    P4[...] = jnp.concatenate([rise, rise], axis=0)

    pl.semaphore_wait(barrier, len(around + mates + peers + columns))

    def remote(src, dst, send, recv, **target):
        return pltpu.make_async_remote_copy(
            src_ref=src, dst_ref=dst, send_sem=send, recv_sem=recv, device_id=target, device_id_type=MESH
        )

    def drain(ref, count, sem):
        if count:
            pltpu.make_async_copy(ref.at[pl.ds(0, count)], ref.at[pl.ds(0, count)], sem).wait()

    above_y, below_y = lax.rem(me_y + 1, across_y), lax.rem(me_y + across_y - 1, across_y)
    above_x, below_x = lax.rem(me_x + 1, across_x), lax.rem(me_x + across_x - 1, across_x)

    y0_up = remote(q.at[:, pl.ds(CY - 4, 4)], E.at[:, pl.ds(4, 4)], y0_send.at[0], y0_recv.at[0], gy=above_y)
    y0_down = remote(q.at[:, pl.ds(0, 4)], E.at[:, pl.ds(40, 4)], y0_send.at[1], y0_recv.at[1], gy=below_y)
    pl.when(jnp.logical_not(last_y))(y0_up.start)
    pl.when(jnp.logical_not(first_y))(y0_down.start)

    for load in loads:
        load.wait()

    T1[0, 8:40, :] = 2.0 * E[0, 8:40, :] + E[1, 8:40, :]
    T1[64, 8:40, :] = E[CX - 1, 8:40, :]

    def down_x(i, carry):
        T1[i, 8:40, :] = E[2 * i - 1, 8:40, :] + 2.0 * E[2 * i, 8:40, :] + E[2 * i + 1, 8:40, :]
        return carry

    lax.fori_loop(1, 64, down_x, 0, unroll=3)

    def down_y(i, carry):
        E1Z[i] = (
            T1[i, pl.ds(7, 24, stride=2), :] + 2.0 * T1[i, pl.ds(8, 24, stride=2), :] + T1[i, pl.ds(9, 24, stride=2), :]
        )
        return carry

    lax.fori_loop(0, 65, down_y, 0, unroll=5)

    few.wait()
    WZ[...] = stacked(coarse_z(taps))
    W0[...] = stacked(toeplitz(taps, 0, (CZ, CZ), iota((CZ, CZ), 0) - iota((CZ, CZ), 1)))
    A1[4:69] = product(E1Z[...].reshape(66 * 24, CZ), WZ[...]).reshape(66, 24, CZ)[0:65]

    for level in (2, 3, 4):
        finer, mid = A[level - 1], T[level]
        coarser, shift = (A[level], 4) if level < 4 else (A4, 0)
        inner, rows = ROWS[level - 1], ROWS[level]

        n = NXL[level]
        pairs = finer[4 : 2 * n + 4].reshape(n, 2, inner, CZ)
        even, odd = pairs[:, 0], pairs[:, 1]
        mid[0:n, 8 : 8 + inner, :] = 2.0 * even + odd + finer[3 : 2 * n + 3].reshape(n, 2, inner, CZ)[:, 0]
        mid[n, 8 : 8 + inner, :] = finer[2 * n + 3] + 2.0 * finer[2 * n + 4]
        coarser[shift : shift + n + 1] = (
            mid[:, pl.ds(7, rows, stride=2), :]
            + 2.0 * mid[:, pl.ds(8, rows, stride=2), :]
            + mid[:, pl.ds(9, rows, stride=2), :]
        )

    lane8 = iota((8, CZ), 1)
    message = jnp.zeros((8, CZ), F32)
    for x in range(9):
        value = jnp.where((lane8 >= 112) & (lane8 < 120), A4[x], 0.0)
        message = message + pltpu.roll(value, (8 * x - 112) % CZ, 1)
    GA[me_y] = message
    for y in mates:
        remote(GA.at[me_y], GA.at[me_y], ga_send, ga_recv, gy=y).start()

    @pl.when(last_x)
    def _():
        for level in (1, 2, 3):
            A[level][NXL[level] + 4] = jnp.zeros((ROWS[level], CZ), F32)

    for way in (0, 1):
        for i in range(5):
            at = {level: (NXL[level] if way == 0 else 4) + i for level in (1, 2, 3)}
            wide = A1[at[1]]
            lane = iota((24, CZ), 1)
            XS[way, i] = jnp.where(lane < 64, wide, 0.0)
            lane = iota((16, CZ), 1)
            XS[way, i, 0:16, :] = jnp.where(lane >= 64, A2[at[2]], XS[way, i, 0:16, :])
            lane = iota((8, CZ), 1)
            XS[way, i, 0:8, :] = jnp.where(lane >= 96, A3[at[3]], XS[way, i, 0:8, :])
    cx_up = remote(XS.at[0], XR.at[0], cx_send.at[0], cx_recv.at[0], gx=above_x)
    cx_down = remote(XS.at[1], XR.at[1], cx_send.at[1], cx_recv.at[1], gx=below_x)
    pl.when(jnp.logical_not(last_x))(cx_up.start)
    pl.when(jnp.logical_not(first_x))(cx_down.start)

    w0 = [taps[0, k] for k in range(2 * REACH + 1)]

    def mid_y(i, carry):
        C[4 + i, 8:24, :] = weighted([E[i, 12 + k : 28 + k, :] for k in range(9)], w0)
        return carry

    lax.fori_loop(0, CX, mid_y, 0, unroll=2)

    pl.when(jnp.logical_not(first_y))(y0_up.wait_recv)
    pl.when(jnp.logical_not(last_y))(y0_down.wait_recv)

    def outer_y(i, carry):
        C[4 + i, 0:8, :] = weighted([E[i, 4 + k : 12 + k, :] for k in range(9)], w0)
        C[4 + i, 24:32, :] = weighted([E[i, 28 + k : 36 + k, :] for k in range(9)], w0)
        return carry

    lax.fori_loop(0, 4, outer_y, 0, unroll=2)
    lax.fori_loop(CX - 4, CX, outer_y, 0, unroll=2)
    x0_up = remote(C.at[pl.ds(CX, 4)], C.at[pl.ds(0, 4)], x0_send.at[0], x0_recv.at[0], gx=above_x)
    x0_down = remote(C.at[pl.ds(4, 4)], C.at[pl.ds(CX + 4, 4)], x0_send.at[1], x0_recv.at[1], gx=below_x)
    pl.when(jnp.logical_not(last_x))(x0_up.start)
    pl.when(jnp.logical_not(first_x))(x0_down.start)

    lax.fori_loop(4, CX - 4, outer_y, 0, unroll=2)

    drain(GA, group - 1, ga_recv)
    for y in peers:
        remote(GA.at[pl.ds(base, group)], GA.at[pl.ds(base, group)], gc_send, gc_recv, gy=y).start()

    pl.when(jnp.logical_not(first_x))(cx_up.wait_recv)
    pl.when(jnp.logical_not(last_x))(cx_down.wait_recv)
    for level in (1, 2, 3):
        array, rows, n = A[level], ROWS[level], NXL[level]
        array[0:4] = XR[0, 0:4, 0:rows, :]
        array[4] = array[4] + XR[0, 4, 0:rows, :]
        array[n + 4] = array[n + 4] + XR[1, 0, 0:rows, :]
        array[n + 5 : n + 9] = XR[1, 1:5, 0:rows, :]
        wl = [taps[level, k] for k in range(2 * REACH + 1)]

        def along_x(i, carry, array=array, target=B[level], rows=rows, wl=wl):
            target[i, pl.ds(8, rows), :] = weighted([array[i + k] for k in range(9)], wl)
            return carry

        lax.fori_loop(0, n + 1, along_x, 0, unroll={1: 5, 2: 3, 3: 1}[level])

        @pl.when(last_x)
        def _(target=B[level], rows=rows, n=n):
            target[n, pl.ds(8, rows), :] = jnp.zeros((rows, CZ), F32)

        @pl.when(last_y)
        def _(target=B[level], level=level, n=n):
            target[:, pl.ds(8 + NYL[level], 1), :] = jnp.zeros((n + 1, 1, CZ), F32)

    lane = iota((8, CZ), 1)
    for way in (0, 1):
        start = {level: 8 + (NYL[level] - 4 if way == 0 else 0) for level in (1, 2, 3)}
        YS[way] = B1[:, start[1] : start[1] + 8, :]
        YS[way, 0:33] = jnp.where(lane >= 64, B2[:, start[2] : start[2] + 8, :], B1[0:33, start[1] : start[1] + 8, :])
        YS[way, 0:17] = jnp.where(lane >= 96, B3[:, start[3] : start[3] + 8, :], YS[way, 0:17])
    rows5 = pl.ds(0, 5)
    cy_up = remote(YS.at[0, :, rows5], YR.at[0, :, rows5], cy_send.at[0], cy_recv.at[0], gy=above_y)
    cy_down = remote(YS.at[1, :, rows5], YR.at[1, :, rows5], cy_send.at[1], cy_recv.at[1], gy=below_y)
    pl.when(jnp.logical_not(last_y))(cy_up.start)
    pl.when(jnp.logical_not(first_y))(cy_down.start)
    near, far = pl.ds(0, 17), pl.ds(5, 1)
    c2_up = remote(
        YS.at[0, near, pl.ds(4, 1)], YR.at[0, near, far], c2_send.at[0], c2_recv.at[0],
        gy=lax.rem(me_y + 2, across_y),
    )
    c2_down = remote(
        YS.at[1, near, pl.ds(0, 1)], YR.at[1, near, far], c2_send.at[1], c2_recv.at[1],
        gy=lax.rem(me_y + across_y - 2, across_y),
    )
    pl.when(me_y < across_y - 2)(c2_up.start)
    pl.when(me_y >= 2)(c2_down.start)

    pl.when(jnp.logical_not(first_x))(x0_up.wait_recv)
    pl.when(jnp.logical_not(last_x))(x0_down.wait_recv)

    def finest_x(i, carry):
        w0 = [taps[0, k] for k in range(2 * REACH + 1)]
        for t in range(4):
            rows = pl.ds(8 * t, 8)
            value = C[pl.ds(16 * i, 24), rows, :]
            out[pl.ds(16 * i, 16), rows, :] = weighted([value[k : k + 16] for k in range(9)], w0)
        return carry

    lax.fori_loop(0, CX // 16, finest_x, 0)

    out[...] = product(out[...].reshape(CX * CY, CZ), W0[...]).reshape(CX, CY, CZ)

    drain(GA, (groups - 1) * group, gc_recv)
    row, col = iota((8, 8 * across_y), 0), iota((8, 8 * across_y), 1)
    spot, place = 2 * me_y + row, 2 * (col // 8) + col % 8
    valid = (row < 3) & (spot < 2 * across_y) & (col % 8 < 3) & (place < 2 * across_y)
    along = jnp.where(valid, gauss(spot - place, 2 * across_y), 0.0)
    value = jnp.dot(along, GA[...].reshape(8 * across_y, CZ), precision=HIGHEST, preferred_element_type=F32)
    lane16, row16 = iota((16, CZ), 1), iota((16, CZ), 0)
    keep = (lane16 // 8 == row16) & (row16 < 9)
    spread = jnp.concatenate(
        [jnp.where(keep, jnp.broadcast_to(value[y : y + 1], (16, CZ)), 0.0) for y in range(3)], axis=1
    )
    r, c = iota((3 * CZ, CZ), 0), iota((3 * CZ, CZ), 1)
    pick = (c == 8 * (r // CZ) + r % 8).astype(F32)
    GB[me_x] = jnp.dot(spread, pick, precision=HIGHEST, preferred_element_type=F32)
    for x in columns:
        remote(GB.at[me_x], GB.at[me_x], gb_send, gb_recv, gx=x).start()

    pl.when(jnp.logical_not(first_y))(cy_up.wait_recv)
    pl.when(jnp.logical_not(last_y))(cy_down.wait_recv)
    pl.when(me_y >= 2)(c2_up.wait_recv)
    pl.when(me_y < across_y - 2)(c2_down.wait_recv)
    row8 = iota((8, CZ), 0)
    for level in (1, 2, 3):
        array, n, rows, count = B[level], NYL[level], ROWS[level], NXL[level] + 1
        wl = [taps[level, k] for k in range(2 * REACH + 1)]

        def along_y(x, carry, array=array, target=U[level], n=n, rows=rows, level=level, wl=wl):
            array[x, 4:12, :] = array[x, 4:12, :] + jnp.where(row8 < 5, YR[0, x], 0.0)
            array[x, 8 + n : 16 + n, :] = array[x, 8 + n : 16 + n, :] + jnp.where(row8 < 5, YR[1, x], 0.0)
            if level == 3:
                array[x, 4:5, :] = array[x, 4:5, :] + YR[0, x, 5:6, :]
                array[x, 16:17, :] = array[x, 16:17, :] + YR[1, x, 5:6, :]
            target[x] = weighted([array[x, 4 + k : 4 + k + rows, :] for k in range(9)], wl)
            return carry

        lax.fori_loop(0, count, along_y, 0, unroll={1: 5, 2: 3, 3: 1}[level])

        @pl.when(last_y)
        def _(target=U[level], n=n, count=count):
            target[0:count, n : n + 1, :] = jnp.zeros((count, 1, CZ), F32)

    lane = iota((8, CZ), 1)
    U3[...] = jnp.where((lane >= 96) & (lane < 112), U3[...], 0.0)
    for level, source, wide in ((2, U3, G2), (1, U2, G1)):
        half = {2: 8, 1: 16}[level]
        target, rows, n = U[level], ROWS[level], NXL[level]
        first, cells = LANES[level]

        low = source[:, 0:half, :]
        high = pltpu.roll(low, half - 1, 1)
        wide[:, pl.ds(0, half, stride=2), :] = low
        wide[:, pl.ds(1, half, stride=2), :] = 0.5 * (low + high)
        lane = iota((rows, CZ), 1)
        own = (lane >= first) & (lane < first + cells)
        low, high = wide[0 : n // 2, 0:rows, :], wide[1 : n // 2 + 1, 0:rows, :]
        both = jnp.stack([low, 0.5 * (low + high)], axis=1).reshape(n, rows, CZ)
        target[0:n] = jnp.where(own, target[0:n], both)
        target[n] = jnp.where(own, target[n], wide[n // 2, 0:rows, :])

    high, low = split(U1[...].reshape(66 * 24, CZ))
    both = jnp.concatenate([high, low], axis=1)
    E1Z[...] = jnp.dot(both, PZ[...], preferred_element_type=F32).reshape(66, 24, CZ)

    def rise_y(x, carry):
        low, high = E1Z[x, 0:16, :], E1Z[x, 1:17, :]
        G0[x, pl.ds(0, 16, stride=2), :] = low
        G0[x, pl.ds(1, 16, stride=2), :] = 0.5 * (low + high)
        return carry

    lax.fori_loop(0, 65, rise_y, 0, unroll=5)

    def finish(i, carry):
        low, high = G0[i], G0[i + 1]
        out[2 * i] = out[2 * i] + low
        out[2 * i + 1] = out[2 * i + 1] + 0.5 * (low + high)
        return carry

    lax.fori_loop(0, CX // 2, finish, 0, unroll=2)

    drain(GB, across_x - 1, gb_recv)
    row, col = iota((16, 16 * across_x), 0), iota((16, 16 * across_x), 1)
    spot, place = 8 * me_x + row, 8 * (col // 16) + col % 16
    valid = (row < 9) & (spot < 8 * across_x) & (col % 16 < 9) & (place < 8 * across_x)
    along = jnp.where(valid, gauss(spot - place, 8 * across_x), 0.0)
    value = jnp.dot(along, GB[...].reshape(16 * across_x, CZ), precision=HIGHEST, preferred_element_type=F32)
    y, lane = iota((CY, CZ), 0), iota((CY, CZ), 1)
    share = jnp.maximum(0, 16 - jnp.abs(y - 16 * (lane // 8))).astype(F32) / 16.0
    share = jnp.where(lane < 24, share, 0.0)
    spread = jnp.concatenate([share * value[x : x + 1] for x in range(9)], axis=0)
    high, low = split(spread)
    both = jnp.concatenate([high, low], axis=1)
    value = jnp.dot(both, P4[...], preferred_element_type=F32).reshape(9, CY, CZ)
    coarsest[...] = value[:8]
    slopes[...] = (value[1:] - value[:8]) * (1.0 / 16.0)

    pl.when(jnp.logical_not(last_y))(y0_up.wait_send)
    pl.when(jnp.logical_not(first_y))(y0_down.wait_send)
    pl.when(jnp.logical_not(last_x))(x0_up.wait_send)
    pl.when(jnp.logical_not(first_x))(x0_down.wait_send)
    pl.when(jnp.logical_not(last_x))(cx_up.wait_send)
    pl.when(jnp.logical_not(first_x))(cx_down.wait_send)
    pl.when(jnp.logical_not(last_y))(cy_up.wait_send)
    pl.when(jnp.logical_not(first_y))(cy_down.wait_send)
    pl.when(me_y < across_y - 2)(c2_up.wait_send)
    pl.when(me_y >= 2)(c2_down.wait_send)
    drain(GA, group - 1, ga_send)
    drain(GA, (groups - 1) * group, gc_send)
    drain(GB, across_x - 1, gb_send)


def solution(mesh):
    across_x, across_y = mesh.shape["gx"], mesh.shape["gy"]

    def vmem(*shape, dtype=F32):
        return pltpu.VMEM(shape, dtype)

    pair = pltpu.SemaphoreType.DMA((2,))
    single = pltpu.SemaphoreType.DMA
    scratch = [
        pltpu.SMEM((4, 9), F32),
        vmem(CX, 48, CZ),
        vmem(CX + 8, CY, CZ),
        vmem(65, 56, CZ), vmem(33, 40, CZ), vmem(17, 24, CZ), vmem(9, 24, CZ),
        vmem(73, 24, CZ), vmem(41, 16, CZ), vmem(25, 8, CZ), vmem(9, 8, CZ),
        vmem(65, 40, CZ), vmem(33, 32, CZ), vmem(17, 24, CZ),
        vmem(66, 24, CZ), vmem(33, 16, CZ), vmem(17, 8, CZ),
        vmem(17, 16, CZ), vmem(33, 32, CZ), vmem(65, 32, CZ),
        vmem(2, 5, 24, CZ), vmem(2, 5, 24, CZ),
        vmem(2, 65, 8, CZ), vmem(2, 65, 8, CZ),
        vmem(across_y, 8, CZ), vmem(across_x, 16, CZ),
        vmem(2 * CZ, 2 * CZ, dtype=BF16), vmem(2 * CZ, 2 * CZ, dtype=BF16), vmem(2 * CZ, CZ, dtype=BF16), vmem(2 * CZ, CZ, dtype=BF16),
        vmem(66, 24, CZ),
        single, pltpu.SemaphoreType.DMA((4,)),
        pair, pair, pair, pair, pair, pair, pair, pair, pair, pair,
        single, single, single, single, single, single,
    ]

    def local(charge, level_taps):
        fine, coarse, slope = pl.pallas_call(
            functools.partial(kernel, across_x, across_y),
            out_shape=[jax.ShapeDtypeStruct((CX, CY, CZ), F32), *[jax.ShapeDtypeStruct((8, CY, CZ), F32)] * 2],
            in_specs=[pl.BlockSpec(memory_space=pltpu.HBM), pl.BlockSpec(memory_space=pltpu.HBM)],
            out_specs=[pl.BlockSpec(memory_space=pltpu.VMEM)] * 3,
            scratch_shapes=scratch,
            compiler_params=pltpu.CompilerParams(
                collective_id=0, has_side_effects=True, vmem_limit_bytes=48 * 1024 * 1024
            ),
        )(*(pltpu.with_memory_space_constraint(array, pltpu.HBM) for array in (level_taps, charge)))
        step = lax.broadcasted_iota(F32, (8, 16, CY, CZ), 1)
        rise = coarse[:, None] + step * slope[:, None]
        return (fine.reshape(8, 16, CY, CZ) + rise).reshape(CX, CY, CZ)

    spec = P("gx", "gy", None)
    return jax.shard_map(local, mesh=mesh, in_specs=(spec, P()), out_specs=spec, check_vma=False)
```

```python
import functools
import math

import jax
import jax.numpy as jnp
from jax import lax
from jax.experimental import pallas as pl
from jax.experimental.pallas import tpu as pltpu
from jax.sharding import PartitionSpec as P

F32 = jnp.float32
BF16 = jnp.bfloat16
HIGHEST = lax.Precision.HIGHEST
MESH = pl.DeviceIdType.MESH

CX, CY, CZ = 128, 32, 128
REACH = 4
LANES = {1: (0, 64), 2: (64, 32), 3: (96, 16)}
NXL = {1: 64, 2: 32, 3: 16, 4: 8}
NYL = {1: 16, 2: 8, 3: 4, 4: 2}
ROWS = {1: 24, 2: 16, 3: 8, 4: 8}


def iota(shape, dim):
    return lax.broadcasted_iota(jnp.int32, shape, dim)


def gauss(distance, length):
    spread = max(length, 4) / 2.0
    scaled = distance.astype(F32) / spread
    return jnp.exp(-scaled * scaled) / (math.sqrt(math.pi) * spread)


def split(value):
    high = value.astype(BF16)
    return high, (value - high.astype(F32)).astype(BF16)


def stacked(matrix):
    high, low = split(matrix)
    upper = jnp.concatenate([high, low], axis=1)
    lower = jnp.concatenate([high, jnp.zeros_like(high)], axis=1)
    return jnp.concatenate([upper, lower], axis=0)


def product(value, weights):
    high, low = split(value)
    both = jnp.dot(jnp.concatenate([high, low], axis=1), weights, preferred_element_type=F32)
    return both[:, :CZ] + both[:, CZ:]


def toeplitz(taps, level, shape, offset):
    matrix = jnp.zeros(shape, F32)
    for k in range(2 * REACH + 1):
        matrix = jnp.where(offset == k - REACH, taps[level, k], matrix)
    return matrix


def coarse_z(taps):
    a, c = iota((CZ, CZ), 0), iota((CZ, CZ), 1)
    down = jnp.zeros((CZ, CZ), F32)
    mix = jnp.zeros((CZ, CZ), F32)
    for level, (first, cells) in LANES.items():
        step = 2**level
        here = (c >= first) & (c < first + cells)
        weight = jnp.maximum(0, step - jnp.abs(a - step * (c - first)))
        down = jnp.where(here, weight.astype(F32) * 2.0 ** (-5 * level), down)
        inside = here & (a >= first) & (a < first + cells)
        block = toeplitz(taps, level, (CZ, CZ), a - c)
        mix = jnp.where(inside, block, mix)
    return jnp.dot(down, mix, precision=HIGHEST, preferred_element_type=F32)


def prolong_z():
    r, a = iota((CZ, CZ), 0), iota((CZ, CZ), 1)
    up = jnp.zeros((CZ, CZ), F32)
    for level, (first, cells) in LANES.items():
        step = 2**level
        here = (r >= first) & (r < first + cells)
        weight = jnp.maximum(0, step - jnp.abs(a - step * (r - first)))
        up = jnp.where(here, weight.astype(F32) * 2.0**-level, up)
    return up.astype(BF16)


def weighted(pieces, weights):
    total = weights[REACH] * pieces[REACH]
    for k in range(REACH):
        total = total + weights[k] * (pieces[k] + pieces[2 * REACH - k])
    return total


def kernel(
    across_x, across_y, taps_in, q, out, coarsest, slopes,
    taps,
    E, C, T1, T2, T3, T4, R1, R2, R3, A1, A2, A3, B1, B2, B3, U1, U2, U3, G2, G1, G0,
    XS, XR, YS, YR, GA, GB, WZ, W0, PZ, P4, Z4, E1Z,
    taps_sem, in_sem, y0_send, y0_recv, x0_send, x0_recv, cx_send, cx_recv, cy_send, cy_recv,
    c2_send, c2_recv, ga_send, ga_recv, gb_send, gb_recv,
):
    me_x, me_y = lax.axis_index("gx"), lax.axis_index("gy")
    first_x, last_x = me_x == 0, me_x == across_x - 1
    first_y, last_y = me_y == 0, me_y == across_y - 1
    R, A, B, U, T = {1: R1, 2: R2, 3: R3}, {1: A1, 2: A2, 3: A3}, {1: B1, 2: B2, 3: B3}, {1: U1, 2: U2, 3: U3}, {2: T2, 3: T3, 4: T4}

    few = pltpu.make_async_copy(taps_in, taps, taps_sem)
    few.start()
    parts = 4
    depth = CX // parts
    loads = [
        pltpu.make_async_copy(
            q.at[pl.ds(i * depth, depth)], E.at[pl.ds(i * depth, depth), pl.ds(8, CY)], in_sem.at[i]
        )
        for i in range(parts)
    ]
    for load in loads:
        load.start()

    cores = 2 if across_y > 1 else 1
    chips = across_y // cores
    core = lax.rem(me_y, cores)
    near_by = [
        (lax.rem(me_x + x, across_x), me_y - core + lax.rem(core + c, cores))
        for x in range(across_x) for c in range(cores) if x or c
    ]
    far_off = [(me_x, lax.rem(me_y + cores * step, across_y)) for step in range(1, chips)]
    steps = (1, 2, across_y - 2, across_y - 1) if across_y > 4 else ()
    around = [(me_x, lax.rem(me_y + step, across_y)) for step in steps]
    barrier = pltpu.get_barrier_semaphore()
    for x, y in around + near_by + far_off:
        pl.semaphore_signal(barrier, inc=1, device_id=(x, y), device_id_type=MESH)


    def blank(ref, count, *spans):
        for start, size in spans:
            ref[:, start : start + size, :] = jnp.zeros((count, size, CZ), F32)

    blank(T1, 65, (0, 8), (40, 16))
    blank(T2, 33, (0, 8), (32, 8))
    blank(T3, 17, (0, 8))
    blank(T4, 9, (0, 8), (16, 8))
    for level in (1, 2, 3):
        blank(B[level], NXL[level] + 1, (0, 8), *(((16, 8),) if level == 3 else ()))
        rows = ROWS[level]
        R[level][0] = jnp.zeros((rows, CZ), F32)
    GA[:, 2:8, :] = jnp.zeros((across_x * cores, 6, CZ), F32)
    GB[:, 6:8, :] = jnp.zeros((chips, 2, CZ), F32)

    @pl.when(first_y)
    def _():
        E[:, 4:8, :] = jnp.zeros((CX, 4, CZ), F32)
        YR[0, :, 0:5, :] = jnp.zeros((65, 5, CZ), F32)

    @pl.when(last_y)
    def _():
        E[:, 40:44, :] = jnp.zeros((CX, 4, CZ), F32)
        YR[1, :, 0:5, :] = jnp.zeros((65, 5, CZ), F32)

    @pl.when(me_y < 2)
    def _():
        YR[0, 0:17, 5:6, :] = jnp.zeros((17, 1, CZ), F32)

    @pl.when(me_y >= across_y - 2)
    def _():
        YR[1, 0:17, 5:6, :] = jnp.zeros((17, 1, CZ), F32)

    @pl.when(first_x)
    def _():
        C[0:4] = jnp.zeros((4, CY, CZ), F32)
        XR[0] = jnp.zeros((5, 24, CZ), F32)

    @pl.when(last_x)
    def _():
        C[CX + 4 : CX + 8] = jnp.zeros((4, CY, CZ), F32)
        XR[1] = jnp.zeros((5, 24, CZ), F32)

    a, c = iota((CZ, CZ), 0), iota((CZ, CZ), 1)
    weight = jnp.maximum(0, 16 - jnp.abs(a - 16 * c)).astype(F32) * 2.0**-20
    weight = jnp.where(c < 8, weight, 0.0)
    block = jnp.where(a < 8, gauss(a - c % 8, 8), 0.0)
    Z4[...] = jnp.dot(weight, block, precision=HIGHEST, preferred_element_type=F32)
    rise = prolong_z()
    PZ[...] = jnp.concatenate([rise, rise], axis=0)
    r, a = iota((CZ, CZ), 0), iota((CZ, CZ), 1)
    rise = jnp.maximum(0, 16 - jnp.abs(a - 16 * (r % 8))).astype(F32) / 16.0
    rise = jnp.where(r < 72, rise, 0.0).astype(BF16)
    P4[...] = jnp.concatenate([rise, rise], axis=0)


    def remote(src, dst, send, recv, **target):
        return pltpu.make_async_remote_copy(
            src_ref=src, dst_ref=dst, send_sem=send, recv_sem=recv, device_id=target, device_id_type=MESH
        )

    def drain(ref, count, rows, sem):
        if count:
            part = ref.at[pl.ds(0, count), pl.ds(0, rows)]
            pltpu.make_async_copy(part, part, sem).wait()

    above_y, below_y = lax.rem(me_y + 1, across_y), lax.rem(me_y + across_y - 1, across_y)
    above_x, below_x = lax.rem(me_x + 1, across_x), lax.rem(me_x + across_x - 1, across_x)

    y0_up = remote(q.at[:, pl.ds(CY - 4, 4)], E.at[:, pl.ds(4, 4)], y0_send.at[0], y0_recv.at[0], gy=above_y)
    y0_down = remote(q.at[:, pl.ds(0, 4)], E.at[:, pl.ds(40, 4)], y0_send.at[1], y0_recv.at[1], gy=below_y)
    for load in loads:
        load.wait()

    T1[0, 8:40, :] = 2.0 * E[0, 8:40, :] + E[1, 8:40, :]
    T1[64, 8:40, :] = E[CX - 1, 8:40, :]

    def down_x(i, carry):
        T1[i, 8:40, :] = E[2 * i - 1, 8:40, :] + 2.0 * E[2 * i, 8:40, :] + E[2 * i + 1, 8:40, :]
        return carry

    lax.fori_loop(1, 64, down_x, 0, unroll=3)

    def down_y(i, carry):
        R1[i + 1] = (
            T1[i, pl.ds(7, 24, stride=2), :] + 2.0 * T1[i, pl.ds(8, 24, stride=2), :] + T1[i, pl.ds(9, 24, stride=2), :]
        )
        return carry

    lax.fori_loop(0, 65, down_y, 0, unroll=5)

    pl.semaphore_wait(barrier, len(around + near_by + far_off))
    pl.when(jnp.logical_not(last_y))(y0_up.start)
    pl.when(jnp.logical_not(first_y))(y0_down.start)
    for level in (2, 3, 4):
        finer, mid, n = R[level - 1], T[level], NXL[level]
        inner, rows = ROWS[level - 1], ROWS[level]
        pairs = finer[1 : 2 * n + 1].reshape(n, 2, inner, CZ)
        before = finer[0 : 2 * n].reshape(n, 2, inner, CZ)
        mid[0:n, 8 : 8 + inner, :] = before[:, 0] + 2.0 * pairs[:, 0] + pairs[:, 1]
        mid[n, 8 : 8 + inner, :] = finer[2 * n] + 2.0 * finer[2 * n + 1]
        value = (
            mid[:, pl.ds(7, rows, stride=2), :]
            + 2.0 * mid[:, pl.ds(8, rows, stride=2), :]
            + mid[:, pl.ds(9, rows, stride=2), :]
        )
        if level < 4:
            R[level][1 : n + 2] = value

    value = jnp.dot(value.reshape(72, CZ), Z4[...], precision=HIGHEST, preferred_element_type=F32)
    row, lane = iota((72, CZ), 0), iota((72, CZ), 1)
    value = jnp.where((lane // 8 == 3 * (row // 16) + row % 8) & (row % 8 < 3), value, 0.0)
    pick = ((iota((8, 72), 1) // 8) % 2 == iota((8, 72), 0)).astype(F32)
    mine = me_x * cores + core
    GA[mine, 0:2, :] = jnp.dot(pick, value, precision=HIGHEST, preferred_element_type=F32)[0:2]
    two = pl.ds(0, 2)
    for x, y in near_by:
        remote(GA.at[mine, two], GA.at[mine, two], ga_send, ga_recv, gx=x, gy=y).start()


    few.wait()
    WZ[...] = stacked(coarse_z(taps))
    W0[...] = stacked(toeplitz(taps, 0, (CZ, CZ), iota((CZ, CZ), 0) - iota((CZ, CZ), 1)))
    A1[4:69] = product(R1[1:67].reshape(66 * 24, CZ), WZ[...]).reshape(66, 24, CZ)[0:65]
    A2[4:37] = product(R2[1:34].reshape(33 * 16, CZ), WZ[...]).reshape(33, 16, CZ)
    A3[4:21] = product(R3[1:19].reshape(18 * 8, CZ), WZ[...]).reshape(18, 8, CZ)[0:17]

    @pl.when(last_x)
    def _():
        for level in (1, 2, 3):
            A[level][NXL[level] + 4] = jnp.zeros((ROWS[level], CZ), F32)

    for way in (0, 1):
        for i in range(5):
            at = {level: (NXL[level] if way == 0 else 4) + i for level in (1, 2, 3)}
            wide = A1[at[1]]
            lane = iota((24, CZ), 1)
            XS[way, i] = jnp.where(lane < 64, wide, 0.0)
            lane = iota((16, CZ), 1)
            XS[way, i, 0:16, :] = jnp.where(lane >= 64, A2[at[2]], XS[way, i, 0:16, :])
            lane = iota((8, CZ), 1)
            XS[way, i, 0:8, :] = jnp.where(lane >= 96, A3[at[3]], XS[way, i, 0:8, :])
    cx_up = remote(XS.at[0], XR.at[0], cx_send.at[0], cx_recv.at[0], gx=above_x)
    cx_down = remote(XS.at[1], XR.at[1], cx_send.at[1], cx_recv.at[1], gx=below_x)
    pl.when(jnp.logical_not(last_x))(cx_up.start)
    pl.when(jnp.logical_not(first_x))(cx_down.start)

    w0 = [taps[0, k] for k in range(2 * REACH + 1)]

    def mid_y(i, carry):
        C[4 + i, 8:24, :] = weighted([E[i, 12 + k : 28 + k, :] for k in range(9)], w0)
        return carry

    lax.fori_loop(0, CX, mid_y, 0, unroll=2)

    pl.when(jnp.logical_not(first_x))(cx_up.wait_recv)
    pl.when(jnp.logical_not(last_x))(cx_down.wait_recv)
    for level in (1, 2, 3):
        array, rows, n = A[level], ROWS[level], NXL[level]
        array[0:4] = XR[0, 0:4, 0:rows, :]
        array[4] = array[4] + XR[0, 4, 0:rows, :]
        array[n + 4] = array[n + 4] + XR[1, 0, 0:rows, :]
        array[n + 5 : n + 9] = XR[1, 1:5, 0:rows, :]
        wl = [taps[level, k] for k in range(2 * REACH + 1)]

        def along_x(i, carry, array=array, target=B[level], rows=rows, wl=wl):
            target[i, pl.ds(8, rows), :] = weighted([array[i + k] for k in range(9)], wl)
            return carry

        lax.fori_loop(0, n + 1, along_x, 0, unroll={1: 5, 2: 3, 3: 1}[level])

        @pl.when(last_x)
        def _(target=B[level], rows=rows, n=n):
            target[n, pl.ds(8, rows), :] = jnp.zeros((rows, CZ), F32)

        @pl.when(last_y)
        def _(target=B[level], level=level, n=n):
            target[:, pl.ds(8 + NYL[level], 1), :] = jnp.zeros((n + 1, 1, CZ), F32)

    lane = iota((8, CZ), 1)
    for way in (0, 1):
        start = {level: 8 + (NYL[level] - 4 if way == 0 else 0) for level in (1, 2, 3)}
        YS[way] = B1[:, start[1] : start[1] + 8, :]
        YS[way, 0:33] = jnp.where(lane >= 64, B2[:, start[2] : start[2] + 8, :], B1[0:33, start[1] : start[1] + 8, :])
        YS[way, 0:17] = jnp.where(lane >= 96, B3[:, start[3] : start[3] + 8, :], YS[way, 0:17])
    rows5 = pl.ds(0, 5)
    cy_up = remote(YS.at[0, :, rows5], YR.at[0, :, rows5], cy_send.at[0], cy_recv.at[0], gy=above_y)
    cy_down = remote(YS.at[1, :, rows5], YR.at[1, :, rows5], cy_send.at[1], cy_recv.at[1], gy=below_y)
    pl.when(jnp.logical_not(last_y))(cy_up.start)
    pl.when(jnp.logical_not(first_y))(cy_down.start)
    near, far = pl.ds(0, 17), pl.ds(5, 1)
    c2_up = remote(
        YS.at[0, near, pl.ds(4, 1)], YR.at[0, near, far], c2_send.at[0], c2_recv.at[0],
        gy=lax.rem(me_y + 2, across_y),
    )
    c2_down = remote(
        YS.at[1, near, pl.ds(0, 1)], YR.at[1, near, far], c2_send.at[1], c2_recv.at[1],
        gy=lax.rem(me_y + across_y - 2, across_y),
    )
    pl.when(me_y < across_y - 2)(c2_up.start)
    pl.when(me_y >= 2)(c2_down.start)

    pl.when(jnp.logical_not(first_y))(y0_up.wait_recv)
    pl.when(jnp.logical_not(last_y))(y0_down.wait_recv)

    def outer_y(i, carry):
        C[4 + i, 0:8, :] = weighted([E[i, 4 + k : 12 + k, :] for k in range(9)], w0)
        C[4 + i, 24:32, :] = weighted([E[i, 28 + k : 36 + k, :] for k in range(9)], w0)
        return carry

    lax.fori_loop(0, 4, outer_y, 0, unroll=2)
    lax.fori_loop(CX - 4, CX, outer_y, 0, unroll=2)
    x0_up = remote(C.at[pl.ds(CX, 4)], C.at[pl.ds(0, 4)], x0_send.at[0], x0_recv.at[0], gx=above_x)
    x0_down = remote(C.at[pl.ds(4, 4)], C.at[pl.ds(CX + 4, 4)], x0_send.at[1], x0_recv.at[1], gx=below_x)
    pl.when(jnp.logical_not(last_x))(x0_up.start)
    pl.when(jnp.logical_not(first_x))(x0_down.start)

    lax.fori_loop(4, CX - 4, outer_y, 0, unroll=2)

    row, col = iota((cores * 80, 8 * across_x * cores), 0), iota((cores * 80, 8 * across_x * cores), 1)
    cell, slot = 2 * ((row // 16) % 5) + col % 8, col // 8
    spot, place = 8 * me_x + row % 16, 8 * (slot // cores) + cell
    valid = (slot % cores == row // 80) & (col % 8 < 2) & (cell < 9) & (place < 8 * across_x)
    valid = valid & (row % 16 < 9) & (spot < 8 * across_x)
    along = jnp.where(valid, gauss(spot - place, 8 * across_x), 0.0)
    r, c = iota((CZ, 3 * CZ), 0), iota((CZ, 3 * CZ), 1)
    pick = (r == 8 * (c // CZ) + c % 8).astype(F32)
    row, col = iota((8, 48 * cores), 0), iota((8, 48 * cores), 1)
    gather = ((row // 3 == (col // 16) % cores) & (row % 3 == col // (16 * cores))).astype(F32)
    drain(GA, across_x * cores - 1, 2, ga_recv)
    value = jnp.dot(along, GA[...].reshape(8 * across_x * cores, CZ), precision=HIGHEST, preferred_element_type=F32)
    value = value.reshape(cores, 5, 16, CZ)
    lane = iota((cores, 16, CZ), 2)
    total = jnp.where(lane < 24, value[:, 0], 0.0)
    for g in range(1, 5):
        total = total + jnp.where(lane < 24, pltpu.roll(value[:, g], CZ - 24 * g, 2), 0.0)
    value = jnp.dot(total.reshape(cores * 16, CZ), pick, precision=HIGHEST, preferred_element_type=F32)
    row, lane = iota((cores * 16, CZ), 0), iota((cores * 16, CZ), 1)
    keep = (lane // 8 == row % 16) & (lane < 72)
    value = jnp.concatenate([jnp.where(keep, value[:, y * CZ : y * CZ + CZ], 0.0) for y in range(3)], axis=0)
    here = me_y // cores
    GB[here] = jnp.dot(gather, value, precision=HIGHEST, preferred_element_type=F32)
    six = pl.ds(0, 6)
    for x, y in far_off:
        remote(GB.at[here, six], GB.at[here, six], gb_send, gb_recv, gy=y).start()

    pl.when(jnp.logical_not(first_x))(x0_up.wait_recv)
    pl.when(jnp.logical_not(last_x))(x0_down.wait_recv)

    def finest_x(i, carry):
        w0 = [taps[0, k] for k in range(2 * REACH + 1)]
        for t in range(4):
            rows = pl.ds(8 * t, 8)
            value = C[pl.ds(16 * i, 24), rows, :]
            out[pl.ds(16 * i, 16), rows, :] = weighted([value[k : k + 16] for k in range(9)], w0)
        return carry

    lax.fori_loop(0, CX // 16, finest_x, 0)

    out[...] = product(out[...].reshape(CX * CY, CZ), W0[...]).reshape(CX, CY, CZ)

    pl.when(jnp.logical_not(first_y))(cy_up.wait_recv)
    pl.when(jnp.logical_not(last_y))(cy_down.wait_recv)
    pl.when(me_y >= 2)(c2_up.wait_recv)
    pl.when(me_y < across_y - 2)(c2_down.wait_recv)
    row8 = iota((8, CZ), 0)
    for level in (1, 2, 3):
        array, n, rows, count = B[level], NYL[level], ROWS[level], NXL[level] + 1
        wl = [taps[level, k] for k in range(2 * REACH + 1)]

        def along_y(x, carry, array=array, target=U[level], n=n, rows=rows, level=level, wl=wl):
            array[x, 4:12, :] = array[x, 4:12, :] + jnp.where(row8 < 5, YR[0, x], 0.0)
            array[x, 8 + n : 16 + n, :] = array[x, 8 + n : 16 + n, :] + jnp.where(row8 < 5, YR[1, x], 0.0)
            if level == 3:
                array[x, 4:5, :] = array[x, 4:5, :] + YR[0, x, 5:6, :]
                array[x, 16:17, :] = array[x, 16:17, :] + YR[1, x, 5:6, :]
            target[x] = weighted([array[x, 4 + k : 4 + k + rows, :] for k in range(9)], wl)
            return carry

        lax.fori_loop(0, count, along_y, 0, unroll={1: 5, 2: 3, 3: 1}[level])

        @pl.when(last_y)
        def _(target=U[level], n=n, count=count):
            target[0:count, n : n + 1, :] = jnp.zeros((count, 1, CZ), F32)

    lane = iota((8, CZ), 1)
    U3[...] = jnp.where((lane >= 96) & (lane < 112), U3[...], 0.0)
    for level, source, wide in ((2, U3, G2), (1, U2, G1)):
        half = {2: 8, 1: 16}[level]
        target, rows, n = U[level], ROWS[level], NXL[level]
        first, cells = LANES[level]

        low = source[:, 0:half, :]
        high = pltpu.roll(low, half - 1, 1)
        wide[:, pl.ds(0, half, stride=2), :] = low
        wide[:, pl.ds(1, half, stride=2), :] = 0.5 * (low + high)
        lane = iota((rows, CZ), 1)
        own = (lane >= first) & (lane < first + cells)
        low, high = wide[0 : n // 2, 0:rows, :], wide[1 : n // 2 + 1, 0:rows, :]
        both = jnp.stack([low, 0.5 * (low + high)], axis=1).reshape(n, rows, CZ)
        target[0:n] = jnp.where(own, target[0:n], both)
        target[n] = jnp.where(own, target[n], wide[n // 2, 0:rows, :])

    high, low = split(U1[...].reshape(66 * 24, CZ))
    both = jnp.concatenate([high, low], axis=1)
    E1Z[...] = jnp.dot(both, PZ[...], preferred_element_type=F32).reshape(66, 24, CZ)

    def rise_y(x, carry):
        low, high = E1Z[x, 0:16, :], E1Z[x, 1:17, :]
        G0[x, pl.ds(0, 16, stride=2), :] = low
        G0[x, pl.ds(1, 16, stride=2), :] = 0.5 * (low + high)
        return carry

    lax.fori_loop(0, 65, rise_y, 0, unroll=5)

    def finish(i, carry):
        low, high = G0[i], G0[i + 1]
        out[2 * i] = out[2 * i] + low
        out[2 * i + 1] = out[2 * i + 1] + 0.5 * (low + high)
        return carry

    lax.fori_loop(0, CX // 2, finish, 0, unroll=2)

    row, col = iota((CY, 8 * chips), 0), iota((CY, 8 * chips), 1)
    place = 2 * (cores * (col // 8) + (col % 8) // 3) + (col % 8) % 3
    valid = (col % 8 < 3 * cores) & (place < 2 * across_y)
    along = jnp.zeros((CY, 8 * chips), F32)
    for y in range(3):
        spot = 2 * me_y + y
        share = jnp.maximum(0, 16 - jnp.abs(row - 16 * y)).astype(F32) / 16.0
        term = jnp.where(valid & (spot < 2 * across_y), gauss(spot - place, 2 * across_y), 0.0)
        along = along + share * term
    drain(GB, chips - 1, 6, gb_recv)
    value = jnp.dot(along, GB[...].reshape(8 * chips, CZ), precision=HIGHEST, preferred_element_type=F32)
    lane = iota((CY, CZ), 1)
    spread = jnp.concatenate([jnp.where(lane // 8 == x, value, 0.0) for x in range(9)], axis=0)
    high, low = split(spread)
    both = jnp.concatenate([high, low], axis=1)
    value = jnp.dot(both, P4[...], preferred_element_type=F32).reshape(9, CY, CZ)
    coarsest[...] = value[:8]
    slopes[...] = (value[1:] - value[:8]) * (1.0 / 16.0)

    pl.when(jnp.logical_not(last_y))(y0_up.wait_send)
    pl.when(jnp.logical_not(first_y))(y0_down.wait_send)
    pl.when(jnp.logical_not(last_x))(x0_up.wait_send)
    pl.when(jnp.logical_not(first_x))(x0_down.wait_send)
    pl.when(jnp.logical_not(last_x))(cx_up.wait_send)
    pl.when(jnp.logical_not(first_x))(cx_down.wait_send)
    pl.when(jnp.logical_not(last_y))(cy_up.wait_send)
    pl.when(jnp.logical_not(first_y))(cy_down.wait_send)
    pl.when(me_y < across_y - 2)(c2_up.wait_send)
    pl.when(me_y >= 2)(c2_down.wait_send)
    drain(GA, across_x * cores - 1, 2, ga_send)
    drain(GB, chips - 1, 6, gb_send)


def last(fine, coarse, slope, out, done, sem):
    chunks = 8
    depth = CX // chunks
    copies = []
    for i in range(chunks):
        for x in range(i * depth, i * depth + depth):
            done[x] = fine[x] + (coarse[x // 16] + float(x % 16) * slope[x // 16])
        at = pl.ds(i * depth, depth)
        copies.append(pltpu.make_async_copy(done.at[at], out.at[at], sem.at[i]))
        copies[-1].start()
    for copy in copies:
        copy.wait()


def solution(mesh):
    across_x, across_y = mesh.shape["gx"], mesh.shape["gy"]

    cores = 2 if across_y > 1 else 1

    def vmem(*shape, dtype=F32):
        return pltpu.VMEM(shape, dtype)

    pair = pltpu.SemaphoreType.DMA((2,))
    single = pltpu.SemaphoreType.DMA
    scratch = [
        pltpu.SMEM((4, 9), F32),
        vmem(CX, 48, CZ),
        vmem(CX + 8, CY, CZ),
        vmem(65, 56, CZ), vmem(33, 40, CZ), vmem(17, 24, CZ), vmem(9, 24, CZ),
        vmem(67, 24, CZ), vmem(35, 16, CZ), vmem(19, 8, CZ),
        vmem(73, 24, CZ), vmem(41, 16, CZ), vmem(25, 8, CZ),
        vmem(65, 40, CZ), vmem(33, 32, CZ), vmem(17, 24, CZ),
        vmem(66, 24, CZ), vmem(33, 16, CZ), vmem(17, 8, CZ),
        vmem(17, 16, CZ), vmem(33, 32, CZ), vmem(65, 32, CZ),
        vmem(2, 5, 24, CZ), vmem(2, 5, 24, CZ),
        vmem(2, 65, 8, CZ), vmem(2, 65, 8, CZ),
        vmem(across_x * cores, 8, CZ), vmem(across_y // cores, 8, CZ),
        vmem(2 * CZ, 2 * CZ, dtype=BF16), vmem(2 * CZ, 2 * CZ, dtype=BF16), vmem(2 * CZ, CZ, dtype=BF16), vmem(2 * CZ, CZ, dtype=BF16),
        vmem(CZ, CZ), vmem(66, 24, CZ),
        single, pltpu.SemaphoreType.DMA((4,)),
        pair, pair, pair, pair, pair, pair, pair, pair, pair, pair,
        single, single, single, single,
    ]

    def local(charge, level_taps):
        fine, coarse, slope = pl.pallas_call(
            functools.partial(kernel, across_x, across_y),
            out_shape=[jax.ShapeDtypeStruct((CX, CY, CZ), F32), *[jax.ShapeDtypeStruct((8, CY, CZ), F32)] * 2],
            in_specs=[pl.BlockSpec(memory_space=pltpu.HBM), pl.BlockSpec(memory_space=pltpu.HBM)],
            out_specs=[pl.BlockSpec(memory_space=pltpu.VMEM)] * 3,
            scratch_shapes=scratch,
            compiler_params=pltpu.CompilerParams(
                collective_id=0, has_side_effects=True, vmem_limit_bytes=48 * 1024 * 1024
            ),
        )(*(pltpu.with_memory_space_constraint(array, pltpu.HBM) for array in (level_taps, charge)))
        return pl.pallas_call(
            last,
            out_shape=jax.ShapeDtypeStruct((CX, CY, CZ), F32),
            in_specs=[pl.BlockSpec(memory_space=pltpu.VMEM)] * 3,
            out_specs=pl.BlockSpec(memory_space=pltpu.HBM),
            scratch_shapes=[vmem(CX, CY, CZ), pltpu.SemaphoreType.DMA((8,))],
            compiler_params=pltpu.CompilerParams(vmem_limit_bytes=8 * 1024 * 1024),
        )(fine, coarse, slope)

    spec = P("gx", "gy", None)
    return jax.shard_map(local, mesh=mesh, in_specs=(spec, P()), out_specs=spec, check_vma=False)
```

```python
import functools
import math

import jax
import jax.numpy as jnp
from jax import lax
from jax.experimental import pallas as pl
from jax.experimental.pallas import tpu as pltpu
from jax.sharding import PartitionSpec as P

F32 = jnp.float32
BF16 = jnp.bfloat16
HIGHEST = lax.Precision.HIGHEST
MESH = pl.DeviceIdType.MESH

CX, CY, CZ = 128, 32, 128
REACH = 4
LANES = {1: (0, 64), 2: (64, 32), 3: (96, 16)}
NXL = {1: 64, 2: 32, 3: 16, 4: 8}
NYL = {1: 16, 2: 8, 3: 4, 4: 2}
ROWS = {1: 24, 2: 16, 3: 8, 4: 8}


def iota(shape, dim):
    return lax.broadcasted_iota(jnp.int32, shape, dim)


def gauss(distance, length):
    spread = max(length, 4) / 2.0
    scaled = distance.astype(F32) / spread
    return jnp.exp(-scaled * scaled) / (math.sqrt(math.pi) * spread)


def split(value):
    high = value.astype(BF16)
    return high, (value - high.astype(F32)).astype(BF16)


def stacked(matrix):
    high, low = split(matrix)
    upper = jnp.concatenate([high, low], axis=1)
    lower = jnp.concatenate([high, jnp.zeros_like(high)], axis=1)
    return jnp.concatenate([upper, lower], axis=0)


def product(value, weights):
    high, low = split(value)
    both = jnp.dot(jnp.concatenate([high, low], axis=1), weights, preferred_element_type=F32)
    return both[:, :CZ] + both[:, CZ:]


def picked(matrix, value):
    both = jnp.concatenate(split(value), axis=0)
    return jnp.dot(jnp.concatenate([matrix.astype(BF16)] * 2, axis=1), both, preferred_element_type=F32)


def general(matrix, value):
    (m_high, m_low), (v_high, v_low) = split(matrix), split(value)
    left = jnp.concatenate([m_high, m_low, m_high], axis=1)
    right = jnp.concatenate([v_high, v_high, v_low], axis=0)
    return jnp.dot(left, right, preferred_element_type=F32)


def toeplitz(taps, level, shape, offset):
    matrix = jnp.zeros(shape, F32)
    for k in range(2 * REACH + 1):
        matrix = jnp.where(offset == k - REACH, taps[level, k], matrix)
    return matrix


def coarse_z(taps):
    a, c = iota((CZ, CZ), 0), iota((CZ, CZ), 1)
    down = jnp.zeros((CZ, CZ), F32)
    mix = jnp.zeros((CZ, CZ), F32)
    for level, (first, cells) in LANES.items():
        step = 2**level
        here = (c >= first) & (c < first + cells)
        weight = jnp.maximum(0, step - jnp.abs(a - step * (c - first)))
        down = jnp.where(here, weight.astype(F32) * 2.0 ** (-5 * level), down)
        inside = here & (a >= first) & (a < first + cells)
        block = toeplitz(taps, level, (CZ, CZ), a - c)
        mix = jnp.where(inside, block, mix)
    return jnp.dot(down, mix, precision=HIGHEST, preferred_element_type=F32)


def prolong_z():
    r, a = iota((CZ, CZ), 0), iota((CZ, CZ), 1)
    up = jnp.zeros((CZ, CZ), F32)
    for level, (first, cells) in LANES.items():
        step = 2**level
        here = (r >= first) & (r < first + cells)
        weight = jnp.maximum(0, step - jnp.abs(a - step * (r - first)))
        up = jnp.where(here, weight.astype(F32) * 2.0**-level, up)
    return up.astype(BF16)


def weighted(pieces, weights):
    total = weights[REACH] * pieces[REACH]
    for k in range(REACH):
        total = total + weights[k] * (pieces[k] + pieces[2 * REACH - k])
    return total


def kernel(
    across_x, across_y, taps_in, q, out, coarsest, slopes,
    taps,
    E, C, T1, T2, T3, X4, R1, R2, R3, A1, A2, A3, B1, B2, B3, U1, U2, U3, G2, G1, G0,
    XS, XR, YS, YR, GA, GB, WZ, W0, PZ, P4, Z4, K4, GX, PX, GY, E1Z,
    taps_sem, in_sem, y0_send, y0_recv, x0_send, x0_recv, cx_send, cx_recv, cy_send, cy_recv,
    c2_send, c2_recv, ga_send, ga_recv, gb_send, gb_recv,
):
    me_x, me_y = lax.axis_index("gx"), lax.axis_index("gy")
    first_x, last_x = me_x == 0, me_x == across_x - 1
    first_y, last_y = me_y == 0, me_y == across_y - 1
    R, A, B, U, T = {1: R1, 2: R2, 3: R3}, {1: A1, 2: A2, 3: A3}, {1: B1, 2: B2, 3: B3}, {1: U1, 2: U2, 3: U3}, {2: T2, 3: T3}

    few = pltpu.make_async_copy(taps_in, taps, taps_sem)
    few.start()
    def load(i):
        at = pl.ds(i * 16, 16)
        return pltpu.make_async_copy(q.at[at], E.at[at, pl.ds(8, CY)], in_sem.at[i])

    for i in range(CX // 16):
        load(i).start()

    cores = 2 if across_y > 1 else 1
    chips = across_y // cores
    core = lax.rem(me_y, cores)
    near_by = [
        (lax.rem(me_x + x, across_x), me_y - core + lax.rem(core + c, cores))
        for x in range(across_x) for c in range(cores) if x or c
    ]
    far_off = [(me_x, lax.rem(me_y + cores * step, across_y)) for step in range(1, chips)]
    steps = (1, 2, across_y - 2, across_y - 1) if across_y > 4 else ()
    around = [(me_x, lax.rem(me_y + step, across_y)) for step in steps]
    barrier = pltpu.get_barrier_semaphore()
    for x, y in around + near_by + far_off:
        pl.semaphore_signal(barrier, inc=1, device_id=(x, y), device_id_type=MESH)


    def blank(ref, count, *spans):
        for start, size in spans:
            ref[:, start : start + size, :] = jnp.zeros((count, size, CZ), F32)

    blank(T1, 65, (0, 8), (40, 16))
    blank(T2, 33, (0, 8), (32, 8))
    blank(T3, 17, (0, 8))
    X4[0] = jnp.zeros((CY, CZ), F32)
    for level in (1, 2, 3):
        blank(B[level], NXL[level] + 1, (0, 8), *(((16, 8),) if level == 3 else ()))
        rows = ROWS[level]
        R[level][0] = jnp.zeros((rows, CZ), F32)
    GA[:, 2:8, :] = jnp.zeros((across_x * cores, 6, CZ), F32)
    GB[:, 6:8, :] = jnp.zeros((chips, 2, CZ), F32)

    @pl.when(first_y)
    def _():
        E[:, 4:8, :] = jnp.zeros((CX, 4, CZ), F32)
        YR[0, :, 0:5, :] = jnp.zeros((65, 5, CZ), F32)

    @pl.when(last_y)
    def _():
        E[:, 40:44, :] = jnp.zeros((CX, 4, CZ), F32)
        YR[1, :, 0:5, :] = jnp.zeros((65, 5, CZ), F32)

    @pl.when(me_y < 2)
    def _():
        YR[0, 0:17, 5:6, :] = jnp.zeros((17, 1, CZ), F32)

    @pl.when(me_y >= across_y - 2)
    def _():
        YR[1, 0:17, 5:6, :] = jnp.zeros((17, 1, CZ), F32)

    @pl.when(first_x)
    def _():
        C[0:4] = jnp.zeros((4, CY, CZ), F32)
        XR[0] = jnp.zeros((5, 24, CZ), F32)

    @pl.when(last_x)
    def _():
        C[CX + 4 : CX + 8] = jnp.zeros((4, CY, CZ), F32)
        XR[1] = jnp.zeros((5, 24, CZ), F32)

    a, c = iota((CZ, CZ), 0), iota((CZ, CZ), 1)
    weight = jnp.maximum(0, 16 - jnp.abs(a - 16 * c)).astype(F32) * 2.0**-20
    weight = jnp.where(c < 8, weight, 0.0)
    block = jnp.where(a < 8, gauss(a - c % 8, 8), 0.0)
    Z4[...] = stacked(jnp.dot(weight, block, precision=HIGHEST, preferred_element_type=F32))
    row, lane = iota((9 * CY, CZ), 0), iota((9 * CY, CZ), 1)
    weight = jnp.maximum(0, 16 - jnp.abs(row % CY - 16 * ((lane // 8) % 3))).astype(F32)
    K4[...] = jnp.where(lane // 24 == row // (2 * CY), weight, 0.0)
    rise = prolong_z()
    PZ[...] = jnp.concatenate([rise, rise], axis=0)
    r, a = iota((CZ, CZ), 0), iota((CZ, CZ), 1)
    rise = jnp.maximum(0, 16 - jnp.abs(a - 16 * (r % 8))).astype(F32) / 16.0
    rise = jnp.where(r < 72, rise, 0.0).astype(BF16)
    P4[...] = jnp.concatenate([rise, rise], axis=0)
    row, col = iota((cores * 80, 8 * across_x * cores), 0), iota((cores * 80, 8 * across_x * cores), 1)
    cell, slot = 2 * ((row // 16) % 5) + col % 8, col // 8
    spot, place = 8 * me_x + row % 16, 8 * (slot // cores) + cell
    valid = (slot % cores == row // 80) & (col % 8 < 2) & (cell < 9) & (place < 8 * across_x)
    valid = valid & (row % 16 < 9) & (spot < 8 * across_x)
    GX[...] = jnp.where(valid, gauss(spot - place, 8 * across_x), 0.0)
    r, c = iota((2 * CZ, 3 * CZ), 0), iota((2 * CZ, 3 * CZ), 1)
    PX[...] = (r % CZ == 8 * (c // CZ) + c % 8).astype(F32).astype(BF16)
    row, col = iota((CY, 8 * chips), 0), iota((CY, 8 * chips), 1)
    place = 2 * (cores * (col // 8) + (col % 8) // 3) + (col % 8) % 3
    valid = (col % 8 < 3 * cores) & (place < 2 * across_y)
    along = jnp.zeros((CY, 8 * chips), F32)
    for y in range(3):
        spot = 2 * me_y + y
        share = jnp.maximum(0, 16 - jnp.abs(row - 16 * y)).astype(F32) / 16.0
        term = jnp.where(valid & (spot < 2 * across_y), gauss(spot - place, 2 * across_y), 0.0)
        along = along + share * term
    GY[...] = along
    few.wait()
    WZ[...] = stacked(coarse_z(taps))
    W0[...] = stacked(toeplitz(taps, 0, (CZ, CZ), iota((CZ, CZ), 0) - iota((CZ, CZ), 1)))

    def remote(src, dst, send, recv, **target):
        return pltpu.make_async_remote_copy(
            src_ref=src, dst_ref=dst, send_sem=send, recv_sem=recv, device_id=target, device_id_type=MESH
        )

    def drain(ref, count, rows, sem):
        if count:
            part = ref.at[pl.ds(0, count), pl.ds(0, rows)]
            pltpu.make_async_copy(part, part, sem).wait()

    above_y, below_y = lax.rem(me_y + 1, across_y), lax.rem(me_y + across_y - 1, across_y)
    above_x, below_x = lax.rem(me_x + 1, across_x), lax.rem(me_x + across_x - 1, across_x)

    y0_up = remote(q.at[:, pl.ds(CY - 4, 4)], E.at[:, pl.ds(4, 4)], y0_send.at[0], y0_recv.at[0], gy=above_y)
    y0_down = remote(q.at[:, pl.ds(0, 4)], E.at[:, pl.ds(40, 4)], y0_send.at[1], y0_recv.at[1], gy=below_y)
    def down_x(i, carry):
        load(i).wait()
        for t in range(4):
            rows = pl.ds(8 + 8 * t, 8)
            value = E[pl.ds(16 * i, 16), rows, :]
            before = E[jnp.maximum(16 * i - 1, 0), rows, :]
            before = jnp.where(i > 0, before, 0.0)
            for k in range(8):
                T1[8 * i + k, rows, :] = (before if k == 0 else value[2 * k - 1]) + 2.0 * value[2 * k] + value[2 * k + 1]
            running = value[15]
            rising = running
            for k in range(14, 0, -1):
                running = running + value[k]
                rising = rising + running
            fine = pl.ds(8 * t, 8)
            X4[i, fine, :] = X4[i, fine, :] + (16.0 * (running + value[0]) - rising)
            X4[i + 1, fine, :] = rising
        return carry

    lax.fori_loop(0, CX // 16, down_x, 0)
    T1[64, 8:40, :] = E[CX - 1, 8:40, :]

    value = product(X4[...].reshape(9 * CY, CZ), Z4[...]) * K4[...]
    pick = ((iota((8, 9 * CY), 1) // CY) % 2 == iota((8, 9 * CY), 0)).astype(F32)
    mine = me_x * cores + core
    GA[mine, 0:2, :] = picked(pick, value)[0:2]
    pl.semaphore_wait(barrier, len(around + near_by + far_off))
    two = pl.ds(0, 2)
    for x, y in near_by:
        remote(GA.at[mine, two], GA.at[mine, two], ga_send, ga_recv, gx=x, gy=y).start()
    pl.when(jnp.logical_not(last_y))(y0_up.start)
    pl.when(jnp.logical_not(first_y))(y0_down.start)

    def down_y(i, carry):
        R1[i + 1] = (
            T1[i, pl.ds(7, 24, stride=2), :] + 2.0 * T1[i, pl.ds(8, 24, stride=2), :] + T1[i, pl.ds(9, 24, stride=2), :]
        )
        return carry

    lax.fori_loop(0, 65, down_y, 0, unroll=13)

    for level in (2, 3):
        finer, mid, n = R[level - 1], T[level], NXL[level]
        inner, rows = ROWS[level - 1], ROWS[level]
        pairs = finer[1 : 2 * n + 1].reshape(n, 2, inner, CZ)
        before = finer[0 : 2 * n].reshape(n, 2, inner, CZ)
        mid[0:n, 8 : 8 + inner, :] = before[:, 0] + 2.0 * pairs[:, 0] + pairs[:, 1]
        mid[n, 8 : 8 + inner, :] = finer[2 * n] + 2.0 * finer[2 * n + 1]
        R[level][1 : n + 2] = (
            mid[:, pl.ds(7, rows, stride=2), :]
            + 2.0 * mid[:, pl.ds(8, rows, stride=2), :]
            + mid[:, pl.ds(9, rows, stride=2), :]
        )

    A1[4:69] = product(R1[1:67].reshape(66 * 24, CZ), WZ[...]).reshape(66, 24, CZ)[0:65]
    A2[4:37] = product(R2[1:34].reshape(33 * 16, CZ), WZ[...]).reshape(33, 16, CZ)
    A3[4:21] = product(R3[1:19].reshape(18 * 8, CZ), WZ[...]).reshape(18, 8, CZ)[0:17]

    @pl.when(last_x)
    def _():
        for level in (1, 2, 3):
            A[level][NXL[level] + 4] = jnp.zeros((ROWS[level], CZ), F32)

    for way in (0, 1):
        for i in range(5):
            at = {level: (NXL[level] if way == 0 else 4) + i for level in (1, 2, 3)}
            wide = A1[at[1]]
            lane = iota((24, CZ), 1)
            XS[way, i] = jnp.where(lane < 64, wide, 0.0)
            lane = iota((16, CZ), 1)
            XS[way, i, 0:16, :] = jnp.where(lane >= 64, A2[at[2]], XS[way, i, 0:16, :])
            lane = iota((8, CZ), 1)
            XS[way, i, 0:8, :] = jnp.where(lane >= 96, A3[at[3]], XS[way, i, 0:8, :])
    cx_up = remote(XS.at[0], XR.at[0], cx_send.at[0], cx_recv.at[0], gx=above_x)
    cx_down = remote(XS.at[1], XR.at[1], cx_send.at[1], cx_recv.at[1], gx=below_x)
    pl.when(jnp.logical_not(last_x))(cx_up.start)
    pl.when(jnp.logical_not(first_x))(cx_down.start)

    w0 = [taps[0, k] for k in range(2 * REACH + 1)]

    def mid_y(i, carry):
        C[4 + i, 8:24, :] = weighted([E[i, 12 + k : 28 + k, :] for k in range(9)], w0)
        return carry

    def outer_y(i, carry):
        C[4 + i, 0:8, :] = weighted([E[i, 4 + k : 12 + k, :] for k in range(9)], w0)
        C[4 + i, 24:32, :] = weighted([E[i, 28 + k : 36 + k, :] for k in range(9)], w0)
        return carry

    def finest_x(i, tiles):
        for t in tiles:
            rows = pl.ds(8 * t, 8)
            value = C[pl.ds(16 * i, 24), rows, :]
            out[pl.ds(16 * i, 16), rows, :] = weighted([value[k : k + 16] for k in range(9)], w0)

    def finest_z(first, count):
        at = pl.ds(first, count)
        out[at] = product(out[at].reshape(count * CY, CZ), W0[...]).reshape(count, CY, CZ)

    lax.fori_loop(0, CX, mid_y, 0, unroll=8)

    pl.when(jnp.logical_not(first_x))(cx_up.wait_recv)
    pl.when(jnp.logical_not(last_x))(cx_down.wait_recv)
    for level in (1, 2, 3):
        array, rows, n = A[level], ROWS[level], NXL[level]
        array[0:4] = XR[0, 0:4, 0:rows, :]
        array[4] = array[4] + XR[0, 4, 0:rows, :]
        array[n + 4] = array[n + 4] + XR[1, 0, 0:rows, :]
        array[n + 5 : n + 9] = XR[1, 1:5, 0:rows, :]
        wl = [taps[level, k] for k in range(2 * REACH + 1)]

        def along_x(i, carry, array=array, target=B[level], rows=rows, wl=wl):
            target[i, pl.ds(8, rows), :] = weighted([array[i + k] for k in range(9)], wl)
            return carry

        lax.fori_loop(0, n + 1, along_x, 0, unroll={1: 5, 2: 11, 3: 17}[level])

        @pl.when(last_x)
        def _(target=B[level], rows=rows, n=n):
            target[n, pl.ds(8, rows), :] = jnp.zeros((rows, CZ), F32)

        @pl.when(last_y)
        def _(target=B[level], level=level, n=n):
            target[:, pl.ds(8 + NYL[level], 1), :] = jnp.zeros((n + 1, 1, CZ), F32)

    lane = iota((8, CZ), 1)
    for way in (0, 1):
        start = {level: 8 + (NYL[level] - 4 if way == 0 else 0) for level in (1, 2, 3)}
        YS[way] = B1[:, start[1] : start[1] + 8, :]
        YS[way, 0:33] = jnp.where(lane >= 64, B2[:, start[2] : start[2] + 8, :], B1[0:33, start[1] : start[1] + 8, :])
        YS[way, 0:17] = jnp.where(lane >= 96, B3[:, start[3] : start[3] + 8, :], YS[way, 0:17])
    rows5 = pl.ds(0, 5)
    cy_up = remote(YS.at[0, :, rows5], YR.at[0, :, rows5], cy_send.at[0], cy_recv.at[0], gy=above_y)
    cy_down = remote(YS.at[1, :, rows5], YR.at[1, :, rows5], cy_send.at[1], cy_recv.at[1], gy=below_y)
    pl.when(jnp.logical_not(last_y))(cy_up.start)
    pl.when(jnp.logical_not(first_y))(cy_down.start)
    near, far = pl.ds(0, 17), pl.ds(5, 1)
    c2_up = remote(
        YS.at[0, near, pl.ds(4, 1)], YR.at[0, near, far], c2_send.at[0], c2_recv.at[0],
        gy=lax.rem(me_y + 2, across_y),
    )
    c2_down = remote(
        YS.at[1, near, pl.ds(0, 1)], YR.at[1, near, far], c2_send.at[1], c2_recv.at[1],
        gy=lax.rem(me_y + across_y - 2, across_y),
    )
    pl.when(me_y < across_y - 2)(c2_up.start)
    pl.when(me_y >= 2)(c2_down.start)

    pl.when(jnp.logical_not(first_y))(y0_up.wait_recv)
    pl.when(jnp.logical_not(last_y))(y0_down.wait_recv)

    lax.fori_loop(0, 4, outer_y, 0, unroll=4)
    lax.fori_loop(CX - 4, CX, outer_y, 0, unroll=4)
    x0_up = remote(C.at[pl.ds(CX, 4)], C.at[pl.ds(0, 4)], x0_send.at[0], x0_recv.at[0], gx=above_x)
    x0_down = remote(C.at[pl.ds(4, 4)], C.at[pl.ds(CX + 4, 4)], x0_send.at[1], x0_recv.at[1], gx=below_x)
    pl.when(jnp.logical_not(last_x))(x0_up.start)
    pl.when(jnp.logical_not(first_x))(x0_down.start)

    row, col = iota((8, 48 * cores), 0), iota((8, 48 * cores), 1)
    gather = ((row // 3 == (col // 16) % cores) & (row % 3 == col // (16 * cores))).astype(F32)
    drain(GA, across_x * cores - 1, 2, ga_recv)
    value = general(GX[...], GA[...].reshape(8 * across_x * cores, CZ))
    value = value.reshape(cores, 5, 16, CZ)
    lane = iota((cores, 16, CZ), 2)
    total = jnp.where(lane < 24, value[:, 0], 0.0)
    for g in range(1, 5):
        total = total + jnp.where(lane < 24, pltpu.roll(value[:, g], CZ - 24 * g, 2), 0.0)
    both = jnp.concatenate(split(total.reshape(cores * 16, CZ)), axis=1)
    value = jnp.dot(both, PX[...], preferred_element_type=F32)
    row, lane = iota((cores * 16, CZ), 0), iota((cores * 16, CZ), 1)
    keep = (lane // 8 == row % 16) & (lane < 72)
    value = jnp.concatenate([jnp.where(keep, value[:, y * CZ : y * CZ + CZ], 0.0) for y in range(3)], axis=0)
    here = me_y // cores
    GB[here] = picked(gather, value)
    six = pl.ds(0, 6)
    for x, y in far_off:
        remote(GB.at[here, six], GB.at[here, six], gb_send, gb_recv, gy=y).start()

    lax.fori_loop(4, CX - 4, outer_y, 0, unroll=6)

    lax.fori_loop(1, CX // 16 - 1, lambda i, c: (finest_x(i, (1, 2)), c)[1], 0)

    lax.fori_loop(1, CX // 16 - 1, lambda i, c: (finest_x(i, (0, 3)), c)[1], 0)

    finest_z(16, CX - 32)

    pl.when(jnp.logical_not(first_x))(x0_up.wait_recv)
    pl.when(jnp.logical_not(last_x))(x0_down.wait_recv)
    finest_x(0, range(4))
    finest_x(CX // 16 - 1, range(4))
    finest_z(0, 16)
    finest_z(CX - 16, 16)

    pl.when(jnp.logical_not(first_y))(cy_up.wait_recv)
    pl.when(jnp.logical_not(last_y))(cy_down.wait_recv)
    pl.when(me_y >= 2)(c2_up.wait_recv)
    pl.when(me_y < across_y - 2)(c2_down.wait_recv)
    row8 = iota((8, CZ), 0)
    for level in (1, 2, 3):
        array, n, rows, count = B[level], NYL[level], ROWS[level], NXL[level] + 1
        wl = [taps[level, k] for k in range(2 * REACH + 1)]

        def along_y(x, carry, array=array, target=U[level], n=n, rows=rows, level=level, wl=wl):
            array[x, 4:12, :] = array[x, 4:12, :] + jnp.where(row8 < 5, YR[0, x], 0.0)
            array[x, 8 + n : 16 + n, :] = array[x, 8 + n : 16 + n, :] + jnp.where(row8 < 5, YR[1, x], 0.0)
            if level == 3:
                array[x, 4:5, :] = array[x, 4:5, :] + YR[0, x, 5:6, :]
                array[x, 16:17, :] = array[x, 16:17, :] + YR[1, x, 5:6, :]
            target[x] = weighted([array[x, 4 + k : 4 + k + rows, :] for k in range(9)], wl)
            return carry

        lax.fori_loop(0, count, along_y, 0, unroll={1: 5, 2: 11, 3: 17}[level])

        @pl.when(last_y)
        def _(target=U[level], n=n, count=count):
            target[0:count, n : n + 1, :] = jnp.zeros((count, 1, CZ), F32)

    lane = iota((8, CZ), 1)
    U3[...] = jnp.where((lane >= 96) & (lane < 112), U3[...], 0.0)
    for level, source, wide in ((2, U3, G2), (1, U2, G1)):
        half = {2: 8, 1: 16}[level]
        target, rows, n = U[level], ROWS[level], NXL[level]
        first, cells = LANES[level]

        low = source[:, 0:half, :]
        high = pltpu.roll(low, half - 1, 1)
        wide[:, pl.ds(0, half, stride=2), :] = low
        wide[:, pl.ds(1, half, stride=2), :] = 0.5 * (low + high)
        lane = iota((rows, CZ), 1)
        own = (lane >= first) & (lane < first + cells)
        low, high = wide[0 : n // 2, 0:rows, :], wide[1 : n // 2 + 1, 0:rows, :]
        both = jnp.stack([low, 0.5 * (low + high)], axis=1).reshape(n, rows, CZ)
        target[0:n] = jnp.where(own, target[0:n], both)
        target[n] = jnp.where(own, target[n], wide[n // 2, 0:rows, :])

    high, low = split(U1[...].reshape(66 * 24, CZ))
    both = jnp.concatenate([high, low], axis=1)
    E1Z[...] = jnp.dot(both, PZ[...], preferred_element_type=F32).reshape(66, 24, CZ)

    def rise_y(x, carry):
        low, high = E1Z[x, 0:16, :], E1Z[x, 1:17, :]
        G0[x, pl.ds(0, 16, stride=2), :] = low
        G0[x, pl.ds(1, 16, stride=2), :] = 0.5 * (low + high)
        return carry

    lax.fori_loop(0, 65, rise_y, 0, unroll=13)

    def finish(i, carry):
        low, high = G0[i], G0[i + 1]
        out[2 * i] = out[2 * i] + low
        out[2 * i + 1] = out[2 * i + 1] + 0.5 * (low + high)
        return carry

    lax.fori_loop(0, CX // 2, finish, 0, unroll=4)

    drain(GB, chips - 1, 6, gb_recv)
    value = general(GY[...], GB[...].reshape(8 * chips, CZ))
    lane = iota((CY, CZ), 1)
    spread = jnp.concatenate([jnp.where(lane // 8 == x, value, 0.0) for x in range(9)], axis=0)
    high, low = split(spread)
    both = jnp.concatenate([high, low], axis=1)
    value = jnp.dot(both, P4[...], preferred_element_type=F32).reshape(9, CY, CZ)
    coarsest[...] = value[:8]
    slopes[...] = (value[1:] - value[:8]) * (1.0 / 16.0)

    pl.when(jnp.logical_not(last_y))(y0_up.wait_send)
    pl.when(jnp.logical_not(first_y))(y0_down.wait_send)
    pl.when(jnp.logical_not(last_x))(x0_up.wait_send)
    pl.when(jnp.logical_not(first_x))(x0_down.wait_send)
    pl.when(jnp.logical_not(last_x))(cx_up.wait_send)
    pl.when(jnp.logical_not(first_x))(cx_down.wait_send)
    pl.when(jnp.logical_not(last_y))(cy_up.wait_send)
    pl.when(jnp.logical_not(first_y))(cy_down.wait_send)
    pl.when(me_y < across_y - 2)(c2_up.wait_send)
    pl.when(me_y >= 2)(c2_down.wait_send)
    drain(GA, across_x * cores - 1, 2, ga_send)
    drain(GB, chips - 1, 6, gb_send)


def last(fine, coarse, slope, out, done, sem):
    chunks = 8
    depth = CX // chunks
    copies = []
    for i in range(chunks):
        for x in range(i * depth, i * depth + depth):
            done[x] = fine[x] + (coarse[x // 16] + float(x % 16) * slope[x // 16])
        at = pl.ds(i * depth, depth)
        copies.append(pltpu.make_async_copy(done.at[at], out.at[at], sem.at[i]))
        copies[-1].start()
    for copy in copies:
        copy.wait()


def solution(mesh):
    across_x, across_y = mesh.shape["gx"], mesh.shape["gy"]

    cores = 2 if across_y > 1 else 1

    def vmem(*shape, dtype=F32):
        return pltpu.VMEM(shape, dtype)

    pair = pltpu.SemaphoreType.DMA((2,))
    single = pltpu.SemaphoreType.DMA
    scratch = [
        pltpu.SMEM((4, 9), F32),
        vmem(CX, 48, CZ),
        vmem(CX + 8, CY, CZ),
        vmem(65, 56, CZ), vmem(33, 40, CZ), vmem(17, 24, CZ), vmem(9, CY, CZ),
        vmem(67, 24, CZ), vmem(35, 16, CZ), vmem(19, 8, CZ),
        vmem(73, 24, CZ), vmem(41, 16, CZ), vmem(25, 8, CZ),
        vmem(65, 40, CZ), vmem(33, 32, CZ), vmem(17, 24, CZ),
        vmem(66, 24, CZ), vmem(33, 16, CZ), vmem(17, 8, CZ),
        vmem(17, 16, CZ), vmem(33, 32, CZ), vmem(65, 32, CZ),
        vmem(2, 5, 24, CZ), vmem(2, 5, 24, CZ),
        vmem(2, 65, 8, CZ), vmem(2, 65, 8, CZ),
        vmem(across_x * cores, 8, CZ), vmem(across_y // cores, 8, CZ),
        vmem(2 * CZ, 2 * CZ, dtype=BF16), vmem(2 * CZ, 2 * CZ, dtype=BF16), vmem(2 * CZ, CZ, dtype=BF16), vmem(2 * CZ, CZ, dtype=BF16),
        vmem(2 * CZ, 2 * CZ, dtype=BF16), vmem(9 * CY, CZ),
        vmem(cores * 80, 8 * across_x * cores), vmem(2 * CZ, 3 * CZ, dtype=BF16), vmem(CY, 8 * across_y // cores),
        vmem(66, 24, CZ),
        single, pltpu.SemaphoreType.DMA((CX // 16,)),
        pair, pair, pair, pair, pair, pair, pair, pair, pair, pair,
        single, single, single, single,
    ]

    def local(charge, level_taps):
        fine, coarse, slope = pl.pallas_call(
            functools.partial(kernel, across_x, across_y),
            out_shape=[jax.ShapeDtypeStruct((CX, CY, CZ), F32), *[jax.ShapeDtypeStruct((8, CY, CZ), F32)] * 2],
            in_specs=[pl.BlockSpec(memory_space=pltpu.HBM), pl.BlockSpec(memory_space=pltpu.HBM)],
            out_specs=[pl.BlockSpec(memory_space=pltpu.VMEM)] * 3,
            scratch_shapes=scratch,
            compiler_params=pltpu.CompilerParams(
                collective_id=0, has_side_effects=True, vmem_limit_bytes=48 * 1024 * 1024
            ),
        )(*(pltpu.with_memory_space_constraint(array, pltpu.HBM) for array in (level_taps, charge)))
        return pl.pallas_call(
            last,
            out_shape=jax.ShapeDtypeStruct((CX, CY, CZ), F32),
            in_specs=[pl.BlockSpec(memory_space=pltpu.VMEM)] * 3,
            out_specs=pl.BlockSpec(memory_space=pltpu.HBM),
            scratch_shapes=[vmem(CX, CY, CZ), pltpu.SemaphoreType.DMA((8,))],
            compiler_params=pltpu.CompilerParams(vmem_limit_bytes=8 * 1024 * 1024),
        )(fine, coarse, slope)

    spec = P("gx", "gy", None)
    return jax.shard_map(local, mesh=mesh, in_specs=(spec, P()), out_specs=spec, check_vma=False)
```

```python
import functools
import math

import jax
import jax.numpy as jnp
from jax import lax
from jax.experimental import pallas as pl
from jax.experimental.pallas import tpu as pltpu
from jax.sharding import PartitionSpec as P

F32 = jnp.float32
BF16 = jnp.bfloat16
HIGHEST = lax.Precision.HIGHEST
MESH = pl.DeviceIdType.MESH

CX, CY, CZ = 128, 32, 128
REACH = 4
LANES = {1: (0, 64), 2: (64, 32), 3: (96, 16)}
NXL = {1: 64, 2: 32, 3: 16, 4: 8}
NYL = {1: 16, 2: 8, 3: 4, 4: 2}
ROWS = {1: 24, 2: 16, 3: 8, 4: 8}


def iota(shape, dim):
    return lax.broadcasted_iota(jnp.int32, shape, dim)


def gauss(distance, length):
    spread = max(length, 4) / 2.0
    scaled = distance.astype(F32) / spread
    return jnp.exp(-scaled * scaled) / (math.sqrt(math.pi) * spread)


def split(value):
    high = value.astype(BF16)
    return high, (value - high.astype(F32)).astype(BF16)


def stacked(matrix):
    high, low = split(matrix)
    upper = jnp.concatenate([high, low], axis=1)
    lower = jnp.concatenate([high, jnp.zeros_like(high)], axis=1)
    return jnp.concatenate([upper, lower], axis=0)


def product(value, weights):
    high, low = split(value)
    both = jnp.dot(jnp.concatenate([high, low], axis=1), weights, preferred_element_type=F32)
    return both[:, :CZ] + both[:, CZ:]


def picked(matrix, value):
    both = jnp.concatenate(split(value), axis=0)
    return jnp.dot(jnp.concatenate([matrix.astype(BF16)] * 2, axis=1), both, preferred_element_type=F32)


def general(matrix, value):
    (m_high, m_low), (v_high, v_low) = split(matrix), split(value)
    left = jnp.concatenate([m_high, m_low, m_high], axis=1)
    right = jnp.concatenate([v_high, v_high, v_low], axis=0)
    return jnp.dot(left, right, preferred_element_type=F32)


def toeplitz(taps, level, shape, offset):
    matrix = jnp.zeros(shape, F32)
    for k in range(2 * REACH + 1):
        matrix = jnp.where(offset == k - REACH, taps[level, k], matrix)
    return matrix


def coarse_z(taps):
    a, c = iota((CZ, CZ), 0), iota((CZ, CZ), 1)
    down = jnp.zeros((CZ, CZ), F32)
    mix = jnp.zeros((CZ, CZ), F32)
    for level, (first, cells) in LANES.items():
        step = 2**level
        here = (c >= first) & (c < first + cells)
        weight = jnp.maximum(0, step - jnp.abs(a - step * (c - first)))
        down = jnp.where(here, weight.astype(F32) * 2.0 ** (-5 * level), down)
        inside = here & (a >= first) & (a < first + cells)
        block = toeplitz(taps, level, (CZ, CZ), a - c)
        mix = jnp.where(inside, block, mix)
    return jnp.dot(down, mix, precision=HIGHEST, preferred_element_type=F32)


def prolong_z():
    r, a = iota((CZ, CZ), 0), iota((CZ, CZ), 1)
    up = jnp.zeros((CZ, CZ), F32)
    for level, (first, cells) in LANES.items():
        step = 2**level
        here = (r >= first) & (r < first + cells)
        weight = jnp.maximum(0, step - jnp.abs(a - step * (r - first)))
        up = jnp.where(here, weight.astype(F32) * 2.0**-level, up)
    return up.astype(BF16)


def weighted(pieces, weights):
    total = weights[REACH] * pieces[REACH]
    for k in range(REACH):
        total = total + weights[k] * (pieces[k] + pieces[2 * REACH - k])
    return total


def kernel(
    across_x, across_y, taps_in, q, out, coarsest, slopes,
    taps,
    E, C, T1, T2, T3, X4, R1, R2, R3, A1, A2, A3, B1, B2, B3, U1, U2, U3, G2, G1, G0,
    XS, XR, YS, YR, GA, GB, WZ, W0, PZ, P4, Z4, K4, GX, PX, GY, E1Z,
    taps_sem, in_sem, y0_send, y0_recv, x0_send, x0_recv, cx_send, cx_recv, cy_send, cy_recv,
    c2_send, c2_recv, ga_send, ga_recv, gb_send, gb_recv,
):
    me_x, me_y = lax.axis_index("gx"), lax.axis_index("gy")
    first_x, last_x = me_x == 0, me_x == across_x - 1
    first_y, last_y = me_y == 0, me_y == across_y - 1
    R, A, B, U, T = {1: R1, 2: R2, 3: R3}, {1: A1, 2: A2, 3: A3}, {1: B1, 2: B2, 3: B3}, {1: U1, 2: U2, 3: U3}, {2: T2, 3: T3}

    few = pltpu.make_async_copy(taps_in, taps, taps_sem)
    few.start()
    def load(i):
        at = pl.ds(i * 16, 16)
        return pltpu.make_async_copy(q.at[at], E.at[at, pl.ds(8, CY)], in_sem.at[i])

    for i in range(CX // 16):
        load(i).start()

    cores = 2 if across_y > 1 else 1
    chips = across_y // cores
    core = lax.rem(me_y, cores)
    near_by = [
        (lax.rem(me_x + x, across_x), me_y - core + lax.rem(core + c, cores))
        for x in range(across_x) for c in range(cores) if x or c
    ]
    far_off = [(me_x, lax.rem(me_y + cores * step, across_y)) for step in sorted(range(1, chips), key=lambda step: abs(2 * step - chips))]
    steps = (1, 2, across_y - 2, across_y - 1) if across_y > 4 else ()
    around = [(me_x, lax.rem(me_y + step, across_y)) for step in steps]
    barrier = pltpu.get_barrier_semaphore()
    for x, y in around + near_by + far_off:
        pl.semaphore_signal(barrier, inc=1, device_id=(x, y), device_id_type=MESH)


    def blank(ref, count, *spans):
        for start, size in spans:
            ref[:, start : start + size, :] = jnp.zeros((count, size, CZ), F32)

    blank(T1, 65, (0, 8), (40, 16))
    blank(T2, 33, (0, 8), (32, 8))
    blank(T3, 17, (0, 8))
    X4[0] = jnp.zeros((CY, CZ), F32)
    for level in (1, 2, 3):
        blank(B[level], NXL[level] + 1, (0, 8), *(((16, 8),) if level == 3 else ()))
        rows = ROWS[level]
        R[level][0] = jnp.zeros((rows, CZ), F32)
    XR[:, :, 17:24, :] = jnp.zeros((2, 5, 7, CZ), F32)
    GA[:, 2:8, :] = jnp.zeros((across_x * cores, 6, CZ), F32)
    GB[:, 6:8, :] = jnp.zeros((chips, 2, CZ), F32)

    @pl.when(first_y)
    def _():
        E[:, 4:8, :] = jnp.zeros((CX, 4, CZ), F32)
        YR[0, :, 0:5, :] = jnp.zeros((65, 5, CZ), F32)

    @pl.when(last_y)
    def _():
        E[:, 40:44, :] = jnp.zeros((CX, 4, CZ), F32)
        YR[1, :, 0:5, :] = jnp.zeros((65, 5, CZ), F32)

    @pl.when(me_y < 2)
    def _():
        YR[0, 0:17, 5:6, :] = jnp.zeros((17, 1, CZ), F32)

    @pl.when(me_y >= across_y - 2)
    def _():
        YR[1, 0:17, 5:6, :] = jnp.zeros((17, 1, CZ), F32)

    @pl.when(first_x)
    def _():
        C[0:4] = jnp.zeros((4, CY, CZ), F32)
        XR[0] = jnp.zeros((5, 24, CZ), F32)

    @pl.when(last_x)
    def _():
        C[CX + 4 : CX + 8] = jnp.zeros((4, CY, CZ), F32)
        XR[1] = jnp.zeros((5, 24, CZ), F32)

    a, c = iota((CZ, CZ), 0), iota((CZ, CZ), 1)
    weight = jnp.maximum(0, 16 - jnp.abs(a - 16 * c)).astype(F32) * 2.0**-20
    weight = jnp.where(c < 8, weight, 0.0)
    block = jnp.where(a < 8, gauss(a - c % 8, 8), 0.0)
    Z4[...] = stacked(jnp.dot(weight, block, precision=HIGHEST, preferred_element_type=F32))
    row, lane = iota((9 * CY, CZ), 0), iota((9 * CY, CZ), 1)
    weight = jnp.maximum(0, 16 - jnp.abs(row % CY - 16 * ((lane // 8) % 3))).astype(F32)
    K4[...] = jnp.where(lane // 24 == row // (2 * CY), weight, 0.0)
    rise = prolong_z()
    PZ[...] = jnp.concatenate([rise, rise], axis=0)
    r, a = iota((CZ, CZ), 0), iota((CZ, CZ), 1)
    rise = jnp.maximum(0, 16 - jnp.abs(a - 16 * (r % 8))).astype(F32) / 16.0
    rise = jnp.where(r < 72, rise, 0.0).astype(BF16)
    P4[...] = jnp.concatenate([rise, rise], axis=0)
    row, col = iota((cores * 80, 8 * across_x * cores), 0), iota((cores * 80, 8 * across_x * cores), 1)
    cell, slot = 2 * ((row // 16) % 5) + col % 8, col // 8
    spot, place = 8 * me_x + row % 16, 8 * (slot // cores) + cell
    valid = (slot % cores == row // 80) & (col % 8 < 2) & (cell < 9) & (place < 8 * across_x)
    valid = valid & (row % 16 < 9) & (spot < 8 * across_x)
    GX[...] = jnp.where(valid, gauss(spot - place, 8 * across_x), 0.0)
    r, c = iota((2 * CZ, 3 * CZ), 0), iota((2 * CZ, 3 * CZ), 1)
    PX[...] = (r % CZ == 8 * (c // CZ) + c % 8).astype(F32).astype(BF16)
    row, col = iota((CY, 8 * chips), 0), iota((CY, 8 * chips), 1)
    place = 2 * (cores * (col // 8) + (col % 8) // 3) + (col % 8) % 3
    valid = (col % 8 < 3 * cores) & (place < 2 * across_y)
    along = jnp.zeros((CY, 8 * chips), F32)
    for y in range(3):
        spot = 2 * me_y + y
        share = jnp.maximum(0, 16 - jnp.abs(row - 16 * y)).astype(F32) / 16.0
        term = jnp.where(valid & (spot < 2 * across_y), gauss(spot - place, 2 * across_y), 0.0)
        along = along + share * term
    GY[...] = along
    few.wait()
    WZ[...] = stacked(coarse_z(taps))
    W0[...] = stacked(toeplitz(taps, 0, (CZ, CZ), iota((CZ, CZ), 0) - iota((CZ, CZ), 1)))

    def remote(src, dst, send, recv, **target):
        return pltpu.make_async_remote_copy(
            src_ref=src, dst_ref=dst, send_sem=send, recv_sem=recv, device_id=target, device_id_type=MESH
        )

    def drain(ref, count, rows, sem):
        if count:
            part = ref.at[pl.ds(0, count), pl.ds(0, rows)]
            pltpu.make_async_copy(part, part, sem).wait()

    above_y, below_y = lax.rem(me_y + 1, across_y), lax.rem(me_y + across_y - 1, across_y)
    above_x, below_x = lax.rem(me_x + 1, across_x), lax.rem(me_x + across_x - 1, across_x)

    y0_up = remote(q.at[:, pl.ds(CY - 4, 4)], E.at[:, pl.ds(4, 4)], y0_send.at[0], y0_recv.at[0], gy=above_y)
    y0_down = remote(q.at[:, pl.ds(0, 4)], E.at[:, pl.ds(40, 4)], y0_send.at[1], y0_recv.at[1], gy=below_y)
    def down_x(i, carry):
        load(i).wait()
        for t in range(4):
            rows = pl.ds(8 + 8 * t, 8)
            value = E[pl.ds(16 * i, 16), rows, :]
            before = E[jnp.maximum(16 * i - 1, 0), rows, :]
            before = jnp.where(i > 0, before, 0.0)
            for k in range(8):
                T1[8 * i + k, rows, :] = (before if k == 0 else value[2 * k - 1]) + 2.0 * value[2 * k] + value[2 * k + 1]
            running = value[15]
            rising = running
            for k in range(14, 0, -1):
                running = running + value[k]
                rising = rising + running
            fine = pl.ds(8 * t, 8)
            X4[i, fine, :] = X4[i, fine, :] + (16.0 * (running + value[0]) - rising)
            X4[i + 1, fine, :] = rising
        return carry

    lax.fori_loop(0, CX // 16, down_x, 0)
    T1[64, 8:40, :] = E[CX - 1, 8:40, :]

    value = product(X4[...].reshape(9 * CY, CZ), Z4[...]) * K4[...]
    pick = ((iota((8, 9 * CY), 1) // CY) % 2 == iota((8, 9 * CY), 0)).astype(F32)
    mine = me_x * cores + core
    GA[mine, 0:2, :] = picked(pick, value)[0:2]
    pl.semaphore_wait(barrier, len(around + near_by + far_off))
    two = pl.ds(0, 2)
    for x, y in near_by:
        remote(GA.at[mine, two], GA.at[mine, two], ga_send, ga_recv, gx=x, gy=y).start()
    pl.when(jnp.logical_not(last_y))(y0_up.start)
    pl.when(jnp.logical_not(first_y))(y0_down.start)

    def down_y(i, carry):
        R1[i + 1] = (
            T1[i, pl.ds(7, 24, stride=2), :] + 2.0 * T1[i, pl.ds(8, 24, stride=2), :] + T1[i, pl.ds(9, 24, stride=2), :]
        )
        return carry

    lax.fori_loop(0, 65, down_y, 0, unroll=13)

    for level in (2, 3):
        finer, mid, n = R[level - 1], T[level], NXL[level]
        inner, rows = ROWS[level - 1], ROWS[level]
        pairs = finer[1 : 2 * n + 1].reshape(n, 2, inner, CZ)
        before = finer[0 : 2 * n].reshape(n, 2, inner, CZ)
        mid[0:n, 8 : 8 + inner, :] = before[:, 0] + 2.0 * pairs[:, 0] + pairs[:, 1]
        mid[n, 8 : 8 + inner, :] = finer[2 * n] + 2.0 * finer[2 * n + 1]
        R[level][1 : n + 2] = (
            mid[:, pl.ds(7, rows, stride=2), :]
            + 2.0 * mid[:, pl.ds(8, rows, stride=2), :]
            + mid[:, pl.ds(9, rows, stride=2), :]
        )

    A1[4:69] = product(R1[1:67].reshape(66 * 24, CZ), WZ[...]).reshape(66, 24, CZ)[0:65]
    A2[4:37] = product(R2[1:34].reshape(33 * 16, CZ), WZ[...]).reshape(33, 16, CZ)
    A3[4:21] = product(R3[1:19].reshape(18 * 8, CZ), WZ[...]).reshape(18, 8, CZ)[0:17]

    @pl.when(last_x)
    def _():
        for level in (1, 2, 3):
            A[level][NXL[level] + 4] = jnp.zeros((ROWS[level], CZ), F32)

    for way in (0, 1):
        for i in range(5):
            at = {level: (NXL[level] if way == 0 else 4) + i for level in (1, 2, 3)}
            wide = A1[at[1]]
            lane = iota((24, CZ), 1)
            XS[way, i] = jnp.where(lane < 64, wide, 0.0)
            lane = iota((16, CZ), 1)
            XS[way, i, 0:16, :] = jnp.where(lane >= 64, A2[at[2]], XS[way, i, 0:16, :])
            lane = iota((8, CZ), 1)
            XS[way, i, 0:8, :] = jnp.where(lane >= 96, A3[at[3]], XS[way, i, 0:8, :])
    used = pl.ds(0, 17)
    cx_up = remote(XS.at[0, :, used], XR.at[0, :, used], cx_send.at[0], cx_recv.at[0], gx=above_x)
    cx_down = remote(XS.at[1, :, used], XR.at[1, :, used], cx_send.at[1], cx_recv.at[1], gx=below_x)
    pl.when(jnp.logical_not(last_x))(cx_up.start)
    pl.when(jnp.logical_not(first_x))(cx_down.start)

    w0 = [taps[0, k] for k in range(2 * REACH + 1)]

    def mid_y(i, carry):
        C[4 + i, 8:24, :] = weighted([E[i, 12 + k : 28 + k, :] for k in range(9)], w0)
        return carry

    def outer_y(i, carry):
        C[4 + i, 0:8, :] = weighted([E[i, 4 + k : 12 + k, :] for k in range(9)], w0)
        C[4 + i, 24:32, :] = weighted([E[i, 28 + k : 36 + k, :] for k in range(9)], w0)
        return carry

    def finest_x(i, tiles):
        for t in tiles:
            rows = pl.ds(8 * t, 8)
            value = C[pl.ds(16 * i, 24), rows, :]
            out[pl.ds(16 * i, 16), rows, :] = weighted([value[k : k + 16] for k in range(9)], w0)

    def finest_z(first, count):
        at = pl.ds(first, count)
        out[at] = product(out[at].reshape(count * CY, CZ), W0[...]).reshape(count, CY, CZ)

    lax.fori_loop(0, CX, mid_y, 0, unroll=8)

    pl.when(jnp.logical_not(first_x))(cx_up.wait_recv)
    pl.when(jnp.logical_not(last_x))(cx_down.wait_recv)
    for level in (1, 2, 3):
        array, rows, n = A[level], ROWS[level], NXL[level]
        array[0:4] = XR[0, 0:4, 0:rows, :]
        array[4] = array[4] + XR[0, 4, 0:rows, :]
        array[n + 4] = array[n + 4] + XR[1, 0, 0:rows, :]
        array[n + 5 : n + 9] = XR[1, 1:5, 0:rows, :]
        wl = [taps[level, k] for k in range(2 * REACH + 1)]

        def along_x(i, carry, array=array, target=B[level], rows=rows, wl=wl):
            target[i, pl.ds(8, rows), :] = weighted([array[i + k] for k in range(9)], wl)
            return carry

        lax.fori_loop(0, n + 1, along_x, 0, unroll={1: 5, 2: 11, 3: 17}[level])

        @pl.when(last_x)
        def _(target=B[level], rows=rows, n=n):
            target[n, pl.ds(8, rows), :] = jnp.zeros((rows, CZ), F32)

        @pl.when(last_y)
        def _(target=B[level], level=level, n=n):
            target[:, pl.ds(8 + NYL[level], 1), :] = jnp.zeros((n + 1, 1, CZ), F32)

    lane = iota((8, CZ), 1)
    for way in (0, 1):
        start = {level: 8 + (NYL[level] - 4 if way == 0 else 0) for level in (1, 2, 3)}
        YS[way] = B1[:, start[1] : start[1] + 8, :]
        YS[way, 0:33] = jnp.where(lane >= 64, B2[:, start[2] : start[2] + 8, :], B1[0:33, start[1] : start[1] + 8, :])
        YS[way, 0:17] = jnp.where(lane >= 96, B3[:, start[3] : start[3] + 8, :], YS[way, 0:17])
    rows5 = pl.ds(0, 5)
    cy_up = remote(YS.at[0, :, rows5], YR.at[0, :, rows5], cy_send.at[0], cy_recv.at[0], gy=above_y)
    cy_down = remote(YS.at[1, :, rows5], YR.at[1, :, rows5], cy_send.at[1], cy_recv.at[1], gy=below_y)
    pl.when(jnp.logical_not(last_y))(cy_up.start)
    pl.when(jnp.logical_not(first_y))(cy_down.start)
    near, far = pl.ds(0, 17), pl.ds(5, 1)
    c2_up = remote(
        YS.at[0, near, pl.ds(4, 1)], YR.at[0, near, far], c2_send.at[0], c2_recv.at[0],
        gy=lax.rem(me_y + 2, across_y),
    )
    c2_down = remote(
        YS.at[1, near, pl.ds(0, 1)], YR.at[1, near, far], c2_send.at[1], c2_recv.at[1],
        gy=lax.rem(me_y + across_y - 2, across_y),
    )
    pl.when(me_y < across_y - 2)(c2_up.start)
    pl.when(me_y >= 2)(c2_down.start)

    pl.when(jnp.logical_not(first_y))(y0_up.wait_recv)
    pl.when(jnp.logical_not(last_y))(y0_down.wait_recv)

    lax.fori_loop(0, 4, outer_y, 0, unroll=4)
    lax.fori_loop(CX - 4, CX, outer_y, 0, unroll=4)
    x0_up = remote(C.at[pl.ds(CX, 4)], C.at[pl.ds(0, 4)], x0_send.at[0], x0_recv.at[0], gx=above_x)
    x0_down = remote(C.at[pl.ds(4, 4)], C.at[pl.ds(CX + 4, 4)], x0_send.at[1], x0_recv.at[1], gx=below_x)
    pl.when(jnp.logical_not(last_x))(x0_up.start)
    pl.when(jnp.logical_not(first_x))(x0_down.start)

    row, col = iota((8, 48 * cores), 0), iota((8, 48 * cores), 1)
    gather = ((row // 3 == (col // 16) % cores) & (row % 3 == col // (16 * cores))).astype(F32)
    drain(GA, across_x * cores - 1, 2, ga_recv)
    value = general(GX[...], GA[...].reshape(8 * across_x * cores, CZ))
    value = value.reshape(cores, 5, 16, CZ)
    lane = iota((cores, 16, CZ), 2)
    total = jnp.where(lane < 24, value[:, 0], 0.0)
    for g in range(1, 5):
        total = total + jnp.where(lane < 24, pltpu.roll(value[:, g], CZ - 24 * g, 2), 0.0)
    both = jnp.concatenate(split(total.reshape(cores * 16, CZ)), axis=1)
    value = jnp.dot(both, PX[...], preferred_element_type=F32)
    row, lane = iota((cores * 16, CZ), 0), iota((cores * 16, CZ), 1)
    keep = (lane // 8 == row % 16) & (lane < 72)
    value = jnp.concatenate([jnp.where(keep, value[:, y * CZ : y * CZ + CZ], 0.0) for y in range(3)], axis=0)
    here = me_y // cores
    GB[here] = picked(gather, value)
    six = pl.ds(0, 6)
    for x, y in far_off:
        remote(GB.at[here, six], GB.at[here, six], gb_send, gb_recv, gy=y).start()

    lax.fori_loop(4, CX - 4, outer_y, 0, unroll=6)

    lax.fori_loop(1, CX // 16 - 1, lambda i, c: (finest_x(i, (1, 2)), c)[1], 0)

    lax.fori_loop(1, CX // 16 - 1, lambda i, c: (finest_x(i, (0, 3)), c)[1], 0)

    finest_z(16, CX - 32)

    pl.when(jnp.logical_not(first_x))(x0_up.wait_recv)
    pl.when(jnp.logical_not(last_x))(x0_down.wait_recv)
    finest_x(0, range(4))
    finest_x(CX // 16 - 1, range(4))
    finest_z(0, 16)
    finest_z(CX - 16, 16)

    pl.when(jnp.logical_not(first_y))(cy_up.wait_recv)
    pl.when(jnp.logical_not(last_y))(cy_down.wait_recv)
    pl.when(me_y >= 2)(c2_up.wait_recv)
    pl.when(me_y < across_y - 2)(c2_down.wait_recv)
    row8 = iota((8, CZ), 0)
    for level in (1, 2, 3):
        array, n, rows, count = B[level], NYL[level], ROWS[level], NXL[level] + 1
        wl = [taps[level, k] for k in range(2 * REACH + 1)]

        def along_y(x, carry, array=array, target=U[level], n=n, rows=rows, level=level, wl=wl):
            array[x, 4:12, :] = array[x, 4:12, :] + jnp.where(row8 < 5, YR[0, x], 0.0)
            array[x, 8 + n : 16 + n, :] = array[x, 8 + n : 16 + n, :] + jnp.where(row8 < 5, YR[1, x], 0.0)
            if level == 3:
                array[x, 4:5, :] = array[x, 4:5, :] + YR[0, x, 5:6, :]
                array[x, 16:17, :] = array[x, 16:17, :] + YR[1, x, 5:6, :]
            target[x] = weighted([array[x, 4 + k : 4 + k + rows, :] for k in range(9)], wl)
            return carry

        lax.fori_loop(0, count, along_y, 0, unroll={1: 5, 2: 11, 3: 17}[level])

        @pl.when(last_y)
        def _(target=U[level], n=n, count=count):
            target[0:count, n : n + 1, :] = jnp.zeros((count, 1, CZ), F32)

    lane = iota((8, CZ), 1)
    U3[...] = jnp.where((lane >= 96) & (lane < 112), U3[...], 0.0)
    for level, source, wide in ((2, U3, G2), (1, U2, G1)):
        half = {2: 8, 1: 16}[level]
        target, rows, n = U[level], ROWS[level], NXL[level]
        first, cells = LANES[level]

        low = source[:, 0:half, :]
        high = pltpu.roll(low, half - 1, 1)
        wide[:, pl.ds(0, half, stride=2), :] = low
        wide[:, pl.ds(1, half, stride=2), :] = 0.5 * (low + high)
        lane = iota((rows, CZ), 1)
        own = (lane >= first) & (lane < first + cells)
        low, high = wide[0 : n // 2, 0:rows, :], wide[1 : n // 2 + 1, 0:rows, :]
        both = jnp.stack([low, 0.5 * (low + high)], axis=1).reshape(n, rows, CZ)
        target[0:n] = jnp.where(own, target[0:n], both)
        target[n] = jnp.where(own, target[n], wide[n // 2, 0:rows, :])

    high, low = split(U1[...].reshape(66 * 24, CZ))
    both = jnp.concatenate([high, low], axis=1)
    E1Z[...] = jnp.dot(both, PZ[...], preferred_element_type=F32).reshape(66, 24, CZ)

    def rise_y(x, carry):
        low, high = E1Z[x, 0:16, :], E1Z[x, 1:17, :]
        G0[x, pl.ds(0, 16, stride=2), :] = low
        G0[x, pl.ds(1, 16, stride=2), :] = 0.5 * (low + high)
        return carry

    lax.fori_loop(0, 65, rise_y, 0, unroll=13)

    def finish(i, carry):
        low, high = G0[i], G0[i + 1]
        out[2 * i] = out[2 * i] + low
        out[2 * i + 1] = out[2 * i + 1] + 0.5 * (low + high)
        return carry

    lax.fori_loop(0, CX // 2, finish, 0, unroll=4)

    drain(GB, chips - 1, 6, gb_recv)
    value = general(GY[...], GB[...].reshape(8 * chips, CZ))
    lane = iota((CY, CZ), 1)
    spread = jnp.concatenate([jnp.where(lane // 8 == x, value, 0.0) for x in range(9)], axis=0)
    high, low = split(spread)
    both = jnp.concatenate([high, low], axis=1)
    value = jnp.dot(both, P4[...], preferred_element_type=F32).reshape(9, CY, CZ)
    coarsest[...] = value[:8]
    slopes[...] = (value[1:] - value[:8]) * (1.0 / 16.0)

    pl.when(jnp.logical_not(last_y))(y0_up.wait_send)
    pl.when(jnp.logical_not(first_y))(y0_down.wait_send)
    pl.when(jnp.logical_not(last_x))(x0_up.wait_send)
    pl.when(jnp.logical_not(first_x))(x0_down.wait_send)
    pl.when(jnp.logical_not(last_x))(cx_up.wait_send)
    pl.when(jnp.logical_not(first_x))(cx_down.wait_send)
    pl.when(jnp.logical_not(last_y))(cy_up.wait_send)
    pl.when(jnp.logical_not(first_y))(cy_down.wait_send)
    pl.when(me_y < across_y - 2)(c2_up.wait_send)
    pl.when(me_y >= 2)(c2_down.wait_send)
    drain(GA, across_x * cores - 1, 2, ga_send)
    drain(GB, chips - 1, 6, gb_send)


def last(fine, coarse, slope, out, done, sem):
    chunks = 8
    depth = CX // chunks
    copies = []
    for i in range(chunks):
        for x in range(i * depth, i * depth + depth):
            done[x] = fine[x] + (coarse[x // 16] + float(x % 16) * slope[x // 16])
        at = pl.ds(i * depth, depth)
        copies.append(pltpu.make_async_copy(done.at[at], out.at[at], sem.at[i]))
        copies[-1].start()
    for copy in copies:
        copy.wait()


def solution(mesh):
    across_x, across_y = mesh.shape["gx"], mesh.shape["gy"]

    cores = 2 if across_y > 1 else 1

    def vmem(*shape, dtype=F32):
        return pltpu.VMEM(shape, dtype)

    pair = pltpu.SemaphoreType.DMA((2,))
    single = pltpu.SemaphoreType.DMA
    scratch = [
        pltpu.SMEM((4, 9), F32),
        vmem(CX, 48, CZ),
        vmem(CX + 8, CY, CZ),
        vmem(65, 56, CZ), vmem(33, 40, CZ), vmem(17, 24, CZ), vmem(9, CY, CZ),
        vmem(67, 24, CZ), vmem(35, 16, CZ), vmem(19, 8, CZ),
        vmem(73, 24, CZ), vmem(41, 16, CZ), vmem(25, 8, CZ),
        vmem(65, 40, CZ), vmem(33, 32, CZ), vmem(17, 24, CZ),
        vmem(66, 24, CZ), vmem(33, 16, CZ), vmem(17, 8, CZ),
        vmem(17, 16, CZ), vmem(33, 32, CZ), vmem(65, 32, CZ),
        vmem(2, 5, 24, CZ), vmem(2, 5, 24, CZ),
        vmem(2, 65, 8, CZ), vmem(2, 65, 8, CZ),
        vmem(across_x * cores, 8, CZ), vmem(across_y // cores, 8, CZ),
        vmem(2 * CZ, 2 * CZ, dtype=BF16), vmem(2 * CZ, 2 * CZ, dtype=BF16), vmem(2 * CZ, CZ, dtype=BF16), vmem(2 * CZ, CZ, dtype=BF16),
        vmem(2 * CZ, 2 * CZ, dtype=BF16), vmem(9 * CY, CZ),
        vmem(cores * 80, 8 * across_x * cores), vmem(2 * CZ, 3 * CZ, dtype=BF16), vmem(CY, 8 * across_y // cores),
        vmem(66, 24, CZ),
        single, pltpu.SemaphoreType.DMA((CX // 16,)),
        pair, pair, pair, pair, pair, pair, pair, pair, pair, pair,
        single, single, single, single,
    ]

    def local(charge, level_taps):
        fine, coarse, slope = pl.pallas_call(
            functools.partial(kernel, across_x, across_y),
            out_shape=[jax.ShapeDtypeStruct((CX, CY, CZ), F32), *[jax.ShapeDtypeStruct((8, CY, CZ), F32)] * 2],
            in_specs=[pl.BlockSpec(memory_space=pltpu.HBM), pl.BlockSpec(memory_space=pltpu.HBM)],
            out_specs=[pl.BlockSpec(memory_space=pltpu.VMEM)] * 3,
            scratch_shapes=scratch,
            compiler_params=pltpu.CompilerParams(
                collective_id=0, has_side_effects=True, vmem_limit_bytes=48 * 1024 * 1024
            ),
        )(*(pltpu.with_memory_space_constraint(array, pltpu.HBM) for array in (level_taps, charge)))
        return pl.pallas_call(
            last,
            out_shape=jax.ShapeDtypeStruct((CX, CY, CZ), F32),
            in_specs=[pl.BlockSpec(memory_space=pltpu.VMEM)] * 3,
            out_specs=pl.BlockSpec(memory_space=pltpu.HBM),
            scratch_shapes=[vmem(CX, CY, CZ), pltpu.SemaphoreType.DMA((8,))],
            compiler_params=pltpu.CompilerParams(vmem_limit_bytes=8 * 1024 * 1024),
        )(fine, coarse, slope)

    spec = P("gx", "gy", None)
    return jax.shard_map(local, mesh=mesh, in_specs=(spec, P()), out_specs=spec, check_vma=False)
```

```python
import functools
import math

import jax
import jax.numpy as jnp
from jax import lax
from jax.experimental import pallas as pl
from jax.experimental.pallas import tpu as pltpu
from jax.sharding import PartitionSpec as P

F32 = jnp.float32
BF16 = jnp.bfloat16
HIGHEST = lax.Precision.HIGHEST
MESH = pl.DeviceIdType.MESH

CX, CY, CZ = 128, 32, 128
REACH = 4
LANES = {1: (0, 64), 2: (64, 32), 3: (96, 16)}
NXL = {1: 64, 2: 32, 3: 16, 4: 8}
NYL = {1: 16, 2: 8, 3: 4, 4: 2}
ROWS = {1: 24, 2: 16, 3: 8, 4: 8}


def iota(shape, dim):
    return lax.broadcasted_iota(jnp.int32, shape, dim)


def gauss(distance, length):
    spread = max(length, 4) / 2.0
    scaled = distance.astype(F32) / spread
    return jnp.exp(-scaled * scaled) / (math.sqrt(math.pi) * spread)


def split(value):
    high = value.astype(BF16)
    return high, (value - high.astype(F32)).astype(BF16)


def stacked(matrix):
    high, low = split(matrix)
    upper = jnp.concatenate([high, low], axis=1)
    lower = jnp.concatenate([high, jnp.zeros_like(high)], axis=1)
    return jnp.concatenate([upper, lower], axis=0)


def product(value, weights):
    high, low = split(value)
    both = jnp.dot(jnp.concatenate([high, low], axis=1), weights, preferred_element_type=F32)
    return both[:, :CZ] + both[:, CZ:]


def picked(matrix, value):
    both = jnp.concatenate(split(value), axis=0)
    return jnp.dot(jnp.concatenate([matrix.astype(BF16)] * 2, axis=1), both, preferred_element_type=F32)


def general(matrix, value):
    (m_high, m_low), (v_high, v_low) = split(matrix), split(value)
    left = jnp.concatenate([m_high, m_low, m_high], axis=1)
    right = jnp.concatenate([v_high, v_high, v_low], axis=0)
    return jnp.dot(left, right, preferred_element_type=F32)


def toeplitz(taps, level, shape, offset):
    matrix = jnp.zeros(shape, F32)
    for k in range(2 * REACH + 1):
        matrix = jnp.where(offset == k - REACH, taps[level, k], matrix)
    return matrix


def coarse_z(taps):
    a, c = iota((CZ, CZ), 0), iota((CZ, CZ), 1)
    down = jnp.zeros((CZ, CZ), F32)
    mix = jnp.zeros((CZ, CZ), F32)
    for level, (first, cells) in LANES.items():
        step = 2**level
        here = (c >= first) & (c < first + cells)
        weight = jnp.maximum(0, step - jnp.abs(a - step * (c - first)))
        down = jnp.where(here, weight.astype(F32) * 2.0 ** (-5 * level), down)
        inside = here & (a >= first) & (a < first + cells)
        block = toeplitz(taps, level, (CZ, CZ), a - c)
        mix = jnp.where(inside, block, mix)
    return jnp.dot(down, mix, precision=HIGHEST, preferred_element_type=F32)


def prolong_z():
    r, a = iota((CZ, CZ), 0), iota((CZ, CZ), 1)
    up = jnp.zeros((CZ, CZ), F32)
    for level, (first, cells) in LANES.items():
        step = 2**level
        here = (r >= first) & (r < first + cells)
        weight = jnp.maximum(0, step - jnp.abs(a - step * (r - first)))
        up = jnp.where(here, weight.astype(F32) * 2.0**-level, up)
    return up.astype(BF16)


def weighted(pieces, weights):
    total = weights[REACH] * pieces[REACH]
    for k in range(REACH):
        total = total + weights[k] * (pieces[k] + pieces[2 * REACH - k])
    return total


def kernel(
    across_x, across_y, taps_in, q, out, coarsest, slopes,
    taps,
    E, C, T1, T2, T3, X4, R1, R2, R3, A1, A2, A3, B1, B2, B3, U1, U2, U3, G2, G1, G0,
    XS, XR, YS, YR, GA, GB, WZ, W0, PZ, P4, Z4, K4, GX, PX, GY, E1Z,
    taps_sem, in_sem, y0_send, y0_recv, x0_send, x0_recv, cx_send, cx_recv, cy_send, cy_recv,
    c2_send, c2_recv, ga_send, ga_recv, gb_send, gb_recv,
):
    me_x, me_y = lax.axis_index("gx"), lax.axis_index("gy")
    first_x, last_x = me_x == 0, me_x == across_x - 1
    first_y, last_y = me_y == 0, me_y == across_y - 1
    R, A, B, U, T = {1: R1, 2: R2, 3: R3}, {1: A1, 2: A2, 3: A3}, {1: B1, 2: B2, 3: B3}, {1: U1, 2: U2, 3: U3}, {2: T2, 3: T3}

    few = pltpu.make_async_copy(taps_in, taps, taps_sem)
    few.start()
    def load(i):
        at = pl.ds(i * 16, 16)
        return pltpu.make_async_copy(q.at[at], E.at[at, pl.ds(8, CY)], in_sem.at[i])

    for i in range(CX // 16):
        load(i).start()

    cores = 2 if across_y > 1 else 1
    chips = across_y // cores
    core = lax.rem(me_y, cores)
    near_by = [
        (lax.rem(me_x + x, across_x), me_y - core + lax.rem(core + c, cores))
        for x in range(across_x) for c in range(cores) if x or c
    ]
    far_off = [(me_x, lax.rem(me_y + cores * step, across_y)) for step in sorted(range(1, chips), key=lambda step: abs(2 * step - chips))]
    steps = (1, 2, across_y - 2, across_y - 1) if across_y > 4 else ()
    around = [(me_x, lax.rem(me_y + step, across_y)) for step in steps]
    barrier = pltpu.get_barrier_semaphore()
    for x, y in around + near_by + far_off:
        pl.semaphore_signal(barrier, inc=1, device_id=(x, y), device_id_type=MESH)


    def blank(ref, count, *spans):
        for start, size in spans:
            ref[:, start : start + size, :] = jnp.zeros((count, size, CZ), F32)

    blank(T1, 65, (0, 8), (40, 16))
    blank(T2, 33, (0, 8), (32, 8))
    blank(T3, 17, (0, 8))
    X4[0] = jnp.zeros((CY, CZ), F32)
    for level in (1, 2, 3):
        blank(B[level], NXL[level] + 1, (0, 8), *(((16, 8),) if level == 3 else ()))
        rows = ROWS[level]
        R[level][0] = jnp.zeros((rows, CZ), F32)
    XR[:, :, 17:24, :] = jnp.zeros((2, 5, 7, CZ), F32)
    GA[:, 2:8, :] = jnp.zeros((across_x * cores, 6, CZ), F32)
    GB[:, 6:8, :] = jnp.zeros((chips, 2, CZ), F32)

    @pl.when(first_y)
    def _():
        E[:, 4:8, :] = jnp.zeros((CX, 4, CZ), F32)
        YR[0, :, 0:5, :] = jnp.zeros((65, 5, CZ), F32)

    @pl.when(last_y)
    def _():
        E[:, 40:44, :] = jnp.zeros((CX, 4, CZ), F32)
        YR[1, :, 0:5, :] = jnp.zeros((65, 5, CZ), F32)

    @pl.when(me_y < 2)
    def _():
        YR[0, 0:17, 5:6, :] = jnp.zeros((17, 1, CZ), F32)

    @pl.when(me_y >= across_y - 2)
    def _():
        YR[1, 0:17, 5:6, :] = jnp.zeros((17, 1, CZ), F32)

    @pl.when(first_x)
    def _():
        C[0:4] = jnp.zeros((4, CY, CZ), F32)
        XR[0] = jnp.zeros((5, 24, CZ), F32)

    @pl.when(last_x)
    def _():
        C[CX + 4 : CX + 8] = jnp.zeros((4, CY, CZ), F32)
        XR[1] = jnp.zeros((5, 24, CZ), F32)

    a, c = iota((CZ, CZ), 0), iota((CZ, CZ), 1)
    weight = jnp.maximum(0, 16 - jnp.abs(a - 16 * c)).astype(F32) * 2.0**-20
    weight = jnp.where(c < 8, weight, 0.0)
    block = jnp.where(a < 8, gauss(a - c % 8, 8), 0.0)
    Z4[...] = stacked(jnp.dot(weight, block, precision=HIGHEST, preferred_element_type=F32))
    row, lane = iota((9 * CY, CZ), 0), iota((9 * CY, CZ), 1)
    weight = jnp.maximum(0, 16 - jnp.abs(row % CY - 16 * ((lane // 8) % 3))).astype(F32)
    K4[...] = jnp.where(lane // 24 == row // (2 * CY), weight, 0.0)
    rise = prolong_z()
    PZ[...] = jnp.concatenate([rise, rise], axis=0)
    r, a = iota((CZ, CZ), 0), iota((CZ, CZ), 1)
    rise = jnp.maximum(0, 16 - jnp.abs(a - 16 * (r % 8))).astype(F32) / 16.0
    rise = jnp.where(r < 72, rise, 0.0).astype(BF16)
    P4[...] = jnp.concatenate([rise, rise], axis=0)
    row, col = iota((cores * 80, 8 * across_x * cores), 0), iota((cores * 80, 8 * across_x * cores), 1)
    cell, slot = 2 * ((row // 16) % 5) + col % 8, col // 8
    spot, place = 8 * me_x + row % 16, 8 * (slot // cores) + cell
    valid = (slot % cores == row // 80) & (col % 8 < 2) & (cell < 9) & (place < 8 * across_x)
    valid = valid & (row % 16 < 9) & (spot < 8 * across_x)
    GX[...] = jnp.where(valid, gauss(spot - place, 8 * across_x), 0.0)
    r, c = iota((2 * CZ, 3 * CZ), 0), iota((2 * CZ, 3 * CZ), 1)
    PX[...] = (r % CZ == 8 * (c // CZ) + c % 8).astype(F32).astype(BF16)
    row, col = iota((CY, 8 * chips), 0), iota((CY, 8 * chips), 1)
    place = 2 * (cores * (col // 8) + (col % 8) // 3) + (col % 8) % 3
    valid = (col % 8 < 3 * cores) & (place < 2 * across_y)
    along = jnp.zeros((CY, 8 * chips), F32)
    for y in range(3):
        spot = 2 * me_y + y
        share = jnp.maximum(0, 16 - jnp.abs(row - 16 * y)).astype(F32) / 16.0
        term = jnp.where(valid & (spot < 2 * across_y), gauss(spot - place, 2 * across_y), 0.0)
        along = along + share * term
    GY[...] = along
    few.wait()
    WZ[...] = stacked(coarse_z(taps))
    W0[...] = stacked(toeplitz(taps, 0, (CZ, CZ), iota((CZ, CZ), 0) - iota((CZ, CZ), 1)))

    def remote(src, dst, send, recv, **target):
        return pltpu.make_async_remote_copy(
            src_ref=src, dst_ref=dst, send_sem=send, recv_sem=recv, device_id=target, device_id_type=MESH
        )

    def drain(ref, count, rows, sem):
        if count:
            part = ref.at[pl.ds(0, count), pl.ds(0, rows)]
            pltpu.make_async_copy(part, part, sem).wait()

    above_y, below_y = lax.rem(me_y + 1, across_y), lax.rem(me_y + across_y - 1, across_y)
    above_x, below_x = lax.rem(me_x + 1, across_x), lax.rem(me_x + across_x - 1, across_x)

    y0_up = remote(q.at[:, pl.ds(CY - 4, 4)], E.at[:, pl.ds(4, 4)], y0_send.at[0], y0_recv.at[0], gy=above_y)
    y0_down = remote(q.at[:, pl.ds(0, 4)], E.at[:, pl.ds(40, 4)], y0_send.at[1], y0_recv.at[1], gy=below_y)
    def down_x(i, carry):
        load(i).wait()
        for t in range(4):
            rows = pl.ds(8 + 8 * t, 8)
            value = E[pl.ds(16 * i, 16), rows, :]
            before = E[jnp.maximum(16 * i - 1, 0), rows, :]
            before = jnp.where(i > 0, before, 0.0)
            for k in range(8):
                T1[8 * i + k, rows, :] = (before if k == 0 else value[2 * k - 1]) + 2.0 * value[2 * k] + value[2 * k + 1]
            running = value[15]
            rising = running
            for k in range(14, 0, -1):
                running = running + value[k]
                rising = rising + running
            fine = pl.ds(8 * t, 8)
            X4[i, fine, :] = X4[i, fine, :] + (16.0 * (running + value[0]) - rising)
            X4[i + 1, fine, :] = rising
        return carry

    lax.fori_loop(0, CX // 16, down_x, 0)
    T1[64, 8:40, :] = E[CX - 1, 8:40, :]

    value = product(X4[...].reshape(9 * CY, CZ), Z4[...]) * K4[...]
    pick = ((iota((8, 9 * CY), 1) // CY) % 2 == iota((8, 9 * CY), 0)).astype(F32)
    mine = me_x * cores + core
    GA[mine, 0:2, :] = picked(pick, value)[0:2]
    pl.semaphore_wait(barrier, len(around + near_by + far_off))
    two = pl.ds(0, 2)
    for x, y in near_by:
        remote(GA.at[mine, two], GA.at[mine, two], ga_send, ga_recv, gx=x, gy=y).start()
    pl.when(jnp.logical_not(last_y))(y0_up.start)
    pl.when(jnp.logical_not(first_y))(y0_down.start)

    def down_y(i, carry):
        R1[i + 1] = (
            T1[i, pl.ds(7, 24, stride=2), :] + 2.0 * T1[i, pl.ds(8, 24, stride=2), :] + T1[i, pl.ds(9, 24, stride=2), :]
        )
        return carry

    lax.fori_loop(0, 65, down_y, 0, unroll=13)

    for level in (2, 3):
        finer, mid, n = R[level - 1], T[level], NXL[level]
        inner, rows = ROWS[level - 1], ROWS[level]
        pairs = finer[1 : 2 * n + 1].reshape(n, 2, inner, CZ)
        before = finer[0 : 2 * n].reshape(n, 2, inner, CZ)
        mid[0:n, 8 : 8 + inner, :] = before[:, 0] + 2.0 * pairs[:, 0] + pairs[:, 1]
        mid[n, 8 : 8 + inner, :] = finer[2 * n] + 2.0 * finer[2 * n + 1]
        R[level][1 : n + 2] = (
            mid[:, pl.ds(7, rows, stride=2), :]
            + 2.0 * mid[:, pl.ds(8, rows, stride=2), :]
            + mid[:, pl.ds(9, rows, stride=2), :]
        )

    def level_1(first, count, kept):
        value = product(R1[first + 1 : first + count + 1].reshape(count * 24, CZ), WZ[...])
        A1[first + 4 : first + kept + 4] = value.reshape(count, 24, CZ)[0:kept]

    level_1(0, 6, 5)
    level_1(60, 6, 5)
    A2[4:37] = product(R2[1:34].reshape(33 * 16, CZ), WZ[...]).reshape(33, 16, CZ)
    A3[4:21] = product(R3[1:19].reshape(18 * 8, CZ), WZ[...]).reshape(18, 8, CZ)[0:17]

    @pl.when(last_x)
    def _():
        for level in (1, 2, 3):
            A[level][NXL[level] + 4] = jnp.zeros((ROWS[level], CZ), F32)

    for way in (0, 1):
        for i in range(5):
            at = {level: (NXL[level] if way == 0 else 4) + i for level in (1, 2, 3)}
            wide = A1[at[1]]
            lane = iota((24, CZ), 1)
            XS[way, i] = jnp.where(lane < 64, wide, 0.0)
            lane = iota((16, CZ), 1)
            XS[way, i, 0:16, :] = jnp.where(lane >= 64, A2[at[2]], XS[way, i, 0:16, :])
            lane = iota((8, CZ), 1)
            XS[way, i, 0:8, :] = jnp.where(lane >= 96, A3[at[3]], XS[way, i, 0:8, :])
    used = pl.ds(0, 17)
    cx_up = remote(XS.at[0, :, used], XR.at[0, :, used], cx_send.at[0], cx_recv.at[0], gx=above_x)
    cx_down = remote(XS.at[1, :, used], XR.at[1, :, used], cx_send.at[1], cx_recv.at[1], gx=below_x)
    pl.when(jnp.logical_not(last_x))(cx_up.start)
    pl.when(jnp.logical_not(first_x))(cx_down.start)
    level_1(5, 56, 55)

    w0 = [taps[0, k] for k in range(2 * REACH + 1)]

    def mid_y(i, carry):
        C[4 + i, 8:24, :] = weighted([E[i, 12 + k : 28 + k, :] for k in range(9)], w0)
        return carry

    def outer_y(i, carry):
        C[4 + i, 0:8, :] = weighted([E[i, 4 + k : 12 + k, :] for k in range(9)], w0)
        C[4 + i, 24:32, :] = weighted([E[i, 28 + k : 36 + k, :] for k in range(9)], w0)
        return carry

    def finest_x(i, tiles):
        for t in tiles:
            rows = pl.ds(8 * t, 8)
            value = C[pl.ds(16 * i, 24), rows, :]
            out[pl.ds(16 * i, 16), rows, :] = weighted([value[k : k + 16] for k in range(9)], w0)

    def finest_z(first, count):
        at = pl.ds(first, count)
        out[at] = product(out[at].reshape(count * CY, CZ), W0[...]).reshape(count, CY, CZ)

    lax.fori_loop(0, CX, mid_y, 0, unroll=8)

    pl.when(jnp.logical_not(first_x))(cx_up.wait_recv)
    pl.when(jnp.logical_not(last_x))(cx_down.wait_recv)
    for level in (1, 2, 3):
        array, rows, n = A[level], ROWS[level], NXL[level]
        array[0:4] = XR[0, 0:4, 0:rows, :]
        array[4] = array[4] + XR[0, 4, 0:rows, :]
        array[n + 4] = array[n + 4] + XR[1, 0, 0:rows, :]
        array[n + 5 : n + 9] = XR[1, 1:5, 0:rows, :]
        wl = [taps[level, k] for k in range(2 * REACH + 1)]

        def along_x(i, carry, array=array, target=B[level], rows=rows, wl=wl):
            target[i, pl.ds(8, rows), :] = weighted([array[i + k] for k in range(9)], wl)
            return carry

        lax.fori_loop(0, n + 1, along_x, 0, unroll={1: 5, 2: 11, 3: 17}[level])

        @pl.when(last_x)
        def _(target=B[level], rows=rows, n=n):
            target[n, pl.ds(8, rows), :] = jnp.zeros((rows, CZ), F32)

        @pl.when(last_y)
        def _(target=B[level], level=level, n=n):
            target[:, pl.ds(8 + NYL[level], 1), :] = jnp.zeros((n + 1, 1, CZ), F32)

    lane = iota((8, CZ), 1)
    for way in (0, 1):
        start = {level: 8 + (NYL[level] - 4 if way == 0 else 0) for level in (1, 2, 3)}
        YS[way] = B1[:, start[1] : start[1] + 8, :]
        YS[way, 0:33] = jnp.where(lane >= 64, B2[:, start[2] : start[2] + 8, :], B1[0:33, start[1] : start[1] + 8, :])
        YS[way, 0:17] = jnp.where(lane >= 96, B3[:, start[3] : start[3] + 8, :], YS[way, 0:17])
    rows5 = pl.ds(0, 5)
    cy_up = remote(YS.at[0, :, rows5], YR.at[0, :, rows5], cy_send.at[0], cy_recv.at[0], gy=above_y)
    cy_down = remote(YS.at[1, :, rows5], YR.at[1, :, rows5], cy_send.at[1], cy_recv.at[1], gy=below_y)
    pl.when(jnp.logical_not(last_y))(cy_up.start)
    pl.when(jnp.logical_not(first_y))(cy_down.start)
    near, far = pl.ds(0, 17), pl.ds(5, 1)
    c2_up = remote(
        YS.at[0, near, pl.ds(4, 1)], YR.at[0, near, far], c2_send.at[0], c2_recv.at[0],
        gy=lax.rem(me_y + 2, across_y),
    )
    c2_down = remote(
        YS.at[1, near, pl.ds(0, 1)], YR.at[1, near, far], c2_send.at[1], c2_recv.at[1],
        gy=lax.rem(me_y + across_y - 2, across_y),
    )
    pl.when(me_y < across_y - 2)(c2_up.start)
    pl.when(me_y >= 2)(c2_down.start)

    pl.when(jnp.logical_not(first_y))(y0_up.wait_recv)
    pl.when(jnp.logical_not(last_y))(y0_down.wait_recv)

    lax.fori_loop(0, 4, outer_y, 0, unroll=4)
    lax.fori_loop(CX - 4, CX, outer_y, 0, unroll=4)
    x0_up = remote(C.at[pl.ds(CX, 4)], C.at[pl.ds(0, 4)], x0_send.at[0], x0_recv.at[0], gx=above_x)
    x0_down = remote(C.at[pl.ds(4, 4)], C.at[pl.ds(CX + 4, 4)], x0_send.at[1], x0_recv.at[1], gx=below_x)
    pl.when(jnp.logical_not(last_x))(x0_up.start)
    pl.when(jnp.logical_not(first_x))(x0_down.start)

    row, col = iota((8, 48 * cores), 0), iota((8, 48 * cores), 1)
    gather = ((row // 3 == (col // 16) % cores) & (row % 3 == col // (16 * cores))).astype(F32)
    drain(GA, across_x * cores - 1, 2, ga_recv)
    value = general(GX[...], GA[...].reshape(8 * across_x * cores, CZ))
    value = value.reshape(cores, 5, 16, CZ)
    lane = iota((cores, 16, CZ), 2)
    total = jnp.where(lane < 24, value[:, 0], 0.0)
    for g in range(1, 5):
        total = total + jnp.where(lane < 24, pltpu.roll(value[:, g], CZ - 24 * g, 2), 0.0)
    both = jnp.concatenate(split(total.reshape(cores * 16, CZ)), axis=1)
    value = jnp.dot(both, PX[...], preferred_element_type=F32)
    row, lane = iota((cores * 16, CZ), 0), iota((cores * 16, CZ), 1)
    keep = (lane // 8 == row % 16) & (lane < 72)
    value = jnp.concatenate([jnp.where(keep, value[:, y * CZ : y * CZ + CZ], 0.0) for y in range(3)], axis=0)
    here = me_y // cores
    GB[here] = picked(gather, value)
    six = pl.ds(0, 6)
    for x, y in far_off:
        remote(GB.at[here, six], GB.at[here, six], gb_send, gb_recv, gy=y).start()

    lax.fori_loop(4, CX - 4, outer_y, 0, unroll=6)

    lax.fori_loop(1, CX // 16 - 1, lambda i, c: (finest_x(i, (1, 2)), c)[1], 0)

    lax.fori_loop(1, CX // 16 - 1, lambda i, c: (finest_x(i, (0, 3)), c)[1], 0)

    finest_z(16, CX - 32)

    pl.when(jnp.logical_not(first_x))(x0_up.wait_recv)
    pl.when(jnp.logical_not(last_x))(x0_down.wait_recv)
    finest_x(0, range(4))
    finest_x(CX // 16 - 1, range(4))
    finest_z(0, 16)
    finest_z(CX - 16, 16)

    pl.when(jnp.logical_not(first_y))(cy_up.wait_recv)
    pl.when(jnp.logical_not(last_y))(cy_down.wait_recv)
    pl.when(me_y >= 2)(c2_up.wait_recv)
    pl.when(me_y < across_y - 2)(c2_down.wait_recv)
    row8 = iota((8, CZ), 0)
    for level in (1, 2, 3):
        array, n, rows, count = B[level], NYL[level], ROWS[level], NXL[level] + 1
        wl = [taps[level, k] for k in range(2 * REACH + 1)]

        def along_y(x, carry, array=array, target=U[level], n=n, rows=rows, level=level, wl=wl):
            array[x, 4:12, :] = array[x, 4:12, :] + jnp.where(row8 < 5, YR[0, x], 0.0)
            array[x, 8 + n : 16 + n, :] = array[x, 8 + n : 16 + n, :] + jnp.where(row8 < 5, YR[1, x], 0.0)
            if level == 3:
                array[x, 4:5, :] = array[x, 4:5, :] + YR[0, x, 5:6, :]
                array[x, 16:17, :] = array[x, 16:17, :] + YR[1, x, 5:6, :]
            target[x] = weighted([array[x, 4 + k : 4 + k + rows, :] for k in range(9)], wl)
            return carry

        lax.fori_loop(0, count, along_y, 0, unroll={1: 5, 2: 11, 3: 17}[level])

        @pl.when(last_y)
        def _(target=U[level], n=n, count=count):
            target[0:count, n : n + 1, :] = jnp.zeros((count, 1, CZ), F32)

    lane = iota((8, CZ), 1)
    U3[...] = jnp.where((lane >= 96) & (lane < 112), U3[...], 0.0)
    for level, source, wide in ((2, U3, G2), (1, U2, G1)):
        half = {2: 8, 1: 16}[level]
        target, rows, n = U[level], ROWS[level], NXL[level]
        first, cells = LANES[level]

        low = source[:, 0:half, :]
        high = pltpu.roll(low, half - 1, 1)
        wide[:, pl.ds(0, half, stride=2), :] = low
        wide[:, pl.ds(1, half, stride=2), :] = 0.5 * (low + high)
        lane = iota((rows, CZ), 1)
        own = (lane >= first) & (lane < first + cells)
        low, high = wide[0 : n // 2, 0:rows, :], wide[1 : n // 2 + 1, 0:rows, :]
        both = jnp.stack([low, 0.5 * (low + high)], axis=1).reshape(n, rows, CZ)
        target[0:n] = jnp.where(own, target[0:n], both)
        target[n] = jnp.where(own, target[n], wide[n // 2, 0:rows, :])

    high, low = split(U1[...].reshape(66 * 24, CZ))
    both = jnp.concatenate([high, low], axis=1)
    E1Z[...] = jnp.dot(both, PZ[...], preferred_element_type=F32).reshape(66, 24, CZ)

    def rise_y(x, carry):
        low, high = E1Z[x, 0:16, :], E1Z[x, 1:17, :]
        G0[x, pl.ds(0, 16, stride=2), :] = low
        G0[x, pl.ds(1, 16, stride=2), :] = 0.5 * (low + high)
        return carry

    lax.fori_loop(0, 65, rise_y, 0, unroll=13)

    def finish(i, carry):
        low, high = G0[i], G0[i + 1]
        out[2 * i] = out[2 * i] + low
        out[2 * i + 1] = out[2 * i + 1] + 0.5 * (low + high)
        return carry

    lax.fori_loop(0, CX // 2, finish, 0, unroll=4)

    drain(GB, chips - 1, 6, gb_recv)
    value = general(GY[...], GB[...].reshape(8 * chips, CZ))
    lane = iota((CY, CZ), 1)
    spread = jnp.concatenate([jnp.where(lane // 8 == x, value, 0.0) for x in range(9)], axis=0)
    high, low = split(spread)
    both = jnp.concatenate([high, low], axis=1)
    value = jnp.dot(both, P4[...], preferred_element_type=F32).reshape(9, CY, CZ)
    coarsest[...] = value[:8]
    slopes[...] = (value[1:] - value[:8]) * (1.0 / 16.0)

    pl.when(jnp.logical_not(last_y))(y0_up.wait_send)
    pl.when(jnp.logical_not(first_y))(y0_down.wait_send)
    pl.when(jnp.logical_not(last_x))(x0_up.wait_send)
    pl.when(jnp.logical_not(first_x))(x0_down.wait_send)
    pl.when(jnp.logical_not(last_x))(cx_up.wait_send)
    pl.when(jnp.logical_not(first_x))(cx_down.wait_send)
    pl.when(jnp.logical_not(last_y))(cy_up.wait_send)
    pl.when(jnp.logical_not(first_y))(cy_down.wait_send)
    pl.when(me_y < across_y - 2)(c2_up.wait_send)
    pl.when(me_y >= 2)(c2_down.wait_send)
    drain(GA, across_x * cores - 1, 2, ga_send)
    drain(GB, chips - 1, 6, gb_send)


def last(fine, coarse, slope, out, done, sem):
    chunks = 8
    depth = CX // chunks
    copies = []
    for i in range(chunks):
        for x in range(i * depth, i * depth + depth):
            done[x] = fine[x] + (coarse[x // 16] + float(x % 16) * slope[x // 16])
        at = pl.ds(i * depth, depth)
        copies.append(pltpu.make_async_copy(done.at[at], out.at[at], sem.at[i]))
        copies[-1].start()
    for copy in copies:
        copy.wait()


def solution(mesh):
    across_x, across_y = mesh.shape["gx"], mesh.shape["gy"]

    cores = 2 if across_y > 1 else 1

    def vmem(*shape, dtype=F32):
        return pltpu.VMEM(shape, dtype)

    pair = pltpu.SemaphoreType.DMA((2,))
    single = pltpu.SemaphoreType.DMA
    scratch = [
        pltpu.SMEM((4, 9), F32),
        vmem(CX, 48, CZ),
        vmem(CX + 8, CY, CZ),
        vmem(65, 56, CZ), vmem(33, 40, CZ), vmem(17, 24, CZ), vmem(9, CY, CZ),
        vmem(67, 24, CZ), vmem(35, 16, CZ), vmem(19, 8, CZ),
        vmem(73, 24, CZ), vmem(41, 16, CZ), vmem(25, 8, CZ),
        vmem(65, 40, CZ), vmem(33, 32, CZ), vmem(17, 24, CZ),
        vmem(66, 24, CZ), vmem(33, 16, CZ), vmem(17, 8, CZ),
        vmem(17, 16, CZ), vmem(33, 32, CZ), vmem(65, 32, CZ),
        vmem(2, 5, 24, CZ), vmem(2, 5, 24, CZ),
        vmem(2, 65, 8, CZ), vmem(2, 65, 8, CZ),
        vmem(across_x * cores, 8, CZ), vmem(across_y // cores, 8, CZ),
        vmem(2 * CZ, 2 * CZ, dtype=BF16), vmem(2 * CZ, 2 * CZ, dtype=BF16), vmem(2 * CZ, CZ, dtype=BF16), vmem(2 * CZ, CZ, dtype=BF16),
        vmem(2 * CZ, 2 * CZ, dtype=BF16), vmem(9 * CY, CZ),
        vmem(cores * 80, 8 * across_x * cores), vmem(2 * CZ, 3 * CZ, dtype=BF16), vmem(CY, 8 * across_y // cores),
        vmem(66, 24, CZ),
        single, pltpu.SemaphoreType.DMA((CX // 16,)),
        pair, pair, pair, pair, pair, pair, pair, pair, pair, pair,
        single, single, single, single,
    ]

    def local(charge, level_taps):
        fine, coarse, slope = pl.pallas_call(
            functools.partial(kernel, across_x, across_y),
            out_shape=[jax.ShapeDtypeStruct((CX, CY, CZ), F32), *[jax.ShapeDtypeStruct((8, CY, CZ), F32)] * 2],
            in_specs=[pl.BlockSpec(memory_space=pltpu.HBM), pl.BlockSpec(memory_space=pltpu.HBM)],
            out_specs=[pl.BlockSpec(memory_space=pltpu.VMEM)] * 3,
            scratch_shapes=scratch,
            compiler_params=pltpu.CompilerParams(
                collective_id=0, has_side_effects=True, vmem_limit_bytes=48 * 1024 * 1024
            ),
        )(*(pltpu.with_memory_space_constraint(array, pltpu.HBM) for array in (level_taps, charge)))
        return pl.pallas_call(
            last,
            out_shape=jax.ShapeDtypeStruct((CX, CY, CZ), F32),
            in_specs=[pl.BlockSpec(memory_space=pltpu.VMEM)] * 3,
            out_specs=pl.BlockSpec(memory_space=pltpu.HBM),
            scratch_shapes=[vmem(CX, CY, CZ), pltpu.SemaphoreType.DMA((8,))],
            compiler_params=pltpu.CompilerParams(vmem_limit_bytes=8 * 1024 * 1024),
        )(fine, coarse, slope)

    spec = P("gx", "gy", None)
    return jax.shard_map(local, mesh=mesh, in_specs=(spec, P()), out_specs=spec, check_vma=False)
```
